768 devices in a mesh: rows: 96 (over x, y, z_lo), feat: 8 (over z_hi, core).
Axes of the slice: x: 4, y: 8, z: 12 (z_hi: 4, z_lo: 3; z = z_hi * 3 + z_lo), core: 2. Of those that a mesh axis runs over, the one named last changes fastest.
Arguments:
- features: bfloat16 [49152, 768], P('rows', 'feat'), may hold values from -6 to 6
- tile_values: bfloat16 [10752, 128, 128], P('rows'), may hold values from -0.09375 to 0.09375
- dest_block: int32 [10752], P('rows'), may hold values from 0 to 3
- source_block: int32 [10752], P('rows'), may hold values from 0 to 383, as said below
- tile_count: int32 [672], P('rows'), may hold values from 1 to 16
- degree: int32 [49152], P('rows'), may hold values from 1 to 4
- self_weight: bfloat16 [768, 1024], P('feat'), may hold values from -0.21875 to 0.21875
- neighbour_weight: bfloat16 [768, 1024], P('feat'), may hold values from -0.21875 to 0.21875
- hidden_bias: bfloat16 [1024], P('feat'), may hold values from -3 to 3
- cotangent: bfloat16 [49152, 1024], P('rows', 'feat'), may hold values from -6 to 6
Outputs:
- activations: bfloat16 [49152, 1024], P('rows', 'feat')
- grad_features: bfloat16 [49152, 768], P('rows', 'feat')
- grad_self: float32 [768, 1024], P('feat')
- grad_neighbour: float32 [768, 1024], P('feat')
- grad_bias: float32 [1024], P('feat')
The draws below stay inside these ranges and needn't reach their ends.
Inputs may be any that keep to these rules, and one draw needn't show every extreme that they name: `source_block`: tile k = (g * 7 + o) * 16 + s reads a block of row group (g + o - 3) mod 96.
All inputs are finite; a program needn't handle non-finite values.
Results may differ from the reference program's by a relative error of at most 0.02.
Values may be sent and summed in bfloat16 or wider, within the bound.
No kernel may reach another device: no remote copies, remote signals or barrier semaphores. Data moves between devices by JAX's collectives and lax.ppermute only.
A program may use at most 32 MiB of HBM per device.

```python
import jax
import jax.numpy as jnp
from jax import lax

F = 768
H = 1024
BLOCK = 128
BLK_DEV = 4
REACH = 3
SLOTS = 16
OFFS = 7
GROUPS = 96
NODES = 49152
N_FEAT = 8


def draw_source_block(key, part):
    key = jax.random.fold_in(key, 2)
    total = GROUPS * OFFS * SLOTS
    local_block = jax.random.randint(key, (total,), 0, BLK_DEV)
    index_all = jnp.arange(total)
    first_end = REACH * SLOTS
    last_end = ((GROUPS - 1) * OFFS + REACH) * SLOTS
    local_block = jnp.where(index_all == first_end, 0, local_block)
    local_block = jnp.where(index_all == last_end, BLK_DEV - 1, local_block)
    group_of = index_all // (OFFS * SLOTS)
    offset_of = index_all // SLOTS % OFFS
    target_group = (group_of + offset_of - REACH) % GROUPS
    return (target_group * BLK_DEV + local_block).astype(jnp.int32)


def draw_tile_count(key, part):
    key = jax.random.fold_in(key, 1)
    first_key, second_key = jax.random.split(key)
    total = GROUPS * OFFS
    counts = jax.random.randint(first_key, (total,), 1, SLOTS + 1)
    chosen = jax.random.randint(second_key, (), 0, total)
    counts = jnp.where(jnp.arange(total) == chosen, SLOTS, counts)
    counts = jnp.where(jnp.arange(total) == (chosen + 1) % total, 1, counts)
    return counts.astype(jnp.int32)


def place_ends(drawn, key, low, high):
    shape = drawn.shape
    index_at = [jax.random.randint(jax.random.fold_in(key, axis), (), 0, shape[axis]) for axis in range(len(shape))]
    drawn = drawn.at[tuple(index_at)].set(low)
    longest = shape.index(max(shape))
    index_at[longest] = (index_at[longest] + 1) % shape[longest]
    return drawn.at[tuple(index_at)].set(high)


def steps_of(stream_key, shape, pieces, low, largest):
    gain = 1.0
    for axis_at, blocks in pieces:
        heights = jax.random.uniform(jax.random.fold_in(jax.random.fold_in(stream_key, 6), axis_at), (blocks,), jnp.float32, low / len(pieces), largest / len(pieces))
        gain = gain * jnp.repeat(jnp.exp(heights), shape[axis_at] // blocks).reshape((-1,) + (1,) * (len(shape) - 1 - axis_at))
    return gain


def noise(key, dims, width, most, shards=(), held_as=jnp.bfloat16):
    loudness = steps_of(key, dims, shards, -0.22, 0.18) if shards else 1.0
    entries = jax.random.normal(key, dims, jnp.float32) * width * loudness
    return jnp.minimum(jnp.maximum(entries, -most), most).astype(held_as)


def setup_inputs(seed: int = 0) -> dict:
    seeds = jax.random.split(jax.random.key(seed), 11)
    features = noise(seeds[0], (NODES, F), 1.0, 6.0, ((0, 96), (1, 8)))
    tile_values = noise(seeds[1], (GROUPS * OFFS * SLOTS, BLOCK, BLOCK), (2 * SLOTS * BLOCK) ** -0.5, 0.09375, ((0, 96),))
    dest_block = place_ends(jax.random.randint(seeds[2], (GROUPS * OFFS * SLOTS,), 0, BLK_DEV), jax.random.fold_in(seeds[2], 1), 0, BLK_DEV - 1).astype(jnp.int32)
    source_block = draw_source_block(jax.random.fold_in(seeds[10], 71), 0)
    tile_count = draw_tile_count(jax.random.fold_in(seeds[10], 71), 0)
    degree = place_ends(jax.random.randint(seeds[5], (NODES,), 1, 5), jax.random.fold_in(seeds[5], 1), 1, 4).astype(jnp.int32)
    self_weight = noise(seeds[6], (F, H), F ** -0.5, 0.21875, ((0, 8),))
    neighbour_weight = noise(seeds[7], (F, H), F ** -0.5, 0.21875, ((0, 8),))
    hidden_bias = noise(seeds[8], (H,), 0.5, 3.0, ((0, 8),))
    cotangent = noise(seeds[9], (NODES, H), 1.0, 6.0, ((0, 96), (1, 8)))
    return {"features": features, "tile_values": tile_values, "dest_block": dest_block, "source_block": source_block, "tile_count": tile_count, "degree": degree, "self_weight": self_weight, "neighbour_weight": neighbour_weight, "hidden_bias": hidden_bias, "cotangent": cotangent}


def reference(features, tile_values, dest_block, source_block, tile_count, degree, self_weight, neighbour_weight, hidden_bias, cotangent):
    feat_width = features.shape[1]
    per_group = OFFS * SLOTS
    blocks = features.reshape(GROUPS * BLK_DEV, BLOCK, feat_width).astype(jnp.float32)
    tiles_grouped = tile_values.reshape(GROUPS, per_group, BLOCK, BLOCK)
    dest_grouped = dest_block.reshape(GROUPS, per_group).astype(jnp.int32)
    source_grouped = source_block.reshape(GROUPS, per_group).astype(jnp.int32)
    slot_ids = jnp.arange(per_group) % SLOTS
    offset_ids = jnp.arange(per_group) // SLOTS
    counts = tile_count.reshape(GROUPS, OFFS)[:, offset_ids]
    live_mask = (slot_ids[None, :] < counts).astype(jnp.float32)
    block_ids = jnp.arange(BLK_DEV)

    def forward_group(args):
        tiles_here, dest_here, source_here, live_here = args
        picked = blocks[source_here]
        products = jnp.einsum('sij,sjf->sif', tiles_here.astype(jnp.float32), picked)
        placing = (dest_here[:, None] == block_ids[None, :]).astype(jnp.float32) * live_here[:, None]
        return jnp.einsum('sb,sif->bif', placing, products)

    summed = lax.map(forward_group, (tiles_grouped, dest_grouped, source_grouped, live_mask))
    summed = summed.reshape(NODES, feat_width)
    degrees = degree.astype(jnp.float32)[:, None]
    aggregate = (summed / degrees).astype(jnp.bfloat16)
    slice_width = feat_width // N_FEAT
    feat_slices = features.reshape(NODES, N_FEAT, slice_width).transpose(1, 0, 2)
    aggr_slices = aggregate.reshape(NODES, N_FEAT, slice_width).transpose(1, 0, 2)
    self_slices = self_weight.reshape(N_FEAT, slice_width, self_weight.shape[1])
    neigh_slices = neighbour_weight.reshape(N_FEAT, slice_width, neighbour_weight.shape[1])

    def add_slice(total, args):
        feat_here, aggr_here, self_here, neigh_here = args
        partial_sum = jnp.dot(feat_here, self_here, preferred_element_type=jnp.float32)
        partial_sum = partial_sum + jnp.dot(aggr_here, neigh_here, preferred_element_type=jnp.float32)
        rounded = lax.optimization_barrier(partial_sum.astype(jnp.bfloat16))
        return total + rounded.astype(jnp.float32), None

    start_total = jnp.zeros((NODES, self_weight.shape[1]), jnp.float32)
    preact, _ = lax.scan(add_slice, start_total, (feat_slices, aggr_slices, self_slices, neigh_slices))
    preact = preact + hidden_bias.astype(jnp.float32)
    gate_value = jax.nn.sigmoid(preact)
    activations = (preact * gate_value).astype(jnp.bfloat16)
    grad_pre = (cotangent.astype(jnp.float32) * gate_value * (1.0 + preact * (1.0 - gate_value))).astype(jnp.bfloat16)
    grad_bias = jnp.sum(grad_pre.astype(jnp.float32), axis=0)
    grad_self = jnp.dot(features.T, grad_pre, preferred_element_type=jnp.float32)
    grad_neighbour = jnp.dot(aggregate.T, grad_pre, preferred_element_type=jnp.float32)
    back_rows = (jnp.dot(grad_pre, neighbour_weight.T, preferred_element_type=jnp.float32) / degrees).astype(jnp.bfloat16)
    back_blocks = back_rows.reshape(GROUPS, BLK_DEV, BLOCK, feat_width)

    def backward_group(carry, args):
        tiles_here, dest_here, source_here, live_here, back_here = args
        placing = (dest_here[:, None] == block_ids[None, :]).astype(jnp.float32) * live_here[:, None]
        rows_in = jnp.einsum('sb,bif->sif', placing, back_here.astype(jnp.float32))
        products = jnp.einsum('sij,sif->sjf', tiles_here.astype(jnp.float32), rows_in)
        return carry.at[source_here].add(products), None

    start_carry = jnp.zeros((GROUPS * BLK_DEV, BLOCK, feat_width), jnp.float32)
    spread, _ = lax.scan(backward_group, start_carry, (tiles_grouped, dest_grouped, source_grouped, live_mask, back_blocks))
    spread = spread.reshape(NODES, feat_width)
    self_term = jnp.dot(grad_pre, self_weight.T, preferred_element_type=jnp.float32)
    grad_features = (self_term + spread).astype(jnp.bfloat16)
    return activations, grad_features, grad_self, grad_neighbour, grad_bias
```

```python
import jax
import jax.numpy as jnp
from jax import lax
from jax.sharding import PartitionSpec as P

REACH = 3
SLOTS = 16


def shifted(value, axis, steps):
    count = lax.axis_size(axis)
    pairs = [(source, (source + steps) % count) for source in range(count)]
    return lax.ppermute(value, axis, pairs)


def on_device(
    features,
    tile_values,
    dest_block,
    source_block,
    tile_count,
    degree,
    self_weight,
    neighbour_weight,
    hidden_bias,
    cotangent,
):
    node_dev, feat_width = features.shape
    block_size = tile_values.shape[1]
    block_count = node_dev // block_size
    groups = lax.axis_size("rows")
    position = lax.axis_index("rows")
    slot_ids = jnp.arange(SLOTS)
    block_ids = jnp.arange(block_count)
    highest = lax.Precision.HIGHEST

    def layout(offset):
        first_slot = offset * SLOTS
        tile_part = tile_values[first_slot : first_slot + SLOTS]
        live_mask = (slot_ids < tile_count[offset]).astype(jnp.float32)
        dest_hot = (
            dest_block[first_slot : first_slot + SLOTS][:, None] == block_ids[None, :]
        ).astype(jnp.float32) * live_mask[:, None]
        source = (position + offset - REACH) % groups
        source_local = source_block[first_slot : first_slot + SLOTS] - source * block_count
        source_hot = (source_local[:, None] == block_ids[None, :]).astype(jnp.float32)
        return (tile_part, dest_hot, source_hot)

    def gather_terms(offset, incoming):
        tile_part, dest_hot, source_hot = layout(offset)
        shaped = incoming.reshape(block_count, block_size, feat_width)
        picked = jnp.einsum(
            "sb,bnf->snf",
            source_hot.astype(jnp.bfloat16),
            shaped,
            preferred_element_type=jnp.float32,
        ).astype(jnp.bfloat16)
        products = jnp.einsum("sij,sjf->sif", tile_part, picked, preferred_element_type=jnp.float32)
        return jnp.einsum("sb,sif->bif", dest_hot, products, precision=highest)

    def scatter_terms(offset, back_blocks):
        tile_part, dest_hot, source_hot = layout(offset)
        rows_in = jnp.einsum(
            "sb,bif->sif",
            dest_hot.astype(jnp.bfloat16),
            back_blocks,
            preferred_element_type=jnp.float32,
        ).astype(jnp.bfloat16)
        products = jnp.einsum(
            "sij,sif->sjf", tile_part, rows_in, preferred_element_type=jnp.float32
        )
        return jnp.einsum("sb,sjf->bjf", source_hot, products, precision=highest)

    summed = gather_terms(REACH, features)
    for shift_by in range(-REACH, REACH + 1):
        if shift_by != 0:
            incoming = shifted(features, "rows", -shift_by)
            summed = summed + gather_terms(REACH + shift_by, incoming)
    degrees = degree.astype(jnp.float32)[:, None]
    aggregate = (summed.reshape(node_dev, feat_width) / degrees).astype(jnp.bfloat16)
    partial_pre = jnp.dot(features, self_weight, preferred_element_type=jnp.float32)
    partial_pre = partial_pre + jnp.dot(
        aggregate, neighbour_weight, preferred_element_type=jnp.float32
    )
    hidden_dev = hidden_bias.shape[0]
    feats = lax.axis_size("feat")
    pieces = partial_pre.astype(jnp.bfloat16).reshape(node_dev, feats, hidden_dev)
    pieces = lax.all_to_all(pieces.transpose(1, 0, 2), "feat", 0, 0)
    preact = jnp.sum(pieces.astype(jnp.float32), axis=0) + hidden_bias.astype(jnp.float32)
    gate_value = jax.nn.sigmoid(preact)
    activations = (preact * gate_value).astype(jnp.bfloat16)
    grad_pre = (
        cotangent.astype(jnp.float32) * gate_value * (1.0 + preact * (1.0 - gate_value))
    ).astype(jnp.bfloat16)
    grad_full = lax.all_to_all(
        jnp.broadcast_to(grad_pre[None], (feats,) + grad_pre.shape), "feat", 0, 0
    )
    grad_full = grad_full.transpose(1, 0, 2).reshape(node_dev, feats * hidden_dev)
    contract_rows = (((0,), (0,)), ((), ()))
    self_part = lax.dot_general(
        features, grad_full, contract_rows, preferred_element_type=jnp.float32
    )
    neighbour_part = lax.dot_general(
        aggregate, grad_full, contract_rows, preferred_element_type=jnp.float32
    )
    bias_part = jnp.sum(grad_pre.astype(jnp.float32), axis=0)
    weight_part = jnp.concatenate([self_part, neighbour_part], axis=0).astype(jnp.bfloat16)
    weight_part = weight_part.reshape(12, 16, feats, hidden_dev).transpose(0, 2, 1, 3)
    weight_part = weight_part.reshape(groups, 16, hidden_dev)
    bias_rows = jnp.broadcast_to(
        bias_part.astype(jnp.bfloat16)[None, None], (groups, 16, hidden_dev)
    )
    sent = jnp.concatenate([weight_part, bias_rows], axis=1)
    got = jnp.sum(lax.all_to_all(sent, "rows", 0, 0).astype(jnp.float32), axis=0)
    grad_bias = got[16]
    owned = jnp.broadcast_to(got[:16].astype(jnp.bfloat16)[None], (groups, 16, hidden_dev))
    whole = lax.all_to_all(owned, "rows", 0, 0).reshape(12, feats, 16, hidden_dev)
    whole = whole.transpose(0, 2, 1, 3).reshape(2, feat_width, feats * hidden_dev)
    grad_self, grad_neighbour = whole[0].astype(jnp.float32), whole[1].astype(jnp.float32)
    contract_hidden = (((1,), (1,)), ((), ()))
    back_rows = (
        lax.dot_general(
            grad_full, neighbour_weight, contract_hidden, preferred_element_type=jnp.float32
        )
        / degrees
    ).astype(jnp.bfloat16)
    back_blocks = back_rows.reshape(block_count, block_size, feat_width)
    spread = scatter_terms(REACH, back_blocks)
    for shift_by in range(-REACH, REACH + 1):
        if shift_by != 0:
            outgoing = scatter_terms(REACH + shift_by, back_blocks)
            spread = spread + shifted(outgoing.astype(jnp.bfloat16), "rows", shift_by).astype(
                outgoing.dtype
            )
    self_term = lax.dot_general(
        grad_full, self_weight, contract_hidden, preferred_element_type=jnp.float32
    )
    grad_features = (self_term + spread.reshape(node_dev, feat_width)).astype(jnp.bfloat16)
    return (activations, grad_features, grad_self, grad_neighbour, grad_bias)


def solution(mesh):
    in_specs = (
        P("rows", "feat"),
        P("rows", None, None),
        P("rows"),
        P("rows"),
        P("rows"),
        P("rows"),
        P("feat", None),
        P("feat", None),
        P("feat"),
        P("rows", "feat"),
    )
    out_specs = (P("rows", "feat"), P("rows", "feat"), P("feat", None), P("feat", None), P("feat"))
    return jax.shard_map(
        on_device, mesh=mesh, in_specs=in_specs, out_specs=out_specs, check_vma=False
    )
```

```python
import functools

import jax
import jax.numpy as jnp
from jax import lax
from jax.experimental import pallas as pl
from jax.experimental.pallas import tpu as pltpu
from jax.sharding import PartitionSpec as P

REACH = 3
SLOTS = 16
OFFS = 2 * REACH + 1
BLOCK = 128
GROUP = 4
CORES = 2
F32 = jnp.float32
BF16 = jnp.bfloat16
VMEM_BYTES = 40 * 1024 * 1024
VMEM = pl.BlockSpec(memory_space=pltpu.VMEM)
SMEM = pl.BlockSpec(memory_space=pltpu.SMEM)


def lanes(block):
    return pl.ds(pl.multiple_of(block * BLOCK, BLOCK), BLOCK)


def live_tiles(offset, count_ref, product, place_of, total_ref):
    count = count_ref[offset]
    spare = total_ref.shape[0] - 1

    def step(at, carry):
        products = []
        places = []
        for inner in range(GROUP):
            slot = at * GROUP + inner
            tile = offset * SLOTS + slot
            products.append(product(tile))
            places.append(jnp.where(slot < count, place_of(tile), spare))
        for place, value in zip(places, products):
            total_ref[place] += value
        return carry

    lax.fori_loop(0, (count + GROUP - 1) // GROUP, step, 0)


def gather_kernel(count_ref, dest_ref, source_ref, tiles_ref, degree_ref, *refs):
    inputs, out_ref, total_ref = refs[:OFFS], refs[OFFS], refs[OFFS + 1]
    blocks = total_ref.shape[0] - 1
    total_ref[...] = jnp.zeros_like(total_ref)
    for offset in range(OFFS):

        def product(tile, offset=offset):
            picked = inputs[offset][:, lanes(source_ref[tile] % blocks)]
            return lax.dot_general(
                picked, tiles_ref[tile], (((1,), (1,)), ((), ())), preferred_element_type=F32
            )

        live_tiles(offset, count_ref, product, lambda tile: dest_ref[tile], total_ref)
    for block in range(blocks):
        part = pl.ds(block * BLOCK, BLOCK)
        out_ref[:, part] = (total_ref[block] / degree_ref[:, part].astype(F32)).astype(BF16)


def middle_kernel(count_ref, dest_ref, source_ref, tiles_ref, degree_ref, *refs):
    inputs, refs = refs[:4], refs[4:]
    self_ref, neighbour_ref, bias_ref, cotangent_ref, refs = *refs[:4], refs[4:]
    act_ref, grad_ref, weight_ref, bias_out_ref, refs = *refs[:4], refs[4:]
    outs, refs = refs[:OFFS], refs[OFFS:]
    scaled_ref, total_ref = refs
    blocks = total_ref.shape[0] - 1
    half = inputs[0].shape[0]
    contract_first = (((0,), (0,)), ((), ()))
    pre = None
    for at, operand in enumerate(inputs):
        weights = (self_ref, neighbour_ref)[at // 2][pl.ds((at % 2) * half, half), :]
        term = lax.dot_general(
            weights, operand[...], contract_first, preferred_element_type=F32
        )
        pre = term if pre is None else pre + term
    preact = pre.T + bias_ref[...].astype(F32)
    gate_value = jax.nn.sigmoid(preact)
    act_ref[...] = (preact * gate_value).astype(BF16)
    grad = cotangent_ref[...].astype(F32) * gate_value * (1.0 + preact * (1.0 - gate_value))
    grad_pre = grad.astype(BF16)
    grad = grad_pre.astype(F32)
    bias_out_ref[...] = jnp.broadcast_to(
        jnp.sum(grad, axis=0, keepdims=True), bias_out_ref.shape
    ).astype(bias_out_ref.dtype)
    turned = grad.T
    grad_ref[...] = turned.astype(BF16)
    scaled = (turned / degree_ref[...].astype(F32)).astype(BF16)
    for block in range(blocks):
        scaled_ref[block] = scaled[:, block * BLOCK : (block + 1) * BLOCK]
    parts = half // 4
    for at, operand in enumerate(inputs):
        term = jnp.dot(operand[...], grad_pre, preferred_element_type=F32).astype(BF16)
        for piece in range(4):
            first = ((at % 2) * 4 + piece) * 2 * parts + (at // 2) * parts
            weight_ref[pl.ds(first, parts), :] = term[piece * parts : (piece + 1) * parts]
    for offset in range(OFFS):
        total_ref[...] = jnp.zeros_like(total_ref)

        def product(tile):
            return jnp.dot(
                scaled_ref[dest_ref[tile]], tiles_ref[tile], preferred_element_type=F32
            )

        live_tiles(offset, count_ref, product, lambda tile: source_ref[tile] % blocks, total_ref)
        for block in range(blocks):
            outs[offset][:, pl.ds(block * BLOCK, BLOCK)] = total_ref[block].astype(
                outs[offset].dtype
            )


def back_kernel(own_ref, *refs):
    received, refs = refs[: OFFS - 1], refs[OFFS - 1 :]
    grad_ref, self_ref, neighbour_ref, keep_ref, send_ref = refs
    spread = own_ref[...]
    for part in received:
        spread = spread + part[...].astype(F32)
    spread = spread.astype(BF16)
    half = keep_ref.shape[0]
    for at, out in enumerate((keep_ref, send_ref)):
        rows = pl.ds(at * half, half)
        value = jnp.dot(self_ref[rows, :], grad_ref[...], preferred_element_type=F32)
        value = value + jnp.dot(neighbour_ref[rows, :], spread, preferred_element_type=F32)
        out[...] = value.astype(out.dtype)


def call(kernel, in_specs, out_shape, scratch, flops, moved):
    return pl.pallas_call(
        kernel,
        in_specs=in_specs,
        out_shape=out_shape,
        out_specs=jax.tree.map(lambda _: VMEM, out_shape),
        scratch_shapes=scratch,
        compiler_params=pltpu.CompilerParams(vmem_limit_bytes=VMEM_BYTES),
        cost_estimate=pl.CostEstimate(flops=flops, bytes_accessed=moved, transcendentals=0),
    )


def shifted(value, steps):
    count = lax.axis_size("rows")
    pairs = [(source, (source + steps) % count) for source in range(count)]
    return lax.ppermute(value, "rows", pairs)


def on_device(
    features,
    tile_values,
    dest_block,
    source_block,
    tile_count,
    degree,
    self_weight,
    neighbour_weight,
    hidden_bias,
    cotangent,
):
    node_dev, width = features.shape
    blocks = node_dev // BLOCK
    groups = lax.axis_size("rows")
    feats = lax.axis_size("feat")
    stacks = feats // CORES
    hidden_dev = hidden_bias.shape[0]
    core = lax.axis_index("feat") % CORES
    same_core = [[z * CORES + c for z in range(stacks)] for c in range(CORES)]
    other_core = [(f, f ^ 1) for f in range(feats)]

    def over_stacks(value):
        return lax.all_to_all(value, "feat", 0, 0, axis_index_groups=same_core)

    def whole(value):
        copies = jnp.broadcast_to(value[None], (stacks,) + value.shape)
        own = over_stacks(copies).reshape(stacks * value.shape[0], value.shape[1])
        return own, lax.ppermute(own, "feat", other_core)

    turned = features.T
    incoming = [
        turned if offset == REACH else shifted(turned, REACH - offset) for offset in range(OFFS)
    ]

    both = jnp.stack([self_weight, neighbour_weight])
    both = both.reshape(2, width, feats, hidden_dev).transpose(2, 0, 1, 3)
    both = lax.all_to_all(both, "feat", 0, 0).reshape(stacks, CORES, 2, width, hidden_dev)
    own_core = lax.dynamic_index_in_dim(both, core, 1, False)
    far_core = lax.dynamic_index_in_dim(both, 1 - core, 1, False)
    both = jnp.stack([own_core, far_core]).transpose(2, 0, 1, 3, 4)
    both = both.reshape(2, CORES * stacks * width, hidden_dev)
    weight_self, weight_neighbour = both[0], both[1]

    features_own, features_far = whole(turned)

    degrees = degree.reshape(1, node_dev)
    scalars = (tile_count, dest_block, source_block)
    tile_flops = 2 * OFFS * SLOTS * BLOCK * BLOCK * BLOCK
    aggregate = call(
        gather_kernel,
        [SMEM] * 3 + [VMEM] * (2 + OFFS),
        jax.ShapeDtypeStruct((width, node_dev), BF16),
        [pltpu.VMEM((blocks + 1, width, BLOCK), F32)],
        tile_flops,
        tile_values.size * 2,
    )(*scalars, tile_values, degrees, *incoming)
    aggregate_own, aggregate_far = whole(aggregate)

    half = stacks * width
    outs = [
        jax.ShapeDtypeStruct((hidden_dev, node_dev), F32 if offset == REACH else BF16)
        for offset in range(OFFS)
    ]
    middle = call(
        middle_kernel,
        [SMEM] * 3 + [VMEM] * 10,
        [
            jax.ShapeDtypeStruct((node_dev, hidden_dev), BF16),
            jax.ShapeDtypeStruct((hidden_dev, node_dev), BF16),
            jax.ShapeDtypeStruct((4 * half, hidden_dev), BF16),
            jax.ShapeDtypeStruct((8, hidden_dev), F32),
        ]
        + outs,
        [
            pltpu.VMEM((blocks, hidden_dev, BLOCK), BF16),
            pltpu.VMEM((blocks + 1, hidden_dev, BLOCK), F32),
        ],
        tile_flops * 2,
        tile_values.size * 2,
    )(
        *scalars,
        tile_values,
        degrees,
        features_own,
        features_far,
        aggregate_own,
        aggregate_far,
        weight_self,
        weight_neighbour,
        hidden_bias.reshape(1, hidden_dev),
        cotangent,
    )
    activations, grad_turned, weight_part, bias_part = middle[:4]
    outgoing = middle[4:]
    received = [
        shifted(outgoing[offset], offset - REACH) for offset in range(OFFS) if offset != REACH
    ]

    rows_each = 4 * half // groups
    weight_part = weight_part.reshape(groups, rows_each, hidden_dev)
    bias_rows = jnp.broadcast_to(bias_part.astype(BF16)[None], (groups, 8, hidden_dev))
    sent = jnp.concatenate([weight_part, bias_rows], axis=1)
    summed = jnp.sum(lax.all_to_all(sent, "rows", 0, 0).astype(F32), axis=0)
    grad_bias = summed[rows_each]
    piece = summed[:rows_each].astype(BF16)
    per_stack = groups // feats
    pairs = []
    for row in range(groups):
        far, stack, part = row // (groups // 2), row // per_stack % stacks, row % per_stack
        for feat in range(feats):
            column = stack * CORES + (feat % CORES + far) % CORES
            pairs.append((row * feats + feat, (part * feats + feat) * feats + column))
    piece = lax.ppermute(piece, ("rows", "feat"), pairs)
    pieces = lax.all_to_all(
        jnp.broadcast_to(piece[None], (groups,) + piece.shape), "rows", 0, 0
    )
    pieces = pieces.reshape(per_stack, feats, rows_each, hidden_dev).transpose(0, 2, 1, 3)
    pieces = pieces.reshape(2, width, feats * hidden_dev).astype(F32)

    keep, send = call(
        back_kernel,
        [VMEM] * (OFFS + 3),
        [
            jax.ShapeDtypeStruct((half, node_dev), F32),
            jax.ShapeDtypeStruct((half, node_dev), BF16),
        ],
        [],
        8 * half * node_dev * hidden_dev,
        4 * half * node_dev,
    )(outgoing[REACH], *received, grad_turned, weight_self, weight_neighbour)
    got = lax.ppermute(send, "feat", other_core)
    chip_sum = (keep + got.astype(F32)).astype(BF16).reshape(stacks, width, node_dev)
    grad_features = jnp.sum(over_stacks(chip_sum).astype(F32), axis=0).astype(BF16).T
    return (activations, grad_features, pieces[0], pieces[1], grad_bias)


def solution(mesh):
    in_specs = (
        P("rows", "feat"),
        P("rows", None, None),
        P("rows"),
        P("rows"),
        P("rows"),
        P("rows"),
        P("feat", None),
        P("feat", None),
        P("feat"),
        P("rows", "feat"),
    )
    out_specs = (P("rows", "feat"), P("rows", "feat"), P("feat", None), P("feat", None), P("feat"))
    return jax.shard_map(
        on_device, mesh=mesh, in_specs=in_specs, out_specs=out_specs, check_vma=False
    )
```

```python
import functools

import jax
import jax.numpy as jnp
from jax import lax
from jax.experimental import pallas as pl
from jax.experimental.pallas import tpu as pltpu
from jax.sharding import PartitionSpec as P

REACH = 3
SLOTS = 16
OFFS = 2 * REACH + 1
BLOCK = 128
GROUP = 4
CORES = 2
TRIO = 3
F32 = jnp.float32
BF16 = jnp.bfloat16
VMEM_BYTES = 40 * 1024 * 1024
VMEM = pl.BlockSpec(memory_space=pltpu.VMEM)
SMEM = pl.BlockSpec(memory_space=pltpu.SMEM)


def lanes(block):
    return pl.ds(pl.multiple_of(block * BLOCK, BLOCK), BLOCK)


def live_tiles(offset, count_ref, product, place_of, total_ref):
    count = count_ref[offset]
    spare = total_ref.shape[0] - 1

    def step(at, carry):
        products = []
        places = []
        for inner in range(GROUP):
            slot = at * GROUP + inner
            tile = offset * SLOTS + slot
            products.append(product(tile))
            places.append(jnp.where(slot < count, place_of(tile), spare))
        for place, value in zip(places, products):
            total_ref[place] += value
        return carry

    lax.fori_loop(0, (count + GROUP - 1) // GROUP, step, 0)


def band_slot(place_ref, offset):
    return (place_ref[0] + offset) // TRIO * TRIO + offset % TRIO


def pack_kernel(features_ref, self_ref, neighbour_ref, out_ref):
    width = features_ref.shape[0]
    for stack in range(out_ref.shape[0]):
        out_ref[stack, pl.ds(0, width), :] = features_ref[...]
        for core in range(CORES):
            for kind, ref in enumerate((self_ref, neighbour_ref)):
                out_ref[stack, pl.ds(width, width), pl.ds((core * 2 + kind) * BLOCK, BLOCK)] = ref[
                    :, pl.ds((stack * CORES + core) * BLOCK, BLOCK)
                ]


def gather_kernel(
    place_ref,
    count_ref,
    dest_ref,
    source_ref,
    tiles_ref,
    degree_ref,
    below_ref,
    level_ref,
    above_ref,
    out_ref,
    total_ref,
    band_ref,
):
    blocks = total_ref.shape[0] - 1
    total_ref[...] = jnp.zeros_like(total_ref)
    for trio, ref in enumerate((below_ref, level_ref, above_ref)):
        band_ref[pl.ds(trio * TRIO, TRIO)] = ref[...]
    for offset in range(OFFS):
        slot = band_slot(place_ref, offset)

        def product(tile, slot=slot):
            picked = band_ref[slot, :, lanes(source_ref[tile] % blocks)]
            return lax.dot_general(
                picked, tiles_ref[tile], (((1,), (1,)), ((), ())), preferred_element_type=F32
            )

        live_tiles(offset, count_ref, product, lambda tile: dest_ref[tile], total_ref)
    for block in range(blocks):
        part = pl.ds(block * BLOCK, BLOCK)
        value = (total_ref[block] / degree_ref[:, part].astype(F32)).astype(BF16)
        for copy in range(out_ref.shape[0]):
            out_ref[copy, :, part] = value


def middle_kernel(place_ref, core_ref, count_ref, dest_ref, source_ref, tiles_ref, degree_ref, *refs):
    packed, aggregates, refs = refs[:2], refs[2:4], refs[4:]
    bias_ref, cotangent_ref, refs = *refs[:2], refs[2:]
    act_ref, grad_ref, weight_ref, bias_out_ref, self_ref, neighbour_ref, refs = (
        *refs[:6],
        refs[6:],
    )
    below_ref, level_ref, above_ref, features_ref, scaled_ref, total_ref = refs
    blocks = scaled_ref.shape[0]
    stacks, width, _ = aggregates[0].shape
    half = stacks * width
    contract_first = (((0,), (0,)), ((), ()))
    for far, ref in enumerate(packed):
        for stack in range(stacks):
            rows = pl.ds(far * half + stack * width, width)
            features_ref[rows, :] = ref[stack, pl.ds(0, width), :]
            for kind, out in enumerate((self_ref, neighbour_ref)):
                out[rows, :] = ref[stack, pl.ds(width, width), lanes(core_ref[0] * 2 + kind)]
    pre = lax.dot_general(
        self_ref[...], features_ref[...], contract_first, preferred_element_type=F32
    )
    for far, ref in enumerate(aggregates):
        pre = pre + lax.dot_general(
            neighbour_ref[pl.ds(far * half, half), :],
            ref[...].reshape(half, -1),
            contract_first,
            preferred_element_type=F32,
        )
    preact = pre.T + bias_ref[...].astype(F32)
    gate_value = jax.nn.sigmoid(preact)
    act_ref[...] = (preact * gate_value).astype(BF16)
    grad = cotangent_ref[...].astype(F32) * gate_value * (1.0 + preact * (1.0 - gate_value))
    grad_pre = grad.astype(BF16)
    grad = grad_pre.astype(F32)
    bias_out_ref[...] = jnp.broadcast_to(
        jnp.sum(grad, axis=0, keepdims=True), bias_out_ref.shape
    ).astype(bias_out_ref.dtype)
    turned = grad.T
    grad_ref[...] = turned.astype(BF16)
    scaled = (turned / degree_ref[...].astype(F32)).astype(BF16)
    for block in range(blocks):
        scaled_ref[block] = scaled[:, block * BLOCK : (block + 1) * BLOCK]
    for far in range(CORES):
        operands = (features_ref[pl.ds(far * half, half), :], aggregates[far][...].reshape(half, -1))
        for kind, operand in enumerate(operands):
            term = jnp.dot(operand, grad_pre, preferred_element_type=F32).astype(BF16)
            for stack in range(stacks):
                first = ((far * stacks + stack) * 2 + kind) * width
                weight_ref[pl.ds(first, width), :] = term[stack * width : (stack + 1) * width]
    total_ref[...] = jnp.zeros_like(total_ref)
    for offset in range(OFFS):
        slot = band_slot(place_ref, offset)

        def product(tile):
            return jnp.dot(
                scaled_ref[dest_ref[tile]], tiles_ref[tile], preferred_element_type=F32
            )

        def place(tile, slot=slot):
            return slot * blocks + source_ref[tile] % blocks

        live_tiles(offset, count_ref, product, place, total_ref)
    for trio, out in enumerate((below_ref, level_ref, above_ref)):
        for slot in range(TRIO):
            for block in range(blocks):
                out[slot, :, pl.ds(block * BLOCK, BLOCK)] = total_ref[
                    (trio * TRIO + slot) * blocks + block
                ].astype(out.dtype)


def trio_kernel(level_ref, below_ref, above_ref, *outs):
    for slot, out in enumerate(outs):
        value = level_ref[slot] + below_ref[slot].astype(F32) + above_ref[slot].astype(F32)
        out[...] = value.astype(out.dtype)


def back_kernel(own_ref, first_ref, second_ref, grad_ref, self_ref, neighbour_ref, keep_ref, send_ref):
    spread = own_ref[...] + first_ref[...].astype(F32) + second_ref[...].astype(F32)
    spread = spread.astype(BF16)
    half = keep_ref.shape[0]
    for at, out in enumerate((keep_ref, send_ref)):
        rows = pl.ds(at * half, half)
        value = jnp.dot(self_ref[rows, :], grad_ref[...], preferred_element_type=F32)
        value = value + jnp.dot(neighbour_ref[rows, :], spread, preferred_element_type=F32)
        out[...] = value.astype(out.dtype)


def chip_kernel(stack_ref, keep_ref, got_ref, *outs):
    for at, out in enumerate(outs):
        piece = (stack_ref[0] + at) % len(outs)
        out[...] = (keep_ref[piece] + got_ref[piece].astype(F32)).astype(out.dtype)


def lay_kernel(pieces_ref, self_ref, neighbour_ref):
    groups, rows, lane = pieces_ref.shape
    feats = self_ref.shape[1] // lane
    for piece in range(groups):
        part, feat = piece // feats, piece % feats
        for first in range(0, rows, 16):
            kind, row = divmod(part * rows + first, self_ref.shape[0])
            out = (self_ref, neighbour_ref)[kind]
            out[pl.ds(row, 16), pl.ds(feat * lane, lane)] = pieces_ref[
                piece, pl.ds(first, 16), :
            ].astype(F32)


def call(kernel, in_specs, out_shape, scratch, flops, moved):
    return pl.pallas_call(
        kernel,
        in_specs=in_specs,
        out_shape=out_shape,
        out_specs=jax.tree.map(lambda _: VMEM, out_shape),
        scratch_shapes=scratch,
        compiler_params=pltpu.CompilerParams(vmem_limit_bytes=VMEM_BYTES),
        cost_estimate=pl.CostEstimate(flops=flops, bytes_accessed=moved, transcendentals=0),
    )


def shifted(value, steps):
    count = lax.axis_size("rows")
    pairs = [(source, (source + steps) % count) for source in range(count)]
    return lax.ppermute(value, "rows", pairs)


def turned_in_trio(value, steps):
    count = lax.axis_size("rows")
    pairs = [
        (source, source // TRIO * TRIO + (source + steps) % TRIO) for source in range(count)
    ]
    return lax.ppermute(value, "rows", pairs)


def on_device(
    features,
    tile_values,
    dest_block,
    source_block,
    tile_count,
    degree,
    self_weight,
    neighbour_weight,
    hidden_bias,
    cotangent,
):
    node_dev, width = features.shape
    blocks = node_dev // BLOCK
    groups = lax.axis_size("rows")
    feats = lax.axis_size("feat")
    stacks = feats // CORES
    half = stacks * width
    hidden_dev = hidden_bias.shape[0]
    core = (lax.axis_index("feat") % CORES).reshape(1)
    stack = (lax.axis_index("feat") // CORES).reshape(1)
    place = (lax.axis_index("rows") % TRIO).reshape(1)
    same_core = [[z * CORES + c for z in range(stacks)] for c in range(CORES)]
    other_core = [(f, f ^ 1) for f in range(feats)]

    def over_stacks(value):
        return lax.all_to_all(value, "feat", 0, 0, axis_index_groups=same_core)

    def to_stack(value, steps):
        pairs = [(f, (f + steps * CORES) % feats) for f in range(feats)]
        return lax.ppermute(value, "feat", pairs)

    turned = features.T
    level = jnp.stack([turned, turned_in_trio(turned, -1), turned_in_trio(turned, -2)])
    below = shifted(level, TRIO)
    above = shifted(level, -TRIO)

    packed = call(
        pack_kernel,
        [VMEM] * 3,
        jax.ShapeDtypeStruct((stacks, 2 * width, node_dev), BF16),
        [],
        0,
        6 * stacks * width * node_dev,
    )(turned, self_weight, neighbour_weight)
    packed_own = over_stacks(packed)
    packed_far = lax.ppermute(packed_own, "feat", other_core)

    degrees = degree.reshape(1, node_dev)
    scalars = (tile_count, dest_block, source_block)
    tile_flops = 2 * OFFS * SLOTS * BLOCK * BLOCK * BLOCK
    aggregate = call(
        gather_kernel,
        [SMEM] * 4 + [VMEM] * 5,
        jax.ShapeDtypeStruct((stacks, width, node_dev), BF16),
        [
            pltpu.VMEM((blocks + 1, width, BLOCK), F32),
            pltpu.VMEM((TRIO * TRIO, width, node_dev), BF16),
        ],
        tile_flops,
        tile_values.size * 2,
    )(place, *scalars, tile_values, degrees, below, level, above)
    aggregate_own = over_stacks(aggregate)
    aggregate_far = lax.ppermute(aggregate_own, "feat", other_core)

    def trio(dtype):
        return jax.ShapeDtypeStruct((TRIO, hidden_dev, node_dev), dtype)

    middle = call(
        middle_kernel,
        [SMEM] * 5 + [VMEM] * 8,
        [
            jax.ShapeDtypeStruct((node_dev, hidden_dev), BF16),
            jax.ShapeDtypeStruct((hidden_dev, node_dev), BF16),
            jax.ShapeDtypeStruct((4 * half, hidden_dev), BF16),
            jax.ShapeDtypeStruct((8, hidden_dev), F32),
            jax.ShapeDtypeStruct((2 * half, hidden_dev), BF16),
            jax.ShapeDtypeStruct((2 * half, hidden_dev), BF16),
            trio(BF16),
            trio(F32),
            trio(BF16),
        ],
        [
            pltpu.VMEM((2 * half, node_dev), BF16),
            pltpu.VMEM((blocks, hidden_dev, BLOCK), BF16),
            pltpu.VMEM((TRIO * TRIO * blocks + 1, hidden_dev, BLOCK), F32),
        ],
        tile_flops * 2,
        tile_values.size * 2,
    )(
        place,
        core,
        *scalars,
        tile_values,
        degrees,
        packed_own,
        packed_far,
        aggregate_own,
        aggregate_far,
        hidden_bias.reshape(1, hidden_dev),
        cotangent,
    )
    activations, grad_turned, weight_part, bias_part, weight_self, weight_neighbour = middle[:6]
    to_below, to_level, to_above = middle[6:]
    from_above = shifted(to_below, -TRIO)
    from_below = shifted(to_above, TRIO)

    rows_each = 4 * half // groups
    weight_part = weight_part.reshape(groups, rows_each, hidden_dev)
    bias_rows = jnp.broadcast_to(bias_part.astype(BF16)[None], (groups, 8, hidden_dev))
    sent = jnp.concatenate([weight_part, bias_rows], axis=1)
    summed = jnp.sum(lax.all_to_all(sent, "rows", 0, 0).astype(F32), axis=0)
    grad_bias = summed[rows_each]
    piece = summed[:rows_each].astype(BF16)
    per_stack = groups // feats
    pairs = []
    for row in range(groups):
        far, at, part = row // (groups // 2), row // per_stack % stacks, row % per_stack
        for feat in range(feats):
            column = at * CORES + (feat % CORES + far) % CORES
            pairs.append((row * feats + feat, (part * feats + feat) * feats + column))
    piece = lax.ppermute(piece, ("rows", "feat"), pairs)
    pieces = lax.all_to_all(
        jnp.broadcast_to(piece[None], (groups,) + piece.shape), "rows", 0, 0
    )
    grad_weight = jax.ShapeDtypeStruct((width, feats * hidden_dev), F32)
    grad_self, grad_neighbour = call(
        lay_kernel, [VMEM], [grad_weight, grad_weight], [], 0, pieces.size * 6
    )(pieces)

    spread = jax.ShapeDtypeStruct((hidden_dev, node_dev), BF16)
    own, first, second = call(
        trio_kernel,
        [VMEM] * 3,
        [jax.ShapeDtypeStruct(spread.shape, F32), spread, spread],
        [],
        9 * spread.size,
        20 * spread.size,
    )(to_level, from_below, from_above)
    first = turned_in_trio(first, 1)
    second = turned_in_trio(second, 2)
    keep, send = call(
        back_kernel,
        [VMEM] * 6,
        [
            jax.ShapeDtypeStruct((half, node_dev), F32),
            jax.ShapeDtypeStruct((half, node_dev), BF16),
        ],
        [],
        8 * half * node_dev * hidden_dev,
        4 * half * node_dev,
    )(own, first, second, grad_turned, weight_self, weight_neighbour)
    got = lax.ppermute(send, "feat", other_core)
    part = jax.ShapeDtypeStruct((width, node_dev), BF16)
    parts = call(
        chip_kernel,
        [SMEM] + [VMEM] * 2,
        [jax.ShapeDtypeStruct(part.shape, F32)] + [part] * (stacks - 1),
        [],
        4 * half * node_dev,
        8 * half * node_dev,
    )(
        stack,
        keep.reshape(stacks, width, node_dev),
        got.reshape(stacks, width, node_dev),
    )
    grad_turned = parts[0]
    for steps in range(1, stacks):
        grad_turned = grad_turned + to_stack(parts[steps], steps).astype(F32)
    return (activations, grad_turned.astype(BF16).T, grad_self, grad_neighbour, grad_bias)


def solution(mesh):
    in_specs = (
        P("rows", "feat"),
        P("rows", None, None),
        P("rows"),
        P("rows"),
        P("rows"),
        P("rows"),
        P("feat", None),
        P("feat", None),
        P("feat"),
        P("rows", "feat"),
    )
    out_specs = (P("rows", "feat"), P("rows", "feat"), P("feat", None), P("feat", None), P("feat"))
    return jax.shard_map(
        on_device, mesh=mesh, in_specs=in_specs, out_specs=out_specs, check_vma=False
    )
```

```python
import functools

import jax
import jax.numpy as jnp
from jax import lax
from jax.experimental import pallas as pl
from jax.experimental.pallas import tpu as pltpu
from jax.sharding import PartitionSpec as P

REACH = 3
SLOTS = 16
OFFS = 2 * REACH + 1
BLOCK = 128
GROUP = 4
CORES = 2
TRIO = 3
F32 = jnp.float32
BF16 = jnp.bfloat16
VMEM_BYTES = 16 * 1024 * 1024
TILES_VMEM_BYTES = 60_500_000
VMEM = pl.BlockSpec(memory_space=pltpu.VMEM)
SMEM = pl.BlockSpec(memory_space=pltpu.SMEM)
ANY = pl.BlockSpec(memory_space=pl.ANY)
HBM = pl.BlockSpec(memory_space=pltpu.HBM)
WHOLE = pl.BlockSpec()


def lanes(block):
    return pl.ds(pl.multiple_of(block * BLOCK, BLOCK), BLOCK)


def live_tiles(offset, count_ref, product, place_of, total_ref):
    count = count_ref[offset]
    spare = total_ref.shape[0] - 1

    def step(at, carry):
        products = []
        places = []
        for inner in range(GROUP):
            slot = at * GROUP + inner
            tile = offset * SLOTS + slot
            products.append(product(tile))
            places.append(jnp.where(slot < count, place_of(tile), spare))
        for place, value in zip(places, products):
            total_ref[place] += value
        return carry

    lax.fori_loop(0, (count + GROUP - 1) // GROUP, step, 0)


def band_slot(place_ref, offset):
    return (place_ref[0] + offset) // TRIO * TRIO + offset % TRIO


def pack_kernel(features_ref, first_ref, second_ref, self_ref, neighbour_ref, level_ref, out_ref):
    width = features_ref.shape[0]
    for slot, ref in enumerate((features_ref, first_ref, second_ref)):
        level_ref[slot] = ref[...]
    for stack in range(out_ref.shape[0]):
        out_ref[stack, pl.ds(0, width), :] = features_ref[...]
        for core in range(CORES):
            for kind, ref in enumerate((self_ref, neighbour_ref)):
                out_ref[stack, pl.ds(width, width), pl.ds((core * 2 + kind) * BLOCK, BLOCK)] = ref[
                    :, pl.ds((stack * CORES + core) * BLOCK, BLOCK)
                ]


def repeat_kernel(piece_ref, after_ref, out_ref):
    for copy in range(out_ref.shape[0]):
        out_ref[copy] = piece_ref[...]


def tile_copies(tiles_hbm, tiles_ref, copied):
    copies = []
    for offset in range(OFFS):
        part = pl.ds(offset * SLOTS, SLOTS)
        copies.append(
            pltpu.make_async_copy(tiles_hbm.at[part], tiles_ref.at[part], copied.at[offset])
        )
    for copy in copies:
        copy.start()
    return copies


def gather_kernel(
    place_ref,
    count_ref,
    dest_ref,
    source_ref,
    tiles_hbm,
    degree_ref,
    below_ref,
    level_ref,
    above_ref,
    out_ref,
    total_ref,
    band_ref,
    tiles_ref,
    copied,
):
    copies = tile_copies(tiles_hbm, tiles_ref, copied)
    blocks = total_ref.shape[0] - 1
    total_ref[...] = jnp.zeros_like(total_ref)
    for trio, ref in enumerate((below_ref, level_ref, above_ref)):
        band_ref[pl.ds(trio * TRIO, TRIO)] = ref[...]
    for offset in range(OFFS):
        slot = band_slot(place_ref, offset)

        def product(tile, slot=slot):
            picked = band_ref[slot, :, lanes(source_ref[tile] % blocks)]
            return lax.dot_general(
                picked, tiles_ref[tile], (((1,), (1,)), ((), ())), preferred_element_type=F32
            )

        copies[offset].wait()
        live_tiles(offset, count_ref, product, lambda tile: dest_ref[tile], total_ref)
    for block in range(blocks):
        part = pl.ds(block * BLOCK, BLOCK)
        value = (total_ref[block] / degree_ref[:, part].astype(F32)).astype(BF16)
        for copy in range(out_ref.shape[0]):
            out_ref[copy, :, part] = value


def middle_kernel(
    place_ref, core_ref, count_ref, dest_ref, source_ref, tiles_hbm, degree_ref, *refs
):
    packed, aggregates, refs = refs[:2], refs[2:4], refs[4:]
    bias_ref, cotangent_ref, refs = *refs[:2], refs[2:]
    act_ref, grad_ref, weight_ref, bias_out_ref, self_ref, neighbour_ref, refs = (
        *refs[:6],
        refs[6:],
    )
    level_ref, below_ref, above_ref, *refs = refs
    features_ref, scaled_ref, total_ref, tiles_ref, copied, *refs = refs
    turned_ref, to_below_ref, to_above_ref, stored = refs
    copies = tile_copies(tiles_hbm, tiles_ref, copied)
    stores = [
        pltpu.make_async_copy(source, target, stored.at[at])
        for at, (source, target) in enumerate(
            ((turned_ref, grad_ref), (to_below_ref, below_ref), (to_above_ref, above_ref))
        )
    ]
    blocks = scaled_ref.shape[0]
    stacks, width, _ = aggregates[0].shape
    half = stacks * width
    contract_first = (((0,), (0,)), ((), ()))
    for far, ref in enumerate(packed):
        for stack in range(stacks):
            rows = pl.ds(far * half + stack * width, width)
            features_ref[rows, :] = ref[stack, pl.ds(0, width), :]
            for kind, out in enumerate((self_ref, neighbour_ref)):
                out[rows, :] = ref[stack, pl.ds(width, width), lanes(core_ref[0] * 2 + kind)]
    pre = lax.dot_general(
        self_ref[...], features_ref[...], contract_first, preferred_element_type=F32
    )
    for far, ref in enumerate(aggregates):
        pre = pre + lax.dot_general(
            neighbour_ref[pl.ds(far * half, half), :],
            ref[...].reshape(half, -1),
            contract_first,
            preferred_element_type=F32,
        )
    preact = pre.T + bias_ref[...].astype(F32)
    gate_value = jax.nn.sigmoid(preact)
    act_ref[...] = (preact * gate_value).astype(BF16)
    grad = cotangent_ref[...].astype(F32) * gate_value * (1.0 + preact * (1.0 - gate_value))
    grad_pre = grad.astype(BF16)
    grad = grad_pre.astype(F32)
    bias_out_ref[...] = jnp.broadcast_to(
        jnp.sum(grad, axis=0, keepdims=True), bias_out_ref.shape
    ).astype(bias_out_ref.dtype)
    turned = grad.T
    turned_ref[...] = turned.astype(BF16)
    stores[0].start()
    scaled = (turned / degree_ref[...].astype(F32)).astype(BF16)
    for block in range(blocks):
        scaled_ref[block] = scaled[:, block * BLOCK : (block + 1) * BLOCK]
    for far in range(CORES):
        operands = (features_ref[pl.ds(far * half, half), :], aggregates[far][...].reshape(half, -1))
        for kind, operand in enumerate(operands):
            term = jnp.dot(operand, grad_pre, preferred_element_type=F32).astype(BF16)
            for stack in range(stacks):
                first = ((far * stacks + stack) * 2 + kind) * width
                weight_ref[pl.ds(first, width), :] = term[stack * width : (stack + 1) * width]
    total_ref[...] = jnp.zeros_like(total_ref)
    for offset in range(OFFS):
        slot = band_slot(place_ref, offset)

        def product(tile):
            return jnp.dot(
                scaled_ref[dest_ref[tile]], tiles_ref[tile], preferred_element_type=F32
            )

        def place(tile, slot=slot):
            return slot * blocks + source_ref[tile] % blocks

        copies[offset].wait()
        live_tiles(offset, count_ref, product, place, total_ref)
    for trio, out, store in (
        (0, to_below_ref, stores[1]),
        (2, to_above_ref, stores[2]),
        (1, level_ref, None),
    ):
        for slot in range(TRIO):
            for block in range(blocks):
                out[slot, :, pl.ds(block * BLOCK, BLOCK)] = total_ref[
                    (trio * TRIO + slot) * blocks + block
                ].astype(out.dtype)
        if store is not None:
            store.start()
    for store in stores:
        store.wait()


def trio_kernel(level_ref, below_ref, above_ref, *outs):
    for slot, out in enumerate(outs):
        value = level_ref[slot] + below_ref[slot].astype(F32) + above_ref[slot].astype(F32)
        out[...] = value.astype(out.dtype)


def back_kernel(own_ref, first_ref, second_ref, grad_ref, self_ref, neighbour_ref, keep_ref, send_ref):
    spread = own_ref[...] + first_ref[...].astype(F32) + second_ref[...].astype(F32)
    spread = spread.astype(BF16)
    half = keep_ref.shape[0]
    for at, out in enumerate((keep_ref, send_ref)):
        rows = pl.ds(at * half, half)
        value = jnp.dot(self_ref[rows, :], grad_ref[...], preferred_element_type=F32)
        value = value + jnp.dot(neighbour_ref[rows, :], spread, preferred_element_type=F32)
        out[...] = value.astype(out.dtype)


def chip_kernel(stack_ref, keep_ref, got_ref, *outs):
    for at, out in enumerate(outs):
        piece = (stack_ref[0] + at) % len(outs)
        out[...] = (keep_ref[piece] + got_ref[piece].astype(F32)).astype(out.dtype)


def lay_kernel(pieces_ref, self_ref, neighbour_ref):
    groups, rows, lane = pieces_ref.shape
    feats = self_ref.shape[1] // lane
    for piece in range(groups):
        part, feat = piece // feats, piece % feats
        for first in range(0, rows, 16):
            kind, row = divmod(part * rows + first, self_ref.shape[0])
            out = (self_ref, neighbour_ref)[kind]
            out[pl.ds(row, 16), pl.ds(feat * lane, lane)] = pieces_ref[
                piece, pl.ds(first, 16), :
            ].astype(F32)


def call(kernel, in_specs, out_shape, scratch, flops, moved, out_specs=None, limit=VMEM_BYTES):
    return pl.pallas_call(
        kernel,
        in_specs=in_specs,
        out_shape=out_shape,
        out_specs=out_specs or jax.tree.map(lambda _: VMEM, out_shape),
        scratch_shapes=scratch,
        compiler_params=pltpu.CompilerParams(vmem_limit_bytes=limit),
        cost_estimate=pl.CostEstimate(flops=flops, bytes_accessed=moved, transcendentals=0),
    )


def shifted(value, steps):
    count = lax.axis_size("rows")
    pairs = [(source, (source + steps) % count) for source in range(count)]
    return lax.ppermute(value, "rows", pairs)


def turned_in_trio(value, steps):
    count = lax.axis_size("rows")
    pairs = [
        (source, source // TRIO * TRIO + (source + steps) % TRIO) for source in range(count)
    ]
    return lax.ppermute(value, "rows", pairs)


def on_device(
    features,
    tile_values,
    dest_block,
    source_block,
    tile_count,
    degree,
    self_weight,
    neighbour_weight,
    hidden_bias,
    cotangent,
):
    node_dev, width = features.shape
    blocks = node_dev // BLOCK
    groups = lax.axis_size("rows")
    feats = lax.axis_size("feat")
    stacks = feats // CORES
    half = stacks * width
    hidden_dev = hidden_bias.shape[0]
    core = (lax.axis_index("feat") % CORES).reshape(1)
    stack = (lax.axis_index("feat") // CORES).reshape(1)
    place = (lax.axis_index("rows") % TRIO).reshape(1)
    same_core = [[z * CORES + c for z in range(stacks)] for c in range(CORES)]
    other_core = [(f, f ^ 1) for f in range(feats)]

    def over_stacks(value):
        return lax.all_to_all(value, "feat", 0, 0, axis_index_groups=same_core)

    def to_stack(value, steps):
        pairs = [(f, (f + steps * CORES) % feats) for f in range(feats)]
        return lax.ppermute(value, "feat", pairs)

    turned = features.T
    level, packed = call(
        pack_kernel,
        [WHOLE] * 5,
        [
            jax.ShapeDtypeStruct((TRIO, width, node_dev), BF16),
            jax.ShapeDtypeStruct((stacks, 2 * width, node_dev), BF16),
        ],
        [],
        0,
        6 * stacks * width * node_dev,
    )(
        turned,
        turned_in_trio(turned, -1),
        turned_in_trio(turned, -2),
        self_weight,
        neighbour_weight,
    )
    below = shifted(level, TRIO)
    above = shifted(level, -TRIO)
    packed_own = over_stacks(packed)
    packed_far = lax.ppermute(packed_own, "feat", other_core)

    degrees = degree.reshape(1, node_dev)
    scalars = (tile_count, dest_block, source_block)
    tile_flops = 2 * OFFS * SLOTS * BLOCK * BLOCK * BLOCK
    aggregate = call(
        gather_kernel,
        [SMEM] * 4 + [HBM] + [VMEM] * 4,
        jax.ShapeDtypeStruct((stacks, width, node_dev), BF16),
        [
            pltpu.VMEM((blocks + 1, width, BLOCK), F32),
            pltpu.VMEM((TRIO * TRIO, width, node_dev), BF16),
            pltpu.VMEM(tile_values.shape, BF16),
            pltpu.SemaphoreType.DMA((OFFS,)),
        ],
        tile_flops,
        tile_values.size * 2,
        limit=TILES_VMEM_BYTES,
    )(place, *scalars, tile_values, degrees, below, level, above)
    aggregate_own = over_stacks(aggregate)
    aggregate_far = lax.ppermute(aggregate_own, "feat", other_core)

    def trio(dtype):
        return jax.ShapeDtypeStruct((TRIO, hidden_dev, node_dev), dtype)

    middle = call(
        middle_kernel,
        [SMEM] * 5 + [HBM] + [VMEM] * 5 + [WHOLE] * 2,
        [
            jax.ShapeDtypeStruct((node_dev, hidden_dev), BF16),
            jax.ShapeDtypeStruct((hidden_dev, node_dev), BF16),
            jax.ShapeDtypeStruct((4 * half, hidden_dev), BF16),
            jax.ShapeDtypeStruct((8, hidden_dev), F32),
            jax.ShapeDtypeStruct((2 * half, hidden_dev), BF16),
            jax.ShapeDtypeStruct((2 * half, hidden_dev), BF16),
            trio(F32),
            trio(BF16),
            trio(BF16),
        ],
        [
            pltpu.VMEM((2 * half, node_dev), BF16),
            pltpu.VMEM((blocks, hidden_dev, BLOCK), BF16),
            pltpu.VMEM((TRIO * TRIO * blocks + 1, hidden_dev, BLOCK), F32),
            pltpu.VMEM(tile_values.shape, BF16),
            pltpu.SemaphoreType.DMA((OFFS,)),
            pltpu.VMEM((hidden_dev, node_dev), BF16),
            pltpu.VMEM((TRIO, hidden_dev, node_dev), BF16),
            pltpu.VMEM((TRIO, hidden_dev, node_dev), BF16),
            pltpu.SemaphoreType.DMA((3,)),
        ],
        tile_flops * 2,
        tile_values.size * 2,
        [WHOLE, HBM, VMEM, VMEM, VMEM, VMEM, VMEM, HBM, HBM],
        TILES_VMEM_BYTES,
    )(
        place,
        core,
        *scalars,
        tile_values,
        degrees,
        packed_own,
        packed_far,
        aggregate_own,
        aggregate_far,
        hidden_bias.reshape(1, hidden_dev),
        cotangent,
    )
    activations, grad_turned, weight_part, bias_part, weight_self, weight_neighbour = middle[:6]
    to_level, to_below, to_above = middle[6:]
    from_above = shifted(to_below, -TRIO)
    from_below = shifted(to_above, TRIO)

    rows_each = 4 * half // groups
    weight_part = weight_part.reshape(groups, rows_each, hidden_dev)
    bias_rows = jnp.broadcast_to(bias_part.astype(BF16)[None], (groups, 8, hidden_dev))
    sent = jnp.concatenate([weight_part, bias_rows], axis=1)
    summed = jnp.sum(lax.all_to_all(sent, "rows", 0, 0).astype(F32), axis=0)
    grad_bias = summed[rows_each]
    piece = summed[:rows_each].astype(BF16)
    per_stack = groups // feats
    pairs = []
    for row in range(groups):
        far, at, part = row // (groups // 2), row // per_stack % stacks, row % per_stack
        for feat in range(feats):
            column = at * CORES + (feat % CORES + far) % CORES
            pairs.append((row * feats + feat, (part * feats + feat) * feats + column))
    piece = lax.ppermute(piece, ("rows", "feat"), pairs)
    spread = jax.ShapeDtypeStruct((hidden_dev, node_dev), BF16)
    own, first, second = call(
        trio_kernel,
        [VMEM] * 3,
        [jax.ShapeDtypeStruct(spread.shape, F32), spread, spread],
        [],
        9 * spread.size,
        20 * spread.size,
    )(to_level, from_below, from_above)
    first = turned_in_trio(first, 1)
    second = turned_in_trio(second, 2)
    keep, send = call(
        back_kernel,
        [VMEM] * 6,
        [
            jax.ShapeDtypeStruct((half, node_dev), F32),
            jax.ShapeDtypeStruct((half, node_dev), BF16),
        ],
        [],
        8 * half * node_dev * hidden_dev,
        4 * half * node_dev,
    )(own, first, second, grad_turned, weight_self, weight_neighbour)
    got = lax.ppermute(send, "feat", other_core)
    part = jax.ShapeDtypeStruct((width, node_dev), BF16)
    parts = call(
        chip_kernel,
        [SMEM] + [VMEM] * 2,
        [jax.ShapeDtypeStruct(part.shape, F32)] + [part] * (stacks - 1),
        [],
        4 * half * node_dev,
        8 * half * node_dev,
    )(
        stack,
        keep.reshape(stacks, width, node_dev),
        got.reshape(stacks, width, node_dev),
    )
    pieces = lax.all_to_all(
        call(
            repeat_kernel,
            [VMEM, ANY],
            jax.ShapeDtypeStruct((groups,) + piece.shape, BF16),
            [],
            0,
            groups * piece.size * 2,
        )(piece, parts[0]),
        "rows",
        0,
        0,
    )
    grad_weight = jax.ShapeDtypeStruct((width, feats * hidden_dev), F32)
    grad_self, grad_neighbour = call(
        lay_kernel, [VMEM], [grad_weight, grad_weight], [], 0, pieces.size * 6
    )(pieces)

    grad_turned = parts[0]
    for steps in range(1, stacks):
        grad_turned = grad_turned + to_stack(parts[steps], steps).astype(F32)
    return (activations, grad_turned.astype(BF16).T, grad_self, grad_neighbour, grad_bias)


def solution(mesh):
    in_specs = (
        P("rows", "feat"),
        P("rows", None, None),
        P("rows"),
        P("rows"),
        P("rows"),
        P("rows"),
        P("feat", None),
        P("feat", None),
        P("feat"),
        P("rows", "feat"),
    )
    out_specs = (P("rows", "feat"), P("rows", "feat"), P("feat", None), P("feat", None), P("feat"))
    return jax.shard_map(
        on_device, mesh=mesh, in_specs=in_specs, out_specs=out_specs, check_vma=False
    )
```

```python
import functools

import jax
import jax.numpy as jnp
from jax import lax
from jax.experimental import pallas as pl
from jax.experimental.pallas import tpu as pltpu
from jax.sharding import PartitionSpec as P

REACH = 3
SLOTS = 16
OFFS = 2 * REACH + 1
BLOCK = 128
GROUP = 4
CORES = 2
TRIO = 3
COLUMN = 8
PIECE = 16
F32 = jnp.float32
BF16 = jnp.bfloat16
VMEM_BYTES = 16 * 1024 * 1024
TILES_VMEM_BYTES = 60_500_000
VMEM = pl.BlockSpec(memory_space=pltpu.VMEM)
SMEM = pl.BlockSpec(memory_space=pltpu.SMEM)
ANY = pl.BlockSpec(memory_space=pl.ANY)
HBM = pl.BlockSpec(memory_space=pltpu.HBM)
WHOLE = pl.BlockSpec()


def lanes(block):
    return pl.ds(pl.multiple_of(block * BLOCK, BLOCK), BLOCK)


def live_tiles(offset, count_ref, product, place_of, total_ref):
    count = count_ref[offset]
    spare = total_ref.shape[0] - 1

    def step(at, carry):
        products = []
        places = []
        for inner in range(GROUP):
            slot = at * GROUP + inner
            tile = offset * SLOTS + slot
            products.append(product(tile))
            places.append(jnp.where(slot < count, place_of(tile), spare))
        for place, value in zip(places, products):
            total_ref[place] += value
        return carry

    lax.fori_loop(0, (count + GROUP - 1) // GROUP, step, 0)


def band_slot(place_ref, offset):
    return (place_ref[0] + offset) // TRIO * TRIO + offset % TRIO


def pack_kernel(features_ref, first_ref, second_ref, self_ref, neighbour_ref, level_ref, out_ref):
    width = features_ref.shape[0]
    for slot, ref in enumerate((features_ref, first_ref, second_ref)):
        level_ref[slot] = ref[...]
    for stack in range(out_ref.shape[0]):
        out_ref[stack, pl.ds(0, width), :] = features_ref[...]
        for core in range(CORES):
            for kind, ref in enumerate((self_ref, neighbour_ref)):
                out_ref[stack, pl.ds(width, width), pl.ds((core * 2 + kind) * BLOCK, BLOCK)] = ref[
                    :, pl.ds((stack * CORES + core) * BLOCK, BLOCK)
                ]


def tile_copies(tiles_hbm, tiles_ref, copied):
    copies = []
    for offset in range(OFFS):
        part = pl.ds(offset * SLOTS, SLOTS)
        copies.append(
            pltpu.make_async_copy(tiles_hbm.at[part], tiles_ref.at[part], copied.at[offset])
        )
    for copy in copies:
        copy.start()
    return copies


def gather_kernel(
    place_ref,
    count_ref,
    dest_ref,
    source_ref,
    tiles_hbm,
    degree_ref,
    below_ref,
    level_ref,
    above_ref,
    out_ref,
    total_ref,
    band_ref,
    tiles_ref,
    copied,
):
    copies = tile_copies(tiles_hbm, tiles_ref, copied)
    blocks = total_ref.shape[0] - 1
    total_ref[...] = jnp.zeros_like(total_ref)
    for trio, ref in enumerate((below_ref, level_ref, above_ref)):
        band_ref[pl.ds(trio * TRIO, TRIO)] = ref[...]
    for offset in range(OFFS):
        slot = band_slot(place_ref, offset)

        def product(tile, slot=slot):
            picked = band_ref[slot, :, lanes(source_ref[tile] % blocks)]
            return lax.dot_general(
                picked, tiles_ref[tile], (((1,), (1,)), ((), ())), preferred_element_type=F32
            )

        copies[offset].wait()
        live_tiles(offset, count_ref, product, lambda tile: dest_ref[tile], total_ref)
    for block in range(blocks):
        part = pl.ds(block * BLOCK, BLOCK)
        value = (total_ref[block] / degree_ref[:, part].astype(F32)).astype(BF16)
        for copy in range(out_ref.shape[0]):
            out_ref[copy, :, part] = value


def middle_kernel(
    place_ref, core_ref, stack_ref, count_ref, dest_ref, source_ref, tiles_hbm, degree_ref, *refs
):
    packed, aggregates, refs = refs[:2], refs[2:4], refs[4:]
    bias_ref, cotangent_ref, refs = *refs[:2], refs[2:]
    act_ref, grad_ref, weight_ref, self_ref, neighbour_ref, refs = *refs[:5], refs[5:]
    level_ref, below_ref, above_ref, *refs = refs
    features_ref, scaled_ref, total_ref, tiles_ref, copied, *refs = refs
    turned_ref, to_below_ref, to_above_ref, stored = refs
    copies = tile_copies(tiles_hbm, tiles_ref, copied)
    stores = [
        pltpu.make_async_copy(source, target, stored.at[at])
        for at, (source, target) in enumerate(
            ((turned_ref, grad_ref), (to_below_ref, below_ref), (to_above_ref, above_ref))
        )
    ]
    blocks = scaled_ref.shape[0]
    stacks, width, _ = aggregates[0].shape
    half = stacks * width
    contract_first = (((0,), (0,)), ((), ()))
    for far, ref in enumerate(packed):
        for stack in range(stacks):
            rows = pl.ds(far * half + stack * width, width)
            features_ref[rows, :] = ref[stack, pl.ds(0, width), :]
            for kind, out in enumerate((self_ref, neighbour_ref)):
                out[rows, :] = ref[stack, pl.ds(width, width), lanes(core_ref[0] * 2 + kind)]
    pre = lax.dot_general(
        self_ref[...], features_ref[...], contract_first, preferred_element_type=F32
    )
    for far, ref in enumerate(aggregates):
        pre = pre + lax.dot_general(
            neighbour_ref[pl.ds(far * half, half), :],
            ref[...].reshape(half, -1),
            contract_first,
            preferred_element_type=F32,
        )
    preact = pre.T + bias_ref[...].astype(F32)
    gate_value = jax.nn.sigmoid(preact)
    act_ref[...] = (preact * gate_value).astype(BF16)
    grad = cotangent_ref[...].astype(F32) * gate_value * (1.0 + preact * (1.0 - gate_value))
    grad_pre = grad.astype(BF16)
    grad = grad_pre.astype(F32)
    planes, _, rows, lane = weight_ref.shape
    bias_rows = jnp.broadcast_to(jnp.sum(grad, axis=0, keepdims=True), (rows, lane)).astype(BF16)
    for plane in range(planes):
        weight_ref[plane, COLUMN] = bias_rows
    turned = grad.T
    turned_ref[...] = turned.astype(BF16)
    stores[0].start()
    scaled = (turned / degree_ref[...].astype(F32)).astype(BF16)
    for block in range(blocks):
        scaled_ref[block] = scaled[:, block * BLOCK : (block + 1) * BLOCK]
    for far in range(CORES):
        operands = (features_ref[pl.ds(far * half, half), :], aggregates[far][...].reshape(half, -1))
        for kind, operand in enumerate(operands):
            term = jnp.dot(operand, grad_pre, preferred_element_type=F32).astype(BF16)
            for stack in range(stacks):
                column = (stack ^ stack_ref[0]) * CORES + far
                for first in range(0, width, PIECE):
                    plane, row = divmod(kind * width + first, rows)
                    begin = stack * width + first
                    weight_ref[plane, column, pl.ds(row, PIECE), :] = term[begin : begin + PIECE]
    total_ref[...] = jnp.zeros_like(total_ref)
    for offset in range(OFFS):
        slot = band_slot(place_ref, offset)

        def product(tile):
            return jnp.dot(
                scaled_ref[dest_ref[tile]], tiles_ref[tile], preferred_element_type=F32
            )

        def place(tile, slot=slot):
            return slot * blocks + source_ref[tile] % blocks

        copies[offset].wait()
        live_tiles(offset, count_ref, product, place, total_ref)
    for trio, out, store in (
        (0, to_below_ref, stores[1]),
        (2, to_above_ref, stores[2]),
        (1, level_ref, None),
    ):
        for slot in range(TRIO):
            for block in range(blocks):
                out[slot, :, pl.ds(block * BLOCK, BLOCK)] = total_ref[
                    (trio * TRIO + slot) * blocks + block
                ].astype(out.dtype)
        if store is not None:
            store.start()
    for store in stores:
        store.wait()


def trio_kernel(level_ref, below_ref, above_ref, *outs):
    for slot, out in enumerate(outs):
        value = level_ref[slot] + below_ref[slot].astype(F32) + above_ref[slot].astype(F32)
        out[...] = value.astype(out.dtype)


def back_kernel(own_ref, first_ref, second_ref, grad_ref, self_ref, neighbour_ref, keep_ref, send_ref):
    spread = own_ref[...] + first_ref[...].astype(F32) + second_ref[...].astype(F32)
    spread = spread.astype(BF16)
    half = keep_ref.shape[0]
    for at, out in enumerate((keep_ref, send_ref)):
        rows = pl.ds(at * half, half)
        value = jnp.dot(self_ref[rows, :], grad_ref[...], preferred_element_type=F32)
        value = value + jnp.dot(neighbour_ref[rows, :], spread, preferred_element_type=F32)
        out[...] = value.astype(out.dtype)


def chip_kernel(stack_ref, keep_ref, got_ref, *outs):
    for at, out in enumerate(outs):
        piece = (stack_ref[0] + at) % len(outs)
        out[...] = (keep_ref[piece] + got_ref[piece].astype(F32)).astype(out.dtype)


def planes_kernel(got_ref, out_ref):
    for column in range(COLUMN + 1):
        value = got_ref[0, column].astype(F32)
        for plane in range(1, got_ref.shape[0]):
            value = value + got_ref[plane, column].astype(F32)
        value = value.astype(BF16)
        if column < COLUMN:
            out_ref[column, 0] = value
        else:
            for copy in range(COLUMN):
                out_ref[copy, 1] = value


def column_kernel(got_ref, piece_ref, bias_ref):
    for at, out in enumerate((piece_ref, bias_ref)):
        value = got_ref[0, at].astype(F32)
        for column in range(1, COLUMN):
            value = value + got_ref[column, at].astype(F32)
        out[...] = value.astype(out.dtype)


def lay_kernel(feat_ref, pieces_ref, self_ref, neighbour_ref):
    planes, _, rows, _ = pieces_ref.shape
    for plane in range(planes):
        for first in range(0, rows, PIECE):
            kind, row = divmod(plane * rows + first, self_ref.shape[0])
            out = (self_ref, neighbour_ref)[kind]
            for column in range(COLUMN):
                out[pl.ds(row, PIECE), lanes(column ^ feat_ref[0])] = pieces_ref[
                    plane, column, pl.ds(first, PIECE), :
                ].astype(F32)


def call(kernel, in_specs, out_shape, scratch, flops, moved, out_specs=None, limit=VMEM_BYTES):
    return pl.pallas_call(
        kernel,
        in_specs=in_specs,
        out_shape=out_shape,
        out_specs=out_specs or jax.tree.map(lambda _: VMEM, out_shape),
        scratch_shapes=scratch,
        compiler_params=pltpu.CompilerParams(vmem_limit_bytes=limit),
        cost_estimate=pl.CostEstimate(flops=flops, bytes_accessed=moved, transcendentals=0),
    )


def shifted(value, steps):
    count = lax.axis_size("rows")
    pairs = [(source, (source + steps) % count) for source in range(count)]
    return lax.ppermute(value, "rows", pairs)


def turned_in_trio(value, steps):
    count = lax.axis_size("rows")
    pairs = [
        (source, source // TRIO * TRIO + (source + steps) % TRIO) for source in range(count)
    ]
    return lax.ppermute(value, "rows", pairs)


def on_device(
    features,
    tile_values,
    dest_block,
    source_block,
    tile_count,
    degree,
    self_weight,
    neighbour_weight,
    hidden_bias,
    cotangent,
):
    node_dev, width = features.shape
    blocks = node_dev // BLOCK
    groups = lax.axis_size("rows")
    feats = lax.axis_size("feat")
    stacks = feats // CORES
    half = stacks * width
    hidden_dev = hidden_bias.shape[0]
    core = (lax.axis_index("feat") % CORES).reshape(1)
    stack = (lax.axis_index("feat") // CORES).reshape(1)
    place = (lax.axis_index("rows") % TRIO).reshape(1)
    same_core = [[z * CORES + c for z in range(stacks)] for c in range(CORES)]
    other_core = [(f, f ^ 1) for f in range(feats)]
    same_plane = [
        [(p // TRIO * COLUMN + c) * TRIO + p % TRIO for c in range(COLUMN)]
        for p in range(groups // COLUMN)
    ]
    same_column = [list(members) for members in zip(*same_plane)]

    def over_stacks(value):
        return lax.all_to_all(value, "feat", 0, 0, axis_index_groups=same_core)

    def to_stack(value, steps):
        pairs = [(f, (f + steps * CORES) % feats) for f in range(feats)]
        return lax.ppermute(value, "feat", pairs)

    turned = features.T
    level, packed = call(
        pack_kernel,
        [WHOLE] * 5,
        [
            jax.ShapeDtypeStruct((TRIO, width, node_dev), BF16),
            jax.ShapeDtypeStruct((stacks, 2 * width, node_dev), BF16),
        ],
        [],
        0,
        6 * stacks * width * node_dev,
    )(
        turned,
        turned_in_trio(turned, -1),
        turned_in_trio(turned, -2),
        self_weight,
        neighbour_weight,
    )
    below = shifted(level, TRIO)
    above = shifted(level, -TRIO)
    packed_own = over_stacks(packed)
    packed_far = lax.ppermute(packed_own, "feat", other_core)

    degrees = degree.reshape(1, node_dev)
    scalars = (tile_count, dest_block, source_block)
    tile_flops = 2 * OFFS * SLOTS * BLOCK * BLOCK * BLOCK
    aggregate = call(
        gather_kernel,
        [SMEM] * 4 + [HBM] + [VMEM] * 4,
        jax.ShapeDtypeStruct((stacks, width, node_dev), BF16),
        [
            pltpu.VMEM((blocks + 1, width, BLOCK), F32),
            pltpu.VMEM((TRIO * TRIO, width, node_dev), BF16),
            pltpu.VMEM(tile_values.shape, BF16),
            pltpu.SemaphoreType.DMA((OFFS,)),
        ],
        tile_flops,
        tile_values.size * 2,
        limit=TILES_VMEM_BYTES,
    )(place, *scalars, tile_values, degrees, below, level, above)
    aggregate_own = over_stacks(aggregate)
    aggregate_far = lax.ppermute(aggregate_own, "feat", other_core)

    planes = groups // COLUMN
    rows_each = 4 * half // groups

    def trio(dtype):
        return jax.ShapeDtypeStruct((TRIO, hidden_dev, node_dev), dtype)

    middle = call(
        middle_kernel,
        [SMEM] * 6 + [HBM] + [VMEM] * 5 + [WHOLE] * 2,
        [
            jax.ShapeDtypeStruct((node_dev, hidden_dev), BF16),
            jax.ShapeDtypeStruct((hidden_dev, node_dev), BF16),
            jax.ShapeDtypeStruct((planes, COLUMN + 1, rows_each, hidden_dev), BF16),
            jax.ShapeDtypeStruct((2 * half, hidden_dev), BF16),
            jax.ShapeDtypeStruct((2 * half, hidden_dev), BF16),
            trio(F32),
            trio(BF16),
            trio(BF16),
        ],
        [
            pltpu.VMEM((2 * half, node_dev), BF16),
            pltpu.VMEM((blocks, hidden_dev, BLOCK), BF16),
            pltpu.VMEM((TRIO * TRIO * blocks + 1, hidden_dev, BLOCK), F32),
            pltpu.VMEM(tile_values.shape, BF16),
            pltpu.SemaphoreType.DMA((OFFS,)),
            pltpu.VMEM((hidden_dev, node_dev), BF16),
            pltpu.VMEM((TRIO, hidden_dev, node_dev), BF16),
            pltpu.VMEM((TRIO, hidden_dev, node_dev), BF16),
            pltpu.SemaphoreType.DMA((3,)),
        ],
        tile_flops * 2,
        tile_values.size * 2,
        [WHOLE, HBM, VMEM, VMEM, VMEM, VMEM, HBM, HBM],
        TILES_VMEM_BYTES,
    )(
        place,
        core,
        stack,
        *scalars,
        tile_values,
        degrees,
        packed_own,
        packed_far,
        aggregate_own,
        aggregate_far,
        hidden_bias.reshape(1, hidden_dev),
        cotangent,
    )
    activations, grad_turned, weight_part, weight_self, weight_neighbour = middle[:5]
    to_level, to_below, to_above = middle[5:]
    from_above = shifted(to_below, -TRIO)
    from_below = shifted(to_above, TRIO)

    got = jax.ShapeDtypeStruct((COLUMN, 2, rows_each, hidden_dev), BF16)
    got = call(planes_kernel, [VMEM], got, [], weight_part.size, weight_part.size * 2)(
        lax.all_to_all(weight_part, "rows", 0, 0, axis_index_groups=same_column)
    )
    piece = jax.ShapeDtypeStruct((rows_each, hidden_dev), BF16)
    piece, bias_sum = call(
        column_kernel,
        [VMEM],
        [piece, jax.ShapeDtypeStruct(piece.shape, F32)],
        [],
        got.size,
        got.size * 2,
    )(lax.all_to_all(got, "rows", 0, 0, axis_index_groups=same_plane))
    pairs = [
        (row * feats + feat, row * feats + (feat ^ (row // TRIO % COLUMN)))
        for row in range(groups)
        for feat in range(feats)
    ]
    piece = lax.ppermute(piece, ("rows", "feat"), pairs)
    pieces = lax.all_to_all(
        jnp.broadcast_to(piece[None], (COLUMN,) + piece.shape),
        "rows",
        0,
        0,
        axis_index_groups=same_plane,
    )
    pieces = lax.all_to_all(
        jnp.broadcast_to(pieces[None], (planes,) + pieces.shape),
        "rows",
        0,
        0,
        axis_index_groups=same_column,
    )
    grad_weight = jax.ShapeDtypeStruct((width, feats * hidden_dev), F32)
    grad_self, grad_neighbour = call(
        lay_kernel, [SMEM, VMEM], [grad_weight, grad_weight], [], 0, pieces.size * 6
    )(lax.axis_index("feat").reshape(1), pieces)

    spread = jax.ShapeDtypeStruct((hidden_dev, node_dev), BF16)
    own, first, second = call(
        trio_kernel,
        [VMEM] * 3,
        [jax.ShapeDtypeStruct(spread.shape, F32), spread, spread],
        [],
        9 * spread.size,
        20 * spread.size,
    )(to_level, from_below, from_above)
    first = turned_in_trio(first, 1)
    second = turned_in_trio(second, 2)
    keep, send = call(
        back_kernel,
        [VMEM] * 6,
        [
            jax.ShapeDtypeStruct((half, node_dev), F32),
            jax.ShapeDtypeStruct((half, node_dev), BF16),
        ],
        [],
        8 * half * node_dev * hidden_dev,
        4 * half * node_dev,
    )(own, first, second, grad_turned, weight_self, weight_neighbour)
    got = lax.ppermute(send, "feat", other_core)
    part = jax.ShapeDtypeStruct((width, node_dev), BF16)
    parts = call(
        chip_kernel,
        [SMEM] + [VMEM] * 2,
        [jax.ShapeDtypeStruct(part.shape, F32)] + [part] * (stacks - 1),
        [],
        4 * half * node_dev,
        8 * half * node_dev,
    )(
        stack,
        keep.reshape(stacks, width, node_dev),
        got.reshape(stacks, width, node_dev),
    )
    grad_turned = parts[0]
    for steps in range(1, stacks):
        grad_turned = grad_turned + to_stack(parts[steps], steps).astype(F32)
    return (activations, grad_turned.astype(BF16).T, grad_self, grad_neighbour, bias_sum[0])


def solution(mesh):
    in_specs = (
        P("rows", "feat"),
        P("rows", None, None),
        P("rows"),
        P("rows"),
        P("rows"),
        P("rows"),
        P("feat", None),
        P("feat", None),
        P("feat"),
        P("rows", "feat"),
    )
    out_specs = (P("rows", "feat"), P("rows", "feat"), P("feat", None), P("feat", None), P("feat"))
    return jax.shard_map(
        on_device, mesh=mesh, in_specs=in_specs, out_specs=out_specs, check_vma=False
    )
```

```python
import functools

import jax
import jax.numpy as jnp
from jax import lax
from jax.experimental import pallas as pl
from jax.experimental.pallas import tpu as pltpu
from jax.sharding import PartitionSpec as P

REACH = 3
SLOTS = 16
OFFS = 2 * REACH + 1
BLOCK = 128
GROUP = 4
CORES = 2
TRIO = 3
COLUMN = 8
PIECE = 16
F32 = jnp.float32
BF16 = jnp.bfloat16
VMEM_BYTES = 16 * 1024 * 1024
TILES_VMEM_BYTES = 60_500_000
VMEM = pl.BlockSpec(memory_space=pltpu.VMEM)
SMEM = pl.BlockSpec(memory_space=pltpu.SMEM)
ANY = pl.BlockSpec(memory_space=pl.ANY)
HBM = pl.BlockSpec(memory_space=pltpu.HBM)
WHOLE = pl.BlockSpec()


def lanes(block):
    return pl.ds(pl.multiple_of(block * BLOCK, BLOCK), BLOCK)


def live_tiles(offset, count_ref, product, place_of, total_ref):
    count = count_ref[offset]
    spare = total_ref.shape[0] - 1

    def step(at, carry):
        products = []
        places = []
        for inner in range(GROUP):
            slot = at * GROUP + inner
            tile = offset * SLOTS + slot
            products.append(product(tile))
            places.append(jnp.where(slot < count, place_of(tile), spare))
        for place, value in zip(places, products):
            total_ref[place] += value
        return carry

    lax.fori_loop(0, (count + GROUP - 1) // GROUP, step, 0)


def relay_kernel(place_ref, below_ref, level_ref, above_ref, *outs):
    for steps, out in enumerate(outs, 1):

        @pl.when(place_ref[0] < steps)
        def _(out=out):
            out[0] = level_ref[...]
            out[1] = above_ref[...]

        @pl.when(place_ref[0] >= steps)
        def _(out=out):
            out[0] = below_ref[...]
            out[1] = level_ref[...]


def pack_kernel(features_ref, self_ref, neighbour_ref, first_ref, second_ref, out_ref):
    width = features_ref.shape[0]
    for stack in range(out_ref.shape[0]):
        out_ref[stack, pl.ds(0, width), :] = features_ref[...]
        for core in range(CORES):
            for kind, ref in enumerate((self_ref, neighbour_ref)):
                out_ref[stack, pl.ds(width, width), pl.ds((core * 2 + kind) * BLOCK, BLOCK)] = ref[
                    :, pl.ds((stack * CORES + core) * BLOCK, BLOCK)
                ]


def tile_copies(tiles_hbm, tiles_ref, copied):
    copies = []
    for offset in range(OFFS):
        part = pl.ds(offset * SLOTS, SLOTS)
        copies.append(
            pltpu.make_async_copy(tiles_hbm.at[part], tiles_ref.at[part], copied.at[offset])
        )
    for copy in copies:
        copy.start()
    return copies


def gather_kernel(
    count_ref,
    dest_ref,
    source_ref,
    tiles_hbm,
    degree_ref,
    below_ref,
    level_ref,
    above_ref,
    first_ref,
    second_ref,
    out_ref,
    total_ref,
    tiles_ref,
    copied,
):
    copies = tile_copies(tiles_hbm, tiles_ref, copied)
    blocks = total_ref.shape[0] - 1
    total_ref[...] = jnp.zeros_like(total_ref)
    straight = (below_ref, level_ref, above_ref)
    for offset in range(OFFS):
        turns, part = offset % TRIO, offset // TRIO
        operand = straight[part] if turns == 0 else (first_ref, second_ref)[turns - 1].at[part]

        def product(tile, operand=operand):
            picked = operand[:, lanes(source_ref[tile] % blocks)]
            return lax.dot_general(
                picked, tiles_ref[tile], (((1,), (1,)), ((), ())), preferred_element_type=F32
            )

        copies[offset].wait()
        live_tiles(offset, count_ref, product, lambda tile: dest_ref[tile], total_ref)
    for block in range(blocks):
        part = pl.ds(block * BLOCK, BLOCK)
        value = (total_ref[block] / degree_ref[:, part].astype(F32)).astype(BF16)
        for copy in range(out_ref.shape[0]):
            out_ref[copy, :, part] = value


def middle_kernel(
    core_ref, stack_ref, count_ref, dest_ref, source_ref, tiles_hbm, degree_ref, *refs
):
    packed, aggregates, refs = refs[:2], refs[2:4], refs[4:]
    bias_ref, cotangent_ref, refs = *refs[:2], refs[2:]
    act_ref, grad_ref, weight_ref, self_ref, neighbour_ref, refs = *refs[:5], refs[5:]
    level_ref, first_ref, second_ref, *refs = refs
    features_ref, scaled_ref, total_ref, tiles_ref, copied, *refs = refs
    turned_ref, to_first_ref, to_second_ref, stored = refs
    copies = tile_copies(tiles_hbm, tiles_ref, copied)
    stores = [
        pltpu.make_async_copy(source, target, stored.at[at])
        for at, (source, target) in enumerate(
            ((turned_ref, grad_ref), (to_first_ref, first_ref), (to_second_ref, second_ref))
        )
    ]
    blocks = scaled_ref.shape[0]
    stacks, width, _ = aggregates[0].shape
    half = stacks * width
    contract_first = (((0,), (0,)), ((), ()))
    for far, ref in enumerate(packed):
        for stack in range(stacks):
            rows = pl.ds(far * half + stack * width, width)
            features_ref[rows, :] = ref[stack, pl.ds(0, width), :]
            for kind, out in enumerate((self_ref, neighbour_ref)):
                out[rows, :] = ref[stack, pl.ds(width, width), lanes(core_ref[0] * 2 + kind)]
    pre = lax.dot_general(
        self_ref[...], features_ref[...], contract_first, preferred_element_type=F32
    )
    for far, ref in enumerate(aggregates):
        pre = pre + lax.dot_general(
            neighbour_ref[pl.ds(far * half, half), :],
            ref[...].reshape(half, -1),
            contract_first,
            preferred_element_type=F32,
        )
    preact = pre.T + bias_ref[...].astype(F32)
    gate_value = jax.nn.sigmoid(preact)
    act_ref[...] = (preact * gate_value).astype(BF16)
    grad = cotangent_ref[...].astype(F32) * gate_value * (1.0 + preact * (1.0 - gate_value))
    grad_pre = grad.astype(BF16)
    grad = grad_pre.astype(F32)
    planes, _, rows, lane = weight_ref.shape
    bias_rows = jnp.broadcast_to(jnp.sum(grad, axis=0, keepdims=True), (rows, lane)).astype(BF16)
    for plane in range(planes):
        weight_ref[plane, COLUMN] = bias_rows
    turned = grad.T
    turned_ref[...] = turned.astype(BF16)
    stores[0].start()
    scaled = (turned / degree_ref[...].astype(F32)).astype(BF16)
    for block in range(blocks):
        scaled_ref[block] = scaled[:, block * BLOCK : (block + 1) * BLOCK]
    for far in range(CORES):
        operands = (features_ref[pl.ds(far * half, half), :], aggregates[far][...].reshape(half, -1))
        for kind, operand in enumerate(operands):
            term = jnp.dot(operand, grad_pre, preferred_element_type=F32).astype(BF16)
            for stack in range(stacks):
                column = (stack ^ stack_ref[0]) * CORES + far
                for first in range(0, width, PIECE):
                    plane, row = divmod(kind * width + first, rows)
                    begin = stack * width + first
                    weight_ref[plane, column, pl.ds(row, PIECE), :] = term[begin : begin + PIECE]
    total_ref[...] = jnp.zeros_like(total_ref)
    for offset in range(OFFS):


        def product(tile):
            return jnp.dot(
                scaled_ref[dest_ref[tile]], tiles_ref[tile], preferred_element_type=F32
            )

        def place(tile, offset=offset):
            return offset * blocks + source_ref[tile] % blocks

        copies[offset].wait()
        live_tiles(offset, count_ref, product, place, total_ref)
    for turns, out, store in (
        (1, to_first_ref, stores[1]),
        (2, to_second_ref, stores[2]),
        (0, level_ref, None),
    ):
        for part, offset in enumerate(range(turns, OFFS, TRIO)):
            for block in range(blocks):
                out[part, :, pl.ds(block * BLOCK, BLOCK)] = total_ref[
                    offset * blocks + block
                ].astype(out.dtype)
        if store is not None:
            store.start()
    for store in stores:
        store.wait()


def trio_kernel(place_ref, level_ref, first_ref, second_ref, keep_ref, below_ref, above_ref):
    sums = [level_ref[part] for part in range(TRIO)]
    for steps, ref in enumerate((first_ref, second_ref), 1):
        past = (place_ref[0] < steps).astype(F32)
        lower, upper = ref[0].astype(F32), ref[1].astype(F32)
        sums[0] += lower * (1.0 - past)
        sums[1] += lower * past + upper * (1.0 - past)
        sums[2] += upper * past
    for value, out in zip(sums, (below_ref, keep_ref, above_ref)):
        out[...] = value.astype(out.dtype)


def back_kernel(own_ref, below_ref, above_ref, grad_ref, self_ref, neighbour_ref, keep_ref, send_ref):
    spread = own_ref[...] + below_ref[...].astype(F32) + above_ref[...].astype(F32)
    spread = spread.astype(BF16)
    half = keep_ref.shape[0]
    for at, out in enumerate((keep_ref, send_ref)):
        rows = pl.ds(at * half, half)
        value = jnp.dot(self_ref[rows, :], grad_ref[...], preferred_element_type=F32)
        value = value + jnp.dot(neighbour_ref[rows, :], spread, preferred_element_type=F32)
        out[...] = value.astype(out.dtype)


def chip_kernel(stack_ref, keep_ref, got_ref, *outs):
    for at, out in enumerate(outs):
        piece = (stack_ref[0] + at) % len(outs)
        out[...] = (keep_ref[piece] + got_ref[piece].astype(F32)).astype(out.dtype)


def planes_kernel(got_ref, out_ref):
    for column in range(COLUMN + 1):
        value = got_ref[0, column].astype(F32)
        for plane in range(1, got_ref.shape[0]):
            value = value + got_ref[plane, column].astype(F32)
        value = value.astype(BF16)
        if column < COLUMN:
            out_ref[column, 0] = value
        else:
            for copy in range(COLUMN):
                out_ref[copy, 1] = value


def column_kernel(got_ref, piece_ref, bias_ref):
    for at, out in enumerate((piece_ref, bias_ref)):
        value = got_ref[0, at].astype(F32)
        for column in range(1, COLUMN):
            value = value + got_ref[column, at].astype(F32)
        out[...] = value.astype(out.dtype)


def lay_kernel(feat_ref, pieces_ref, self_ref, neighbour_ref):
    planes, _, rows, _ = pieces_ref.shape
    for plane in range(planes):
        for first in range(0, rows, PIECE):
            kind, row = divmod(plane * rows + first, self_ref.shape[0])
            out = (self_ref, neighbour_ref)[kind]
            for column in range(COLUMN):
                out[pl.ds(row, PIECE), lanes(column ^ feat_ref[0])] = pieces_ref[
                    plane, column, pl.ds(first, PIECE), :
                ].astype(F32)


def call(kernel, in_specs, out_shape, scratch, flops, moved, out_specs=None, limit=VMEM_BYTES):
    return pl.pallas_call(
        kernel,
        in_specs=in_specs,
        out_shape=out_shape,
        out_specs=out_specs or jax.tree.map(lambda _: VMEM, out_shape),
        scratch_shapes=scratch,
        compiler_params=pltpu.CompilerParams(vmem_limit_bytes=limit),
        cost_estimate=pl.CostEstimate(flops=flops, bytes_accessed=moved, transcendentals=0),
    )


def shifted(value, steps):
    count = lax.axis_size("rows")
    pairs = [(source, (source + steps) % count) for source in range(count)]
    return lax.ppermute(value, "rows", pairs)


def turned_in_trio(value, steps):
    count = lax.axis_size("rows")
    pairs = [
        (source, source // TRIO * TRIO + (source + steps) % TRIO) for source in range(count)
    ]
    return lax.ppermute(value, "rows", pairs)


def on_device(
    features,
    tile_values,
    dest_block,
    source_block,
    tile_count,
    degree,
    self_weight,
    neighbour_weight,
    hidden_bias,
    cotangent,
):
    node_dev, width = features.shape
    blocks = node_dev // BLOCK
    groups = lax.axis_size("rows")
    feats = lax.axis_size("feat")
    stacks = feats // CORES
    half = stacks * width
    hidden_dev = hidden_bias.shape[0]
    core = (lax.axis_index("feat") % CORES).reshape(1)
    stack = (lax.axis_index("feat") // CORES).reshape(1)
    place = (lax.axis_index("rows") % TRIO).reshape(1)
    same_core = [[z * CORES + c for z in range(stacks)] for c in range(CORES)]
    other_core = [(f, f ^ 1) for f in range(feats)]
    same_plane = [
        [(p // TRIO * COLUMN + c) * TRIO + p % TRIO for c in range(COLUMN)]
        for p in range(groups // COLUMN)
    ]
    same_column = [list(members) for members in zip(*same_plane)]

    def over_stacks(value):
        return lax.all_to_all(value, "feat", 0, 0, axis_index_groups=same_core)

    def to_stack(value, steps):
        pairs = [(f, (f + steps * CORES) % feats) for f in range(feats)]
        return lax.ppermute(value, "feat", pairs)

    turned = features.T
    below = shifted(turned, TRIO)
    above = shifted(turned, -TRIO)
    pair = jax.ShapeDtypeStruct((2, width, node_dev), BF16)
    first, second = call(
        relay_kernel, [SMEM] + [VMEM] * 3, [pair, pair], [], 0, 8 * turned.size
    )(place, below, turned, above)
    first = turned_in_trio(first, -1)
    second = turned_in_trio(second, -2)
    packed = call(
        pack_kernel,
        [WHOLE] * 3 + [ANY] * 2,
        jax.ShapeDtypeStruct((stacks, 2 * width, node_dev), BF16),
        [],
        0,
        6 * stacks * width * node_dev,
    )(turned, self_weight, neighbour_weight, first, second)
    packed_own = over_stacks(packed)
    packed_far = lax.ppermute(packed_own, "feat", other_core)

    degrees = degree.reshape(1, node_dev)
    scalars = (tile_count, dest_block, source_block)
    tile_flops = 2 * OFFS * SLOTS * BLOCK * BLOCK * BLOCK
    aggregate = call(
        gather_kernel,
        [SMEM] * 3 + [HBM] + [VMEM] * 6,
        jax.ShapeDtypeStruct((stacks, width, node_dev), BF16),
        [
            pltpu.VMEM((blocks + 1, width, BLOCK), F32),
            pltpu.VMEM(tile_values.shape, BF16),
            pltpu.SemaphoreType.DMA((OFFS,)),
        ],
        tile_flops,
        tile_values.size * 2,
        limit=TILES_VMEM_BYTES,
    )(*scalars, tile_values, degrees, below, turned, above, first, second)
    aggregate_own = over_stacks(aggregate)
    aggregate_far = lax.ppermute(aggregate_own, "feat", other_core)

    planes = groups // COLUMN
    rows_each = 4 * half // groups

    pair = jax.ShapeDtypeStruct((2, hidden_dev, node_dev), BF16)

    middle = call(
        middle_kernel,
        [SMEM] * 5 + [HBM] + [VMEM] * 5 + [WHOLE] * 2,
        [
            jax.ShapeDtypeStruct((node_dev, hidden_dev), BF16),
            jax.ShapeDtypeStruct((hidden_dev, node_dev), BF16),
            jax.ShapeDtypeStruct((planes, COLUMN + 1, rows_each, hidden_dev), BF16),
            jax.ShapeDtypeStruct((2 * half, hidden_dev), BF16),
            jax.ShapeDtypeStruct((2 * half, hidden_dev), BF16),
            jax.ShapeDtypeStruct((TRIO, hidden_dev, node_dev), F32),
            pair,
            pair,
        ],
        [
            pltpu.VMEM((2 * half, node_dev), BF16),
            pltpu.VMEM((blocks, hidden_dev, BLOCK), BF16),
            pltpu.VMEM((OFFS * blocks + 1, hidden_dev, BLOCK), F32),
            pltpu.VMEM(tile_values.shape, BF16),
            pltpu.SemaphoreType.DMA((OFFS,)),
            pltpu.VMEM((hidden_dev, node_dev), BF16),
            pltpu.VMEM(pair.shape, BF16),
            pltpu.VMEM(pair.shape, BF16),
            pltpu.SemaphoreType.DMA((3,)),
        ],
        tile_flops * 2,
        tile_values.size * 2,
        [WHOLE, HBM, VMEM, VMEM, VMEM, VMEM, HBM, HBM],
        TILES_VMEM_BYTES,
    )(
        core,
        stack,
        *scalars,
        tile_values,
        degrees,
        packed_own,
        packed_far,
        aggregate_own,
        aggregate_far,
        hidden_bias.reshape(1, hidden_dev),
        cotangent,
    )
    activations, grad_turned, weight_part, weight_self, weight_neighbour = middle[:5]
    to_level, first, second = middle[5:]
    first = turned_in_trio(first, 1)
    second = turned_in_trio(second, 2)

    got = jax.ShapeDtypeStruct((COLUMN, 2, rows_each, hidden_dev), BF16)
    got = call(planes_kernel, [VMEM], got, [], weight_part.size, weight_part.size * 2)(
        lax.all_to_all(weight_part, "rows", 0, 0, axis_index_groups=same_column)
    )
    piece = jax.ShapeDtypeStruct((rows_each, hidden_dev), BF16)
    piece, bias_sum = call(
        column_kernel,
        [VMEM],
        [piece, jax.ShapeDtypeStruct(piece.shape, F32)],
        [],
        got.size,
        got.size * 2,
    )(lax.all_to_all(got, "rows", 0, 0, axis_index_groups=same_plane))
    pairs = [
        (row * feats + feat, row * feats + (feat ^ (row // TRIO % COLUMN)))
        for row in range(groups)
        for feat in range(feats)
    ]
    piece = lax.ppermute(piece, ("rows", "feat"), pairs)
    pieces = lax.all_to_all(
        jnp.broadcast_to(piece[None], (COLUMN,) + piece.shape),
        "rows",
        0,
        0,
        axis_index_groups=same_plane,
    )
    pieces = lax.all_to_all(
        jnp.broadcast_to(pieces[None], (planes,) + pieces.shape),
        "rows",
        0,
        0,
        axis_index_groups=same_column,
    )
    grad_weight = jax.ShapeDtypeStruct((width, feats * hidden_dev), F32)
    grad_self, grad_neighbour = call(
        lay_kernel, [SMEM, VMEM], [grad_weight, grad_weight], [], 0, pieces.size * 6
    )(lax.axis_index("feat").reshape(1), pieces)

    spread = jax.ShapeDtypeStruct((hidden_dev, node_dev), BF16)
    own, to_below, to_above = call(
        trio_kernel,
        [SMEM] + [VMEM] * 3,
        [jax.ShapeDtypeStruct(spread.shape, F32), spread, spread],
        [],
        9 * spread.size,
        20 * spread.size,
    )(place, to_level, first, second)
    from_above = shifted(to_below, -TRIO)
    from_below = shifted(to_above, TRIO)
    keep, send = call(
        back_kernel,
        [VMEM] * 6,
        [
            jax.ShapeDtypeStruct((half, node_dev), F32),
            jax.ShapeDtypeStruct((half, node_dev), BF16),
        ],
        [],
        8 * half * node_dev * hidden_dev,
        4 * half * node_dev,
    )(own, from_below, from_above, grad_turned, weight_self, weight_neighbour)
    got = lax.ppermute(send, "feat", other_core)
    part = jax.ShapeDtypeStruct((width, node_dev), BF16)
    parts = call(
        chip_kernel,
        [SMEM] + [VMEM] * 2,
        [jax.ShapeDtypeStruct(part.shape, F32)] + [part] * (stacks - 1),
        [],
        4 * half * node_dev,
        8 * half * node_dev,
    )(
        stack,
        keep.reshape(stacks, width, node_dev),
        got.reshape(stacks, width, node_dev),
    )
    grad_turned = parts[0]
    for steps in range(1, stacks):
        grad_turned = grad_turned + to_stack(parts[steps], steps).astype(F32)
    return (activations, grad_turned.astype(BF16).T, grad_self, grad_neighbour, bias_sum[0])


def solution(mesh):
    in_specs = (
        P("rows", "feat"),
        P("rows", None, None),
        P("rows"),
        P("rows"),
        P("rows"),
        P("rows"),
        P("feat", None),
        P("feat", None),
        P("feat"),
        P("rows", "feat"),
    )
    out_specs = (P("rows", "feat"), P("rows", "feat"), P("feat", None), P("feat", None), P("feat"))
    return jax.shard_map(
        on_device, mesh=mesh, in_specs=in_specs, out_specs=out_specs, check_vma=False
    )
```

```python
import functools

import jax
import jax.numpy as jnp
from jax import lax
from jax.experimental import pallas as pl
from jax.experimental.pallas import tpu as pltpu
from jax.sharding import PartitionSpec as P

REACH = 3
SLOTS = 16
OFFS = 2 * REACH + 1
BLOCK = 128
GROUP = 4
CORES = 2
TRIO = 3
COLUMN = 8
PIECE = 16
F32 = jnp.float32
BF16 = jnp.bfloat16
VMEM_BYTES = 16 * 1024 * 1024
TILES_VMEM_BYTES = 60_500_000
VMEM = pl.BlockSpec(memory_space=pltpu.VMEM)
SMEM = pl.BlockSpec(memory_space=pltpu.SMEM)
ANY = pl.BlockSpec(memory_space=pl.ANY)
HBM = pl.BlockSpec(memory_space=pltpu.HBM)
WHOLE = pl.BlockSpec()


def lanes(block):
    return pl.ds(pl.multiple_of(block * BLOCK, BLOCK), BLOCK)


def live_tiles(offset, count_ref, product, place_of, total_ref):
    count = count_ref[offset]
    spare = total_ref.shape[0] - 1

    def step(at, carry):
        products = []
        places = []
        for inner in range(GROUP):
            slot = at * GROUP + inner
            tile = offset * SLOTS + slot
            products.append(product(tile))
            places.append(jnp.where(slot < count, place_of(tile), spare))
        for place, value in zip(places, products):
            total_ref[place] += value
        return carry

    lax.fori_loop(0, (count + GROUP - 1) // GROUP, step, 0)


def relay_kernel(place_ref, below_ref, level_ref, above_ref, *outs):
    for steps, out in enumerate(outs, 1):

        @pl.when(place_ref[0] < steps)
        def _(out=out):
            out[0] = level_ref[...]
            out[1] = above_ref[...]

        @pl.when(place_ref[0] >= steps)
        def _(out=out):
            out[0] = below_ref[...]
            out[1] = level_ref[...]


def pack_kernel(self_ref, neighbour_ref, first_ref, second_ref, third_ref, out_ref):
    for stack in range(out_ref.shape[0]):
        for core in range(CORES):
            for kind, ref in enumerate((self_ref, neighbour_ref)):
                out_ref[stack, :, pl.ds((core * 2 + kind) * BLOCK, BLOCK)] = ref[
                    :, pl.ds((stack * CORES + core) * BLOCK, BLOCK)
                ]


def repeat_kernel(value_ref, after_ref, out_ref):
    for copy in range(out_ref.shape[0]):
        out_ref[copy] = value_ref[...]


def tile_copies(tiles_hbm, tiles_ref, copied):
    copies = []
    for offset in range(OFFS):
        part = pl.ds(offset * SLOTS, SLOTS)
        copies.append(
            pltpu.make_async_copy(tiles_hbm.at[part], tiles_ref.at[part], copied.at[offset])
        )
    for copy in copies:
        copy.start()
    return copies


def gather_kernel(
    count_ref,
    dest_ref,
    source_ref,
    tiles_hbm,
    degree_ref,
    below_ref,
    level_ref,
    above_ref,
    first_ref,
    second_ref,
    out_ref,
    total_ref,
    tiles_ref,
    copied,
):
    copies = tile_copies(tiles_hbm, tiles_ref, copied)
    blocks = total_ref.shape[0] - 1
    total_ref[...] = jnp.zeros_like(total_ref)
    straight = (below_ref, level_ref, above_ref)
    for offset in range(OFFS):
        turns, part = offset % TRIO, offset // TRIO
        operand = straight[part] if turns == 0 else (first_ref, second_ref)[turns - 1].at[part]

        def product(tile, operand=operand):
            picked = operand[:, lanes(source_ref[tile] % blocks)]
            return lax.dot_general(
                picked, tiles_ref[tile], (((1,), (1,)), ((), ())), preferred_element_type=F32
            )

        copies[offset].wait()
        live_tiles(offset, count_ref, product, lambda tile: dest_ref[tile], total_ref)
    for block in range(blocks):
        part = pl.ds(block * BLOCK, BLOCK)
        value = (total_ref[block] / degree_ref[:, part].astype(F32)).astype(BF16)
        out_ref[:, part] = value


def middle_kernel(
    core_ref, stack_ref, count_ref, dest_ref, source_ref, tiles_hbm, degree_ref, *refs
):
    packed, inputs, refs = refs[:2], refs[2:6], refs[6:]
    bias_ref, cotangent_ref, refs = *refs[:2], refs[2:]
    act_ref, grad_ref, weight_ref, self_ref, neighbour_ref, refs = *refs[:5], refs[5:]
    level_ref, first_ref, second_ref, *refs = refs
    scaled_ref, total_ref, tiles_ref, copied, *refs = refs
    turned_ref, to_first_ref, to_second_ref, stored = refs
    copies = tile_copies(tiles_hbm, tiles_ref, copied)
    stores = [
        pltpu.make_async_copy(source, target, stored.at[at])
        for at, (source, target) in enumerate(
            ((turned_ref, grad_ref), (to_first_ref, first_ref), (to_second_ref, second_ref))
        )
    ]
    blocks = scaled_ref.shape[0]
    stacks, width, _ = inputs[0].shape
    half = stacks * width
    contract_first = (((0,), (0,)), ((), ()))
    for far, ref in enumerate(packed):
        for stack in range(stacks):
            rows = pl.ds(far * half + stack * width, width)
            for kind, out in enumerate((self_ref, neighbour_ref)):
                out[rows, :] = ref[stack, :, lanes(core_ref[0] * 2 + kind)]
    pre = None
    for at, ref in enumerate(inputs):
        term = lax.dot_general(
            (self_ref, neighbour_ref)[at // CORES][pl.ds(at % CORES * half, half), :],
            ref[...].reshape(half, -1),
            contract_first,
            preferred_element_type=F32,
        )
        pre = term if pre is None else pre + term
    preact = pre.T + bias_ref[...].astype(F32)
    gate_value = jax.nn.sigmoid(preact)
    act_ref[...] = (preact * gate_value).astype(BF16)
    grad = cotangent_ref[...].astype(F32) * gate_value * (1.0 + preact * (1.0 - gate_value))
    grad_pre = grad.astype(BF16)
    grad = grad_pre.astype(F32)
    planes, _, rows, lane = weight_ref.shape
    bias_rows = jnp.broadcast_to(jnp.sum(grad, axis=0, keepdims=True), (rows, lane)).astype(BF16)
    for plane in range(planes):
        weight_ref[plane, COLUMN] = bias_rows
    turned = grad.T
    turned_ref[...] = turned.astype(BF16)
    stores[0].start()
    scaled = (turned / degree_ref[...].astype(F32)).astype(BF16)
    for block in range(blocks):
        scaled_ref[block] = scaled[:, block * BLOCK : (block + 1) * BLOCK]
    for far in range(CORES):
        for kind, ref in enumerate((inputs[far], inputs[CORES + far])):
            operand = ref[...].reshape(half, -1)
            term = jnp.dot(operand, grad_pre, preferred_element_type=F32).astype(BF16)
            for stack in range(stacks):
                column = (stack ^ stack_ref[0]) * CORES + far
                for first in range(0, width, PIECE):
                    plane, row = divmod(kind * width + first, rows)
                    begin = stack * width + first
                    weight_ref[plane, column, pl.ds(row, PIECE), :] = term[begin : begin + PIECE]
    total_ref[...] = jnp.zeros_like(total_ref)
    for offset in range(OFFS):


        def product(tile):
            return jnp.dot(
                scaled_ref[dest_ref[tile]], tiles_ref[tile], preferred_element_type=F32
            )

        def place(tile, offset=offset):
            return offset * blocks + source_ref[tile] % blocks

        copies[offset].wait()
        live_tiles(offset, count_ref, product, place, total_ref)
    for turns, out, store in (
        (1, to_first_ref, stores[1]),
        (2, to_second_ref, stores[2]),
        (0, level_ref, None),
    ):
        for part, offset in enumerate(range(turns, OFFS, TRIO)):
            for block in range(blocks):
                out[part, :, pl.ds(block * BLOCK, BLOCK)] = total_ref[
                    offset * blocks + block
                ].astype(out.dtype)
        if store is not None:
            store.start()
    for store in stores:
        store.wait()


def trio_kernel(place_ref, level_ref, first_ref, second_ref, keep_ref, below_ref, above_ref):
    sums = [level_ref[part] for part in range(TRIO)]
    for steps, ref in enumerate((first_ref, second_ref), 1):
        past = (place_ref[0] < steps).astype(F32)
        lower, upper = ref[0].astype(F32), ref[1].astype(F32)
        sums[0] += lower * (1.0 - past)
        sums[1] += lower * past + upper * (1.0 - past)
        sums[2] += upper * past
    for value, out in zip(sums, (below_ref, keep_ref, above_ref)):
        out[...] = value.astype(out.dtype)


def back_kernel(own_ref, below_ref, above_ref, grad_ref, self_ref, neighbour_ref, keep_ref, send_ref):
    spread = own_ref[...] + below_ref[...].astype(F32) + above_ref[...].astype(F32)
    spread = spread.astype(BF16)
    half = keep_ref.shape[0]
    for at, out in enumerate((keep_ref, send_ref)):
        rows = pl.ds(at * half, half)
        value = jnp.dot(self_ref[rows, :], grad_ref[...], preferred_element_type=F32)
        value = value + jnp.dot(neighbour_ref[rows, :], spread, preferred_element_type=F32)
        out[...] = value.astype(out.dtype)


def chip_kernel(stack_ref, keep_ref, got_ref, *outs):
    for at, out in enumerate(outs):
        piece = (stack_ref[0] + at) % len(outs)
        out[...] = (keep_ref[piece] + got_ref[piece].astype(F32)).astype(out.dtype)


def planes_kernel(got_ref, after_ref, out_ref):
    for column in range(COLUMN + 1):
        value = got_ref[0, column].astype(F32)
        for plane in range(1, got_ref.shape[0]):
            value = value + got_ref[plane, column].astype(F32)
        value = value.astype(BF16)
        if column < COLUMN:
            out_ref[column, 0] = value
        else:
            for copy in range(COLUMN):
                out_ref[copy, 1] = value


def column_kernel(got_ref, piece_ref, bias_ref):
    for at, out in enumerate((piece_ref, bias_ref)):
        value = got_ref[0, at].astype(F32)
        for column in range(1, COLUMN):
            value = value + got_ref[column, at].astype(F32)
        out[...] = value.astype(out.dtype)


def lay_kernel(feat_ref, pieces_ref, self_ref, neighbour_ref):
    planes, _, rows, _ = pieces_ref.shape
    for plane in range(planes):
        for first in range(0, rows, PIECE):
            kind, row = divmod(plane * rows + first, self_ref.shape[0])
            out = (self_ref, neighbour_ref)[kind]
            for column in range(COLUMN):
                out[pl.ds(row, PIECE), lanes(column ^ feat_ref[0])] = pieces_ref[
                    plane, column, pl.ds(first, PIECE), :
                ].astype(F32)


def call(kernel, in_specs, out_shape, scratch, flops, moved, out_specs=None, limit=VMEM_BYTES):
    return pl.pallas_call(
        kernel,
        in_specs=in_specs,
        out_shape=out_shape,
        out_specs=out_specs or jax.tree.map(lambda _: VMEM, out_shape),
        scratch_shapes=scratch,
        compiler_params=pltpu.CompilerParams(vmem_limit_bytes=limit),
        cost_estimate=pl.CostEstimate(flops=flops, bytes_accessed=moved, transcendentals=0),
    )


def shifted(value, steps):
    count = lax.axis_size("rows")
    pairs = [(source, (source + steps) % count) for source in range(count)]
    return lax.ppermute(value, "rows", pairs)


def turned_in_trio(value, steps):
    count = lax.axis_size("rows")
    pairs = [
        (source, source // TRIO * TRIO + (source + steps) % TRIO) for source in range(count)
    ]
    return lax.ppermute(value, "rows", pairs)


def on_device(
    features,
    tile_values,
    dest_block,
    source_block,
    tile_count,
    degree,
    self_weight,
    neighbour_weight,
    hidden_bias,
    cotangent,
):
    node_dev, width = features.shape
    blocks = node_dev // BLOCK
    groups = lax.axis_size("rows")
    feats = lax.axis_size("feat")
    stacks = feats // CORES
    half = stacks * width
    hidden_dev = hidden_bias.shape[0]
    core = (lax.axis_index("feat") % CORES).reshape(1)
    stack = (lax.axis_index("feat") // CORES).reshape(1)
    place = (lax.axis_index("rows") % TRIO).reshape(1)
    same_core = [[z * CORES + c for z in range(stacks)] for c in range(CORES)]
    other_core = [(f, f ^ 1) for f in range(feats)]
    same_plane = [
        [(p // TRIO * COLUMN + c) * TRIO + p % TRIO for c in range(COLUMN)]
        for p in range(groups // COLUMN)
    ]
    same_column = [list(members) for members in zip(*same_plane)]

    def over_stacks(value):
        return lax.all_to_all(value, "feat", 0, 0, axis_index_groups=same_core)

    def to_stack(value, steps):
        pairs = [(f, (f + steps * CORES) % feats) for f in range(feats)]
        return lax.ppermute(value, "feat", pairs)

    def repeated(value, copies, after):
        return call(
            repeat_kernel,
            [VMEM, ANY],
            jax.ShapeDtypeStruct((copies,) + value.shape, value.dtype),
            [],
            0,
            copies * value.size * 2,
        )(value, after)

    turned = features.T
    def whole(value):
        own = over_stacks(value)
        return own, lax.ppermute(own, "feat", other_core)

    features_both = whole(jnp.broadcast_to(turned[None], (stacks,) + turned.shape))
    below = shifted(turned, TRIO)
    above = shifted(turned, -TRIO)
    pair = jax.ShapeDtypeStruct((2, width, node_dev), BF16)
    first, second = call(
        relay_kernel, [SMEM] + [VMEM] * 3, [pair, pair], [], 0, 8 * turned.size
    )(place, below, turned, above)
    first = turned_in_trio(first, -1)
    second = turned_in_trio(second, -2)
    weights_both = whole(
        call(
            pack_kernel,
            [WHOLE] * 2 + [ANY] * 3,
            jax.ShapeDtypeStruct((stacks, width, 2 * CORES * hidden_dev), BF16),
            [],
            0,
            4 * self_weight.size * 2,
        )(self_weight, neighbour_weight, first, second, features_both[0])
    )

    degrees = degree.reshape(1, node_dev)
    scalars = (tile_count, dest_block, source_block)
    tile_flops = 2 * OFFS * SLOTS * BLOCK * BLOCK * BLOCK
    aggregate = call(
        gather_kernel,
        [SMEM] * 3 + [HBM] + [VMEM] * 6,
        jax.ShapeDtypeStruct((width, node_dev), BF16),
        [
            pltpu.VMEM((blocks + 1, width, BLOCK), F32),
            pltpu.VMEM(tile_values.shape, BF16),
            pltpu.SemaphoreType.DMA((OFFS,)),
        ],
        tile_flops,
        tile_values.size * 2,
        limit=TILES_VMEM_BYTES,
    )(*scalars, tile_values, degrees, below, turned, above, first, second)
    aggregate_both = whole(repeated(aggregate, stacks, weights_both[0]))

    planes = groups // COLUMN
    rows_each = 4 * half // groups

    pair = jax.ShapeDtypeStruct((2, hidden_dev, node_dev), BF16)

    middle = call(
        middle_kernel,
        [SMEM] * 5 + [HBM] + [VMEM] * 7 + [WHOLE] * 2,
        [
            jax.ShapeDtypeStruct((node_dev, hidden_dev), BF16),
            jax.ShapeDtypeStruct((hidden_dev, node_dev), BF16),
            jax.ShapeDtypeStruct((planes, COLUMN + 1, rows_each, hidden_dev), BF16),
            jax.ShapeDtypeStruct((2 * half, hidden_dev), BF16),
            jax.ShapeDtypeStruct((2 * half, hidden_dev), BF16),
            jax.ShapeDtypeStruct((TRIO, hidden_dev, node_dev), F32),
            pair,
            pair,
        ],
        [
            pltpu.VMEM((blocks, hidden_dev, BLOCK), BF16),
            pltpu.VMEM((OFFS * blocks + 1, hidden_dev, BLOCK), F32),
            pltpu.VMEM(tile_values.shape, BF16),
            pltpu.SemaphoreType.DMA((OFFS,)),
            pltpu.VMEM((hidden_dev, node_dev), BF16),
            pltpu.VMEM(pair.shape, BF16),
            pltpu.VMEM(pair.shape, BF16),
            pltpu.SemaphoreType.DMA((3,)),
        ],
        tile_flops * 2,
        tile_values.size * 2,
        [WHOLE, HBM, VMEM, VMEM, VMEM, VMEM, HBM, HBM],
        TILES_VMEM_BYTES,
    )(
        core,
        stack,
        *scalars,
        tile_values,
        degrees,
        *weights_both,
        *features_both,
        *aggregate_both,
        hidden_bias.reshape(1, hidden_dev),
        cotangent,
    )
    activations, grad_turned, weight_part, weight_self, weight_neighbour = middle[:5]
    to_level, first, second = middle[5:]
    first = turned_in_trio(first, 1)
    second = turned_in_trio(second, 2)

    spread = jax.ShapeDtypeStruct((hidden_dev, node_dev), BF16)
    own, to_below, to_above = call(
        trio_kernel,
        [SMEM] + [VMEM] * 3,
        [jax.ShapeDtypeStruct(spread.shape, F32), spread, spread],
        [],
        9 * spread.size,
        20 * spread.size,
    )(place, to_level, first, second)
    from_above = shifted(to_below, -TRIO)
    from_below = shifted(to_above, TRIO)
    keep, send = call(
        back_kernel,
        [VMEM] * 6,
        [
            jax.ShapeDtypeStruct((half, node_dev), F32),
            jax.ShapeDtypeStruct((half, node_dev), BF16),
        ],
        [],
        8 * half * node_dev * hidden_dev,
        4 * half * node_dev,
    )(own, from_below, from_above, grad_turned, weight_self, weight_neighbour)
    mid = jax.ShapeDtypeStruct((COLUMN, 2, rows_each, hidden_dev), BF16)
    mid = call(planes_kernel, [VMEM, ANY], mid, [], weight_part.size, weight_part.size * 2)(
        lax.all_to_all(weight_part, "rows", 0, 0, axis_index_groups=same_column),
        keep,
    )
    piece = jax.ShapeDtypeStruct((rows_each, hidden_dev), BF16)
    piece, bias_sum = call(
        column_kernel,
        [VMEM],
        [piece, jax.ShapeDtypeStruct(piece.shape, F32)],
        [],
        mid.size,
        mid.size * 2,
    )(lax.all_to_all(mid, "rows", 0, 0, axis_index_groups=same_plane))
    pairs = [
        (row * feats + feat, row * feats + (feat ^ (row // TRIO % COLUMN)))
        for row in range(groups)
        for feat in range(feats)
    ]
    piece = lax.ppermute(piece, ("rows", "feat"), pairs)
    got = lax.ppermute(send, "feat", other_core)
    part = jax.ShapeDtypeStruct((width, node_dev), BF16)
    parts = call(
        chip_kernel,
        [SMEM] + [VMEM] * 2,
        [jax.ShapeDtypeStruct(part.shape, F32)] + [part] * (stacks - 1),
        [],
        4 * half * node_dev,
        8 * half * node_dev,
    )(
        stack,
        keep.reshape(stacks, width, node_dev),
        got.reshape(stacks, width, node_dev),
    )
    pieces = lax.all_to_all(
        repeated(piece, COLUMN, parts[0]),
        "rows",
        0,
        0,
        axis_index_groups=same_plane,
    )
    pieces = lax.all_to_all(
        jnp.broadcast_to(pieces[None], (planes,) + pieces.shape),
        "rows",
        0,
        0,
        axis_index_groups=same_column,
    )
    grad_weight = jax.ShapeDtypeStruct((width, feats * hidden_dev), F32)
    grad_self, grad_neighbour = call(
        lay_kernel, [SMEM, VMEM], [grad_weight, grad_weight], [], 0, pieces.size * 6
    )(lax.axis_index("feat").reshape(1), pieces)

    grad_turned = parts[0]
    for steps in range(1, stacks):
        grad_turned = grad_turned + to_stack(parts[steps], steps).astype(F32)
    return (activations, grad_turned.astype(BF16).T, grad_self, grad_neighbour, bias_sum[0])


def solution(mesh):
    in_specs = (
        P("rows", "feat"),
        P("rows", None, None),
        P("rows"),
        P("rows"),
        P("rows"),
        P("rows"),
        P("feat", None),
        P("feat", None),
        P("feat"),
        P("rows", "feat"),
    )
    out_specs = (P("rows", "feat"), P("rows", "feat"), P("feat", None), P("feat", None), P("feat"))
    return jax.shard_map(
        on_device, mesh=mesh, in_specs=in_specs, out_specs=out_specs, check_vma=False
    )
```

```python
import functools

import jax
import jax.numpy as jnp
from jax import lax
from jax.experimental import pallas as pl
from jax.experimental.pallas import tpu as pltpu
from jax.sharding import PartitionSpec as P

REACH = 3
SLOTS = 16
OFFS = 2 * REACH + 1
BLOCK = 128
GROUP = 4
CORES = 2
TRIO = 3
COLUMN = 8
PIECE = 16
F32 = jnp.float32
BF16 = jnp.bfloat16
VMEM_BYTES = 16 * 1024 * 1024
TILES_VMEM_BYTES = 60_500_000
VMEM = pl.BlockSpec(memory_space=pltpu.VMEM)
SMEM = pl.BlockSpec(memory_space=pltpu.SMEM)
ANY = pl.BlockSpec(memory_space=pl.ANY)
HBM = pl.BlockSpec(memory_space=pltpu.HBM)
WHOLE = pl.BlockSpec()


def lanes(block):
    return pl.ds(pl.multiple_of(block * BLOCK, BLOCK), BLOCK)


def live_tiles(offset, count_ref, product, place_of, total_ref):
    count = count_ref[offset]
    spare = total_ref.shape[0] - 1

    def step(at, carry):
        products = []
        places = []
        for inner in range(GROUP):
            slot = at * GROUP + inner
            tile = offset * SLOTS + slot
            products.append(product(tile))
            places.append(jnp.where(slot < count, place_of(tile), spare))
        for place, value in zip(places, products):
            total_ref[place] += value
        return carry

    lax.fori_loop(0, (count + GROUP - 1) // GROUP, step, 0)


def relay_kernel(place_ref, below_ref, level_ref, above_ref, *outs):
    for steps, out in enumerate(outs, 1):

        @pl.when(place_ref[0] < steps)
        def _(out=out):
            out[0] = level_ref[...]
            out[1] = above_ref[...]

        @pl.when(place_ref[0] >= steps)
        def _(out=out):
            out[0] = below_ref[...]
            out[1] = level_ref[...]


def row_group(plane, column):
    return (plane // TRIO * COLUMN + column) * TRIO + plane % TRIO


def repeat_kernel(value_ref, after_ref, out_ref):
    for copy in range(out_ref.shape[0]):
        out_ref[copy] = value_ref[...]


def pack_kernel(features_ref, self_ref, neighbour_ref, out_ref):
    width = features_ref.shape[0]
    for stack in range(out_ref.shape[0]):
        out_ref[stack, pl.ds(0, width), :] = features_ref[...]
        for core in range(CORES):
            for kind, ref in enumerate((self_ref, neighbour_ref)):
                out_ref[stack, pl.ds(width, width), pl.ds((core * 2 + kind) * BLOCK, BLOCK)] = ref[
                    :, pl.ds((stack * CORES + core) * BLOCK, BLOCK)
                ]


def tile_copies(tiles_hbm, tiles_ref, copied):
    copies = []
    for offset in range(OFFS):
        part = pl.ds(offset * SLOTS, SLOTS)
        copies.append(
            pltpu.make_async_copy(tiles_hbm.at[part], tiles_ref.at[part], copied.at[offset])
        )
    for copy in copies:
        copy.start()
    return copies


def gather_kernel(
    count_ref,
    dest_ref,
    source_ref,
    tiles_hbm,
    degree_ref,
    below_ref,
    level_ref,
    above_ref,
    first_ref,
    second_ref,
    out_ref,
    total_ref,
    tiles_ref,
    copied,
):
    copies = tile_copies(tiles_hbm, tiles_ref, copied)
    blocks = total_ref.shape[0] - 1
    total_ref[...] = jnp.zeros_like(total_ref)
    straight = (below_ref, level_ref, above_ref)
    for offset in range(OFFS):
        turns, part = offset % TRIO, offset // TRIO
        operand = straight[part] if turns == 0 else (first_ref, second_ref)[turns - 1].at[part]

        def product(tile, operand=operand):
            picked = operand[:, lanes(source_ref[tile] % blocks)]
            return lax.dot_general(
                picked, tiles_ref[tile], (((1,), (1,)), ((), ())), preferred_element_type=F32
            )

        copies[offset].wait()
        live_tiles(offset, count_ref, product, lambda tile: dest_ref[tile], total_ref)
    for block in range(blocks):
        part = pl.ds(block * BLOCK, BLOCK)
        value = (total_ref[block] / degree_ref[:, part].astype(F32)).astype(BF16)
        for copy in range(out_ref.shape[0]):
            out_ref[copy, :, part] = value


def middle_kernel(
    core_ref, stack_ref, count_ref, dest_ref, source_ref, tiles_hbm, degree_ref, *refs
):
    packed, aggregates, refs = refs[:2], refs[2:4], refs[4:]
    bias_ref, cotangent_ref, refs = *refs[:2], refs[2:]
    act_ref, grad_ref, weight_ref, bias_out_ref, self_ref, neighbour_ref, refs = (
        *refs[:6],
        refs[6:],
    )
    level_ref, first_ref, second_ref, *refs = refs
    features_ref, scaled_ref, total_ref, tiles_ref, copied, *refs = refs
    turned_ref, to_first_ref, to_second_ref, stored = refs
    copies = tile_copies(tiles_hbm, tiles_ref, copied)
    stores = [
        pltpu.make_async_copy(source, target, stored.at[at])
        for at, (source, target) in enumerate(
            ((turned_ref, grad_ref), (to_first_ref, first_ref), (to_second_ref, second_ref))
        )
    ]
    blocks = scaled_ref.shape[0]
    stacks, width, _ = aggregates[0].shape
    half = stacks * width
    contract_first = (((0,), (0,)), ((), ()))
    for far, ref in enumerate(packed):
        for stack in range(stacks):
            rows = pl.ds(far * half + stack * width, width)
            features_ref[rows, :] = ref[stack, pl.ds(0, width), :]
            for kind, out in enumerate((self_ref, neighbour_ref)):
                out[rows, :] = ref[stack, pl.ds(width, width), lanes(core_ref[0] * 2 + kind)]
    pre = lax.dot_general(
        self_ref[...], features_ref[...], contract_first, preferred_element_type=F32
    )
    for far, ref in enumerate(aggregates):
        pre = pre + lax.dot_general(
            neighbour_ref[pl.ds(far * half, half), :],
            ref[...].reshape(half, -1),
            contract_first,
            preferred_element_type=F32,
        )
    preact = pre.T + bias_ref[...].astype(F32)
    gate_value = jax.nn.sigmoid(preact)
    act_ref[...] = (preact * gate_value).astype(BF16)
    grad = cotangent_ref[...].astype(F32) * gate_value * (1.0 + preact * (1.0 - gate_value))
    grad_pre = grad.astype(BF16)
    grad = grad_pre.astype(F32)
    bias_out_ref[...] = jnp.broadcast_to(
        jnp.sum(grad, axis=0, keepdims=True), bias_out_ref.shape
    ).astype(bias_out_ref.dtype)
    rows = weight_ref.shape[1]
    turned = grad.T
    turned_ref[...] = turned.astype(BF16)
    stores[0].start()
    scaled = (turned / degree_ref[...].astype(F32)).astype(BF16)
    for block in range(blocks):
        scaled_ref[block] = scaled[:, block * BLOCK : (block + 1) * BLOCK]
    for far in range(CORES):
        operands = (features_ref[pl.ds(far * half, half), :], aggregates[far][...].reshape(half, -1))
        for kind, operand in enumerate(operands):
            term = jnp.dot(operand, grad_pre, preferred_element_type=F32).astype(BF16)
            for stack in range(stacks):
                column = (stack ^ stack_ref[0]) * CORES + far
                for first in range(0, width, PIECE):
                    plane, row = divmod(kind * width + first, rows)
                    begin = stack * width + first
                    weight_ref[row_group(plane, column), pl.ds(row, PIECE), :] = term[
                        begin : begin + PIECE
                    ]
    total_ref[...] = jnp.zeros_like(total_ref)
    for offset in range(OFFS):


        def product(tile):
            return jnp.dot(
                scaled_ref[dest_ref[tile]], tiles_ref[tile], preferred_element_type=F32
            )

        def place(tile, offset=offset):
            return offset * blocks + source_ref[tile] % blocks

        copies[offset].wait()
        live_tiles(offset, count_ref, product, place, total_ref)
    for turns, out, store in (
        (1, to_first_ref, stores[1]),
        (2, to_second_ref, stores[2]),
        (0, level_ref, None),
    ):
        for part, offset in enumerate(range(turns, OFFS, TRIO)):
            for block in range(blocks):
                out[part, :, pl.ds(block * BLOCK, BLOCK)] = total_ref[
                    offset * blocks + block
                ].astype(out.dtype)
        if store is not None:
            store.start()
    for store in stores:
        store.wait()


def trio_kernel(place_ref, level_ref, first_ref, second_ref, keep_ref, below_ref, above_ref):
    sums = [level_ref[part] for part in range(TRIO)]
    for steps, ref in enumerate((first_ref, second_ref), 1):
        past = (place_ref[0] < steps).astype(F32)
        lower, upper = ref[0].astype(F32), ref[1].astype(F32)
        sums[0] += lower * (1.0 - past)
        sums[1] += lower * past + upper * (1.0 - past)
        sums[2] += upper * past
    for value, out in zip(sums, (below_ref, keep_ref, above_ref)):
        out[...] = value.astype(out.dtype)


def back_kernel(own_ref, below_ref, above_ref, grad_ref, self_ref, neighbour_ref, keep_ref, send_ref):
    spread = own_ref[...] + below_ref[...].astype(F32) + above_ref[...].astype(F32)
    spread = spread.astype(BF16)
    half = keep_ref.shape[0]
    for at, out in enumerate((keep_ref, send_ref)):
        rows = pl.ds(at * half, half)
        value = jnp.dot(self_ref[rows, :], grad_ref[...], preferred_element_type=F32)
        value = value + jnp.dot(neighbour_ref[rows, :], spread, preferred_element_type=F32)
        out[...] = value.astype(out.dtype)


def chip_kernel(stack_ref, keep_ref, got_ref, *outs):
    for at, out in enumerate(outs):
        piece = (stack_ref[0] + at) % len(outs)
        out[...] = (keep_ref[piece] + got_ref[piece].astype(F32)).astype(out.dtype)


def lay_kernel(feat_ref, pieces_ref, self_ref, neighbour_ref):
    groups, rows, _ = pieces_ref.shape
    for plane in range(groups // COLUMN):
        for first in range(0, rows, PIECE):
            kind, row = divmod(plane * rows + first, self_ref.shape[0])
            out = (self_ref, neighbour_ref)[kind]
            for column in range(COLUMN):
                out[pl.ds(row, PIECE), lanes(column ^ feat_ref[0])] = pieces_ref[
                    row_group(plane, column), pl.ds(first, PIECE), :
                ].astype(F32)


def call(kernel, in_specs, out_shape, scratch, flops, moved, out_specs=None, limit=VMEM_BYTES):
    return pl.pallas_call(
        kernel,
        in_specs=in_specs,
        out_shape=out_shape,
        out_specs=out_specs or jax.tree.map(lambda _: VMEM, out_shape),
        scratch_shapes=scratch,
        compiler_params=pltpu.CompilerParams(vmem_limit_bytes=limit),
        cost_estimate=pl.CostEstimate(flops=flops, bytes_accessed=moved, transcendentals=0),
    )


def shifted(value, steps):
    count = lax.axis_size("rows")
    pairs = [(source, (source + steps) % count) for source in range(count)]
    return lax.ppermute(value, "rows", pairs)


def turned_in_trio(value, steps):
    count = lax.axis_size("rows")
    pairs = [
        (source, source // TRIO * TRIO + (source + steps) % TRIO) for source in range(count)
    ]
    return lax.ppermute(value, "rows", pairs)


def on_device(
    features,
    tile_values,
    dest_block,
    source_block,
    tile_count,
    degree,
    self_weight,
    neighbour_weight,
    hidden_bias,
    cotangent,
):
    node_dev, width = features.shape
    blocks = node_dev // BLOCK
    groups = lax.axis_size("rows")
    feats = lax.axis_size("feat")
    stacks = feats // CORES
    half = stacks * width
    hidden_dev = hidden_bias.shape[0]
    core = (lax.axis_index("feat") % CORES).reshape(1)
    stack = (lax.axis_index("feat") // CORES).reshape(1)
    place = (lax.axis_index("rows") % TRIO).reshape(1)
    same_core = [[z * CORES + c for z in range(stacks)] for c in range(CORES)]
    other_core = [(f, f ^ 1) for f in range(feats)]

    def over_stacks(value):
        return lax.all_to_all(value, "feat", 0, 0, axis_index_groups=same_core)

    def to_stack(value, steps):
        pairs = [(f, (f + steps * CORES) % feats) for f in range(feats)]
        return lax.ppermute(value, "feat", pairs)

    turned = features.T
    below = shifted(turned, TRIO)
    above = shifted(turned, -TRIO)
    pair = jax.ShapeDtypeStruct((2, width, node_dev), BF16)
    first, second = call(
        relay_kernel, [SMEM] + [VMEM] * 3, [pair, pair], [], 0, 8 * turned.size
    )(place, below, turned, above)
    first = turned_in_trio(first, -1)
    second = turned_in_trio(second, -2)
    packed = call(
        pack_kernel,
        [WHOLE] * 3,
        jax.ShapeDtypeStruct((stacks, 2 * width, node_dev), BF16),
        [],
        0,
        6 * stacks * width * node_dev,
    )(turned, self_weight, neighbour_weight)
    packed_own = over_stacks(packed)
    packed_far = lax.ppermute(packed_own, "feat", other_core)

    degrees = degree.reshape(1, node_dev)
    scalars = (tile_count, dest_block, source_block)
    tile_flops = 2 * OFFS * SLOTS * BLOCK * BLOCK * BLOCK
    aggregate = call(
        gather_kernel,
        [SMEM] * 3 + [HBM] + [VMEM] * 6,
        jax.ShapeDtypeStruct((stacks, width, node_dev), BF16),
        [
            pltpu.VMEM((blocks + 1, width, BLOCK), F32),
            pltpu.VMEM(tile_values.shape, BF16),
            pltpu.SemaphoreType.DMA((OFFS,)),
        ],
        tile_flops,
        tile_values.size * 2,
        limit=TILES_VMEM_BYTES,
    )(*scalars, tile_values, degrees, below, turned, above, first, second)
    aggregate_own = over_stacks(aggregate)
    aggregate_far = lax.ppermute(aggregate_own, "feat", other_core)

    rows_each = 4 * half // groups

    pair = jax.ShapeDtypeStruct((2, hidden_dev, node_dev), BF16)

    middle = call(
        middle_kernel,
        [SMEM] * 5 + [HBM] + [VMEM] * 5 + [WHOLE] * 2,
        [
            jax.ShapeDtypeStruct((node_dev, hidden_dev), BF16),
            jax.ShapeDtypeStruct((hidden_dev, node_dev), BF16),
            jax.ShapeDtypeStruct((groups, rows_each, hidden_dev), BF16),
            jax.ShapeDtypeStruct((8, hidden_dev), F32),
            jax.ShapeDtypeStruct((2 * half, hidden_dev), BF16),
            jax.ShapeDtypeStruct((2 * half, hidden_dev), BF16),
            jax.ShapeDtypeStruct((TRIO, hidden_dev, node_dev), F32),
            pair,
            pair,
        ],
        [
            pltpu.VMEM((2 * half, node_dev), BF16),
            pltpu.VMEM((blocks, hidden_dev, BLOCK), BF16),
            pltpu.VMEM((OFFS * blocks + 1, hidden_dev, BLOCK), F32),
            pltpu.VMEM(tile_values.shape, BF16),
            pltpu.SemaphoreType.DMA((OFFS,)),
            pltpu.VMEM((hidden_dev, node_dev), BF16),
            pltpu.VMEM(pair.shape, BF16),
            pltpu.VMEM(pair.shape, BF16),
            pltpu.SemaphoreType.DMA((3,)),
        ],
        tile_flops * 2,
        tile_values.size * 2,
        [WHOLE, HBM, VMEM, VMEM, VMEM, VMEM, VMEM, HBM, HBM],
        TILES_VMEM_BYTES,
    )(
        core,
        stack,
        *scalars,
        tile_values,
        degrees,
        packed_own,
        packed_far,
        aggregate_own,
        aggregate_far,
        hidden_bias.reshape(1, hidden_dev),
        cotangent,
    )
    activations, grad_turned, weight_part, bias_part, weight_self, weight_neighbour = middle[:6]
    to_level, first, second = middle[6:]
    first = turned_in_trio(first, 1)
    second = turned_in_trio(second, 2)

    bias_rows = jnp.broadcast_to(bias_part.astype(BF16)[None], (groups,) + bias_part.shape)
    sent = jnp.concatenate([weight_part, bias_rows], axis=1)
    summed = jnp.sum(lax.all_to_all(sent, "rows", 0, 0).astype(F32), axis=0)
    pairs = [
        (row * feats + feat, row * feats + (feat ^ (row // TRIO % COLUMN)))
        for row in range(groups)
        for feat in range(feats)
    ]
    piece = lax.ppermute(summed[:rows_each].astype(BF16), ("rows", "feat"), pairs)

    spread = jax.ShapeDtypeStruct((hidden_dev, node_dev), BF16)
    own, to_below, to_above = call(
        trio_kernel,
        [SMEM] + [VMEM] * 3,
        [jax.ShapeDtypeStruct(spread.shape, F32), spread, spread],
        [],
        9 * spread.size,
        20 * spread.size,
    )(place, to_level, first, second)
    from_above = shifted(to_below, -TRIO)
    from_below = shifted(to_above, TRIO)
    keep, send = call(
        back_kernel,
        [VMEM] * 6,
        [
            jax.ShapeDtypeStruct((half, node_dev), F32),
            jax.ShapeDtypeStruct((half, node_dev), BF16),
        ],
        [],
        8 * half * node_dev * hidden_dev,
        4 * half * node_dev,
    )(own, from_below, from_above, grad_turned, weight_self, weight_neighbour)
    got = lax.ppermute(send, "feat", other_core)
    part = jax.ShapeDtypeStruct((width, node_dev), BF16)
    parts = call(
        chip_kernel,
        [SMEM] + [VMEM] * 2,
        [jax.ShapeDtypeStruct(part.shape, F32)] + [part] * (stacks - 1),
        [],
        4 * half * node_dev,
        8 * half * node_dev,
    )(
        stack,
        keep.reshape(stacks, width, node_dev),
        got.reshape(stacks, width, node_dev),
    )
    pieces = call(
        repeat_kernel,
        [VMEM, ANY],
        jax.ShapeDtypeStruct((groups,) + piece.shape, BF16),
        [],
        0,
        groups * piece.size * 2,
    )(piece, parts[0])
    pieces = lax.all_to_all(pieces, "rows", 0, 0)
    grad_weight = jax.ShapeDtypeStruct((width, feats * hidden_dev), F32)
    grad_self, grad_neighbour = call(
        lay_kernel, [SMEM, VMEM], [grad_weight, grad_weight], [], 0, pieces.size * 6
    )(lax.axis_index("feat").reshape(1), pieces)
    grad_turned = parts[0]
    for steps in range(1, stacks):
        grad_turned = grad_turned + to_stack(parts[steps], steps).astype(F32)
    return (activations, grad_turned.astype(BF16).T, grad_self, grad_neighbour, summed[rows_each])


def solution(mesh):
    in_specs = (
        P("rows", "feat"),
        P("rows", None, None),
        P("rows"),
        P("rows"),
        P("rows"),
        P("rows"),
        P("feat", None),
        P("feat", None),
        P("feat"),
        P("rows", "feat"),
    )
    out_specs = (P("rows", "feat"), P("rows", "feat"), P("feat", None), P("feat", None), P("feat"))
    return jax.shard_map(
        on_device, mesh=mesh, in_specs=in_specs, out_specs=out_specs, check_vma=False
    )
```

```python
import functools

import jax
import jax.numpy as jnp
from jax import lax
from jax.experimental import pallas as pl
from jax.experimental.pallas import tpu as pltpu
from jax.sharding import PartitionSpec as P

REACH = 3
SLOTS = 16
OFFS = 2 * REACH + 1
BLOCK = 128
GROUP = 4
CORES = 2
TRIO = 3
COLUMN = 8
PIECE = 16
F32 = jnp.float32
BF16 = jnp.bfloat16
VMEM_BYTES = 16 * 1024 * 1024
TILES_VMEM_BYTES = 60_500_000
VMEM = pl.BlockSpec(memory_space=pltpu.VMEM)
SMEM = pl.BlockSpec(memory_space=pltpu.SMEM)
ANY = pl.BlockSpec(memory_space=pl.ANY)
HBM = pl.BlockSpec(memory_space=pltpu.HBM)
WHOLE = pl.BlockSpec()


def lanes(block):
    return pl.ds(pl.multiple_of(block * BLOCK, BLOCK), BLOCK)


def live_tiles(offset, count_ref, product, place_of, total_ref):
    count = count_ref[offset]
    spare = total_ref.shape[0] - 1

    def step(at, carry):
        products = []
        places = []
        for inner in range(GROUP):
            slot = at * GROUP + inner
            tile = offset * SLOTS + slot
            products.append(product(tile))
            places.append(jnp.where(slot < count, place_of(tile), spare))
        for place, value in zip(places, products):
            total_ref[place] += value
        return carry

    lax.fori_loop(0, (count + GROUP - 1) // GROUP, step, 0)


def band_slot(place_ref, offset):
    return (place_ref[0] + offset) // TRIO * TRIO + offset % TRIO


def pack_kernel(features_ref, first_ref, second_ref, self_ref, neighbour_ref, level_ref, out_ref):
    width = features_ref.shape[0]
    for slot, ref in enumerate((features_ref, first_ref, second_ref)):
        level_ref[slot] = ref[...]
    for stack in range(out_ref.shape[0]):
        out_ref[stack, pl.ds(0, width), :] = features_ref[...]
        for core in range(CORES):
            for kind, ref in enumerate((self_ref, neighbour_ref)):
                out_ref[stack, pl.ds(width, width), pl.ds((core * 2 + kind) * BLOCK, BLOCK)] = ref[
                    :, pl.ds((stack * CORES + core) * BLOCK, BLOCK)
                ]


def tile_copies(tiles_hbm, tiles_ref, copied):
    copies = []
    for offset in range(OFFS):
        part = pl.ds(offset * SLOTS, SLOTS)
        copies.append(
            pltpu.make_async_copy(tiles_hbm.at[part], tiles_ref.at[part], copied.at[offset])
        )
    for copy in copies:
        copy.start()
    return copies


def gather_kernel(
    place_ref,
    count_ref,
    dest_ref,
    source_ref,
    tiles_hbm,
    degree_ref,
    below_ref,
    level_ref,
    above_ref,
    out_ref,
    total_ref,
    band_ref,
    tiles_ref,
    copied,
):
    copies = tile_copies(tiles_hbm, tiles_ref, copied)
    blocks = total_ref.shape[0] - 1
    total_ref[...] = jnp.zeros_like(total_ref)
    for trio, ref in enumerate((below_ref, level_ref, above_ref)):
        band_ref[pl.ds(trio * TRIO, TRIO)] = ref[...]
    for offset in range(OFFS):
        slot = band_slot(place_ref, offset)

        def product(tile, slot=slot):
            picked = band_ref[slot, :, lanes(source_ref[tile] % blocks)]
            return lax.dot_general(
                picked, tiles_ref[tile], (((1,), (1,)), ((), ())), preferred_element_type=F32
            )

        copies[offset].wait()
        live_tiles(offset, count_ref, product, lambda tile: dest_ref[tile], total_ref)
    for block in range(blocks):
        part = pl.ds(block * BLOCK, BLOCK)
        value = (total_ref[block] / degree_ref[:, part].astype(F32)).astype(BF16)
        for copy in range(out_ref.shape[0]):
            out_ref[copy, :, part] = value


def middle_kernel(
    place_ref, core_ref, stack_ref, count_ref, dest_ref, source_ref, tiles_hbm, degree_ref, *refs
):
    packed, aggregates, refs = refs[:2], refs[2:4], refs[4:]
    bias_ref, cotangent_ref, refs = *refs[:2], refs[2:]
    act_ref, grad_ref, weight_ref, self_ref, neighbour_ref, refs = *refs[:5], refs[5:]
    level_ref, below_ref, above_ref, *refs = refs
    features_ref, scaled_ref, total_ref, tiles_ref, copied, *refs = refs
    turned_ref, to_below_ref, to_above_ref, stored = refs
    copies = tile_copies(tiles_hbm, tiles_ref, copied)
    stores = [
        pltpu.make_async_copy(source, target, stored.at[at])
        for at, (source, target) in enumerate(
            ((turned_ref, grad_ref), (to_below_ref, below_ref), (to_above_ref, above_ref))
        )
    ]
    blocks = scaled_ref.shape[0]
    stacks, width, _ = aggregates[0].shape
    half = stacks * width
    contract_first = (((0,), (0,)), ((), ()))
    for far, ref in enumerate(packed):
        for stack in range(stacks):
            rows = pl.ds(far * half + stack * width, width)
            features_ref[rows, :] = ref[stack, pl.ds(0, width), :]
            for kind, out in enumerate((self_ref, neighbour_ref)):
                out[rows, :] = ref[stack, pl.ds(width, width), lanes(core_ref[0] * 2 + kind)]
    pre = lax.dot_general(
        self_ref[...], features_ref[...], contract_first, preferred_element_type=F32
    )
    for far, ref in enumerate(aggregates):
        pre = pre + lax.dot_general(
            neighbour_ref[pl.ds(far * half, half), :],
            ref[...].reshape(half, -1),
            contract_first,
            preferred_element_type=F32,
        )
    preact = pre.T + bias_ref[...].astype(F32)
    gate_value = jax.nn.sigmoid(preact)
    act_ref[...] = (preact * gate_value).astype(BF16)
    grad = cotangent_ref[...].astype(F32) * gate_value * (1.0 + preact * (1.0 - gate_value))
    grad_pre = grad.astype(BF16)
    grad = grad_pre.astype(F32)
    planes, _, rows, lane = weight_ref.shape
    bias_rows = jnp.broadcast_to(jnp.sum(grad, axis=0, keepdims=True), (rows, lane)).astype(BF16)
    for plane in range(planes):
        weight_ref[plane, COLUMN] = bias_rows
    turned = grad.T
    turned_ref[...] = turned.astype(BF16)
    stores[0].start()
    scaled = (turned / degree_ref[...].astype(F32)).astype(BF16)
    for block in range(blocks):
        scaled_ref[block] = scaled[:, block * BLOCK : (block + 1) * BLOCK]
    for far in range(CORES):
        operands = (features_ref[pl.ds(far * half, half), :], aggregates[far][...].reshape(half, -1))
        for kind, operand in enumerate(operands):
            term = jnp.dot(operand, grad_pre, preferred_element_type=F32).astype(BF16)
            for stack in range(stacks):
                column = (stack ^ stack_ref[0]) * CORES + far
                for first in range(0, width, PIECE):
                    plane, row = divmod(kind * width + first, rows)
                    begin = stack * width + first
                    weight_ref[plane, column, pl.ds(row, PIECE), :] = term[begin : begin + PIECE]
    total_ref[...] = jnp.zeros_like(total_ref)
    for offset in range(OFFS):
        slot = band_slot(place_ref, offset)

        def product(tile):
            return jnp.dot(
                scaled_ref[dest_ref[tile]], tiles_ref[tile], preferred_element_type=F32
            )

        def place(tile, slot=slot):
            return slot * blocks + source_ref[tile] % blocks

        copies[offset].wait()
        live_tiles(offset, count_ref, product, place, total_ref)
    for trio, out, store in (
        (0, to_below_ref, stores[1]),
        (2, to_above_ref, stores[2]),
        (1, level_ref, None),
    ):
        for slot in range(TRIO):
            for block in range(blocks):
                out[slot, :, pl.ds(block * BLOCK, BLOCK)] = total_ref[
                    (trio * TRIO + slot) * blocks + block
                ].astype(out.dtype)
        if store is not None:
            store.start()
    for store in stores:
        store.wait()


def trio_kernel(level_ref, below_ref, above_ref, *outs):
    for slot, out in enumerate(outs):
        value = level_ref[slot] + below_ref[slot].astype(F32) + above_ref[slot].astype(F32)
        out[...] = value.astype(out.dtype)


def back_kernel(own_ref, first_ref, second_ref, grad_ref, self_ref, neighbour_ref, keep_ref, send_ref):
    spread = own_ref[...] + first_ref[...].astype(F32) + second_ref[...].astype(F32)
    spread = spread.astype(BF16)
    half = keep_ref.shape[0]
    for at, out in enumerate((keep_ref, send_ref)):
        rows = pl.ds(at * half, half)
        value = jnp.dot(self_ref[rows, :], grad_ref[...], preferred_element_type=F32)
        value = value + jnp.dot(neighbour_ref[rows, :], spread, preferred_element_type=F32)
        out[...] = value.astype(out.dtype)


def chip_kernel(keep_ref, got_ref, out_ref):
    out_ref[...] = (keep_ref[...] + got_ref[...].astype(F32)).astype(BF16)


def planes_kernel(got_ref, out_ref):
    for column in range(COLUMN + 1):
        value = got_ref[0, column].astype(F32)
        for plane in range(1, got_ref.shape[0]):
            value = value + got_ref[plane, column].astype(F32)
        value = value.astype(BF16)
        if column < COLUMN:
            out_ref[column, 0] = value
        else:
            for copy in range(COLUMN):
                out_ref[copy, 1] = value


def column_kernel(got_ref, piece_ref, bias_ref):
    for at, out in enumerate((piece_ref, bias_ref)):
        value = got_ref[0, at].astype(F32)
        for column in range(1, COLUMN):
            value = value + got_ref[column, at].astype(F32)
        out[...] = value.astype(out.dtype)


def lay_kernel(feat_ref, pieces_ref, self_ref, neighbour_ref):
    planes, _, rows, _ = pieces_ref.shape
    for plane in range(planes):
        for first in range(0, rows, PIECE):
            kind, row = divmod(plane * rows + first, self_ref.shape[0])
            out = (self_ref, neighbour_ref)[kind]
            for column in range(COLUMN):
                out[pl.ds(row, PIECE), lanes(column ^ feat_ref[0])] = pieces_ref[
                    plane, column, pl.ds(first, PIECE), :
                ].astype(F32)


def call(kernel, in_specs, out_shape, scratch, flops, moved, out_specs=None, limit=VMEM_BYTES):
    return pl.pallas_call(
        kernel,
        in_specs=in_specs,
        out_shape=out_shape,
        out_specs=out_specs or jax.tree.map(lambda _: VMEM, out_shape),
        scratch_shapes=scratch,
        compiler_params=pltpu.CompilerParams(vmem_limit_bytes=limit),
        cost_estimate=pl.CostEstimate(flops=flops, bytes_accessed=moved, transcendentals=0),
    )


def shifted(value, steps):
    count = lax.axis_size("rows")
    pairs = [(source, (source + steps) % count) for source in range(count)]
    return lax.ppermute(value, "rows", pairs)


def turned_in_trio(value, steps):
    count = lax.axis_size("rows")
    pairs = [
        (source, source // TRIO * TRIO + (source + steps) % TRIO) for source in range(count)
    ]
    return lax.ppermute(value, "rows", pairs)


def on_device(
    features,
    tile_values,
    dest_block,
    source_block,
    tile_count,
    degree,
    self_weight,
    neighbour_weight,
    hidden_bias,
    cotangent,
):
    node_dev, width = features.shape
    blocks = node_dev // BLOCK
    groups = lax.axis_size("rows")
    feats = lax.axis_size("feat")
    stacks = feats // CORES
    half = stacks * width
    hidden_dev = hidden_bias.shape[0]
    core = (lax.axis_index("feat") % CORES).reshape(1)
    stack = (lax.axis_index("feat") // CORES).reshape(1)
    place = (lax.axis_index("rows") % TRIO).reshape(1)
    same_core = [[z * CORES + c for z in range(stacks)] for c in range(CORES)]
    other_core = [(f, f ^ 1) for f in range(feats)]
    same_plane = [
        [(p // TRIO * COLUMN + c) * TRIO + p % TRIO for c in range(COLUMN)]
        for p in range(groups // COLUMN)
    ]
    same_column = [list(members) for members in zip(*same_plane)]

    def over_stacks(value):
        return lax.all_to_all(value, "feat", 0, 0, axis_index_groups=same_core)

    turned = features.T
    level, packed = call(
        pack_kernel,
        [WHOLE] * 5,
        [
            jax.ShapeDtypeStruct((TRIO, width, node_dev), BF16),
            jax.ShapeDtypeStruct((stacks, 2 * width, node_dev), BF16),
        ],
        [],
        0,
        6 * stacks * width * node_dev,
        limit=TILES_VMEM_BYTES,
    )(
        turned,
        turned_in_trio(turned, -1),
        turned_in_trio(turned, -2),
        self_weight,
        neighbour_weight,
    )
    below = shifted(level, TRIO)
    above = shifted(level, -TRIO)
    packed_own = over_stacks(packed)
    packed_far = lax.ppermute(packed_own, "feat", other_core)

    degrees = degree.reshape(1, node_dev)
    scalars = (tile_count, dest_block, source_block)
    tile_flops = 2 * OFFS * SLOTS * BLOCK * BLOCK * BLOCK
    aggregate = call(
        gather_kernel,
        [SMEM] * 4 + [HBM] + [VMEM] * 4,
        jax.ShapeDtypeStruct((stacks, width, node_dev), BF16),
        [
            pltpu.VMEM((blocks + 1, width, BLOCK), F32),
            pltpu.VMEM((TRIO * TRIO, width, node_dev), BF16),
            pltpu.VMEM(tile_values.shape, BF16),
            pltpu.SemaphoreType.DMA((OFFS,)),
        ],
        tile_flops,
        tile_values.size * 2,
        limit=TILES_VMEM_BYTES,
    )(place, *scalars, tile_values, degrees, below, level, above)
    aggregate_own = over_stacks(aggregate)
    aggregate_far = lax.ppermute(aggregate_own, "feat", other_core)

    planes = groups // COLUMN
    rows_each = 4 * half // groups

    def trio(dtype):
        return jax.ShapeDtypeStruct((TRIO, hidden_dev, node_dev), dtype)

    middle = call(
        middle_kernel,
        [SMEM] * 6 + [HBM] + [VMEM] * 5 + [WHOLE] * 2,
        [
            jax.ShapeDtypeStruct((node_dev, hidden_dev), BF16),
            jax.ShapeDtypeStruct((hidden_dev, node_dev), BF16),
            jax.ShapeDtypeStruct((planes, COLUMN + 1, rows_each, hidden_dev), BF16),
            jax.ShapeDtypeStruct((2 * half, hidden_dev), BF16),
            jax.ShapeDtypeStruct((2 * half, hidden_dev), BF16),
            trio(F32),
            trio(BF16),
            trio(BF16),
        ],
        [
            pltpu.VMEM((2 * half, node_dev), BF16),
            pltpu.VMEM((blocks, hidden_dev, BLOCK), BF16),
            pltpu.VMEM((TRIO * TRIO * blocks + 1, hidden_dev, BLOCK), F32),
            pltpu.VMEM(tile_values.shape, BF16),
            pltpu.SemaphoreType.DMA((OFFS,)),
            pltpu.VMEM((hidden_dev, node_dev), BF16),
            pltpu.VMEM((TRIO, hidden_dev, node_dev), BF16),
            pltpu.VMEM((TRIO, hidden_dev, node_dev), BF16),
            pltpu.SemaphoreType.DMA((3,)),
        ],
        tile_flops * 2,
        tile_values.size * 2,
        [WHOLE, HBM, VMEM, VMEM, VMEM, VMEM, HBM, HBM],
        TILES_VMEM_BYTES,
    )(
        place,
        core,
        stack,
        *scalars,
        tile_values,
        degrees,
        packed_own,
        packed_far,
        aggregate_own,
        aggregate_far,
        hidden_bias.reshape(1, hidden_dev),
        cotangent,
    )
    activations, grad_turned, weight_part, weight_self, weight_neighbour = middle[:5]
    to_level, to_below, to_above = middle[5:]
    from_above = shifted(to_below, -TRIO)
    from_below = shifted(to_above, TRIO)

    got = jax.ShapeDtypeStruct((COLUMN, 2, rows_each, hidden_dev), BF16)
    got = call(planes_kernel, [VMEM], got, [], weight_part.size, weight_part.size * 2)(
        lax.all_to_all(weight_part, "rows", 0, 0, axis_index_groups=same_column)
    )
    piece = jax.ShapeDtypeStruct((rows_each, hidden_dev), BF16)
    piece, bias_sum = call(
        column_kernel,
        [VMEM],
        [piece, jax.ShapeDtypeStruct(piece.shape, F32)],
        [],
        got.size,
        got.size * 2,
    )(lax.all_to_all(got, "rows", 0, 0, axis_index_groups=same_plane))
    pairs = [
        (row * feats + feat, row * feats + (feat ^ (row // TRIO % COLUMN)))
        for row in range(groups)
        for feat in range(feats)
    ]
    piece = lax.ppermute(piece, ("rows", "feat"), pairs)
    pieces = lax.all_to_all(
        jnp.broadcast_to(piece[None], (COLUMN,) + piece.shape),
        "rows",
        0,
        0,
        axis_index_groups=same_plane,
    )
    pieces = lax.all_to_all(
        jnp.broadcast_to(pieces[None], (planes,) + pieces.shape),
        "rows",
        0,
        0,
        axis_index_groups=same_column,
    )
    grad_weight = jax.ShapeDtypeStruct((width, feats * hidden_dev), F32)
    grad_self, grad_neighbour = call(
        lay_kernel, [SMEM, VMEM], [grad_weight, grad_weight], [], 0, pieces.size * 6
    )(lax.axis_index("feat").reshape(1), pieces)

    spread = jax.ShapeDtypeStruct((hidden_dev, node_dev), BF16)
    own, first, second = call(
        trio_kernel,
        [VMEM] * 3,
        [jax.ShapeDtypeStruct(spread.shape, F32), spread, spread],
        [],
        9 * spread.size,
        20 * spread.size,
    )(to_level, from_below, from_above)
    first = turned_in_trio(first, 1)
    second = turned_in_trio(second, 2)
    keep, send = call(
        back_kernel,
        [VMEM] * 6,
        [
            jax.ShapeDtypeStruct((half, node_dev), F32),
            jax.ShapeDtypeStruct((half, node_dev), BF16),
        ],
        [],
        8 * half * node_dev * hidden_dev,
        4 * half * node_dev,
    )(own, first, second, grad_turned, weight_self, weight_neighbour)
    got = lax.ppermute(send, "feat", other_core)
    chip_sum = call(
        chip_kernel,
        [VMEM] * 2,
        jax.ShapeDtypeStruct((half, node_dev), BF16),
        [],
        half * node_dev,
        8 * half * node_dev,
    )(keep, got)
    shares = over_stacks(chip_sum.reshape(stacks, width, node_dev))
    grad_turned = jnp.sum(shares.astype(F32), axis=0)
    return (activations, grad_turned.astype(BF16).T, grad_self, grad_neighbour, bias_sum[0])


def solution(mesh):
    in_specs = (
        P("rows", "feat"),
        P("rows", None, None),
        P("rows"),
        P("rows"),
        P("rows"),
        P("rows"),
        P("feat", None),
        P("feat", None),
        P("feat"),
        P("rows", "feat"),
    )
    out_specs = (P("rows", "feat"), P("rows", "feat"), P("feat", None), P("feat", None), P("feat"))
    return jax.shard_map(
        on_device, mesh=mesh, in_specs=in_specs, out_specs=out_specs, check_vma=False
    )
```

```python
import functools

import jax
import jax.numpy as jnp
from jax import lax
from jax.experimental import pallas as pl
from jax.experimental.pallas import tpu as pltpu
from jax.sharding import PartitionSpec as P

REACH = 3
SLOTS = 16
OFFS = 2 * REACH + 1
BLOCK = 128
GROUP = 4
CORES = 2
TRIO = 3
COLUMN = 8
PIECE = 16
F32 = jnp.float32
BF16 = jnp.bfloat16
VMEM_BYTES = 16 * 1024 * 1024
TILES_VMEM_BYTES = 60_500_000
VMEM = pl.BlockSpec(memory_space=pltpu.VMEM)
SMEM = pl.BlockSpec(memory_space=pltpu.SMEM)
ANY = pl.BlockSpec(memory_space=pl.ANY)
HBM = pl.BlockSpec(memory_space=pltpu.HBM)
WHOLE = pl.BlockSpec()


def lanes(block):
    return pl.ds(pl.multiple_of(block * BLOCK, BLOCK), BLOCK)


def live_tiles(offset, count_ref, product, place_of, total_ref):
    count = count_ref[offset]
    spare = total_ref.shape[0] - 1

    def step(at, carry):
        products = []
        places = []
        for inner in range(GROUP):
            slot = at * GROUP + inner
            tile = offset * SLOTS + slot
            products.append(product(tile))
            places.append(jnp.where(slot < count, place_of(tile), spare))
        for place, value in zip(places, products):
            total_ref[place] += value
        return carry

    lax.fori_loop(0, (count + GROUP - 1) // GROUP, step, 0)


def band_slot(place_ref, offset):
    return (place_ref[0] + offset) // TRIO * TRIO + offset % TRIO


def pack_kernel(features_ref, first_ref, second_ref, self_ref, neighbour_ref, level_ref, out_ref):
    width = features_ref.shape[0]
    for slot, ref in enumerate((features_ref, first_ref, second_ref)):
        level_ref[slot] = ref[...]
    for stack in range(out_ref.shape[0]):
        out_ref[stack, pl.ds(0, width), :] = features_ref[...]
        for core in range(CORES):
            for kind, ref in enumerate((self_ref, neighbour_ref)):
                out_ref[stack, pl.ds(width, width), pl.ds((core * 2 + kind) * BLOCK, BLOCK)] = ref[
                    :, pl.ds((stack * CORES + core) * BLOCK, BLOCK)
                ]


def tile_copies(tiles_hbm, tiles_ref, copied):
    copies = []
    for offset in range(OFFS):
        part = pl.ds(offset * SLOTS, SLOTS)
        copies.append(
            pltpu.make_async_copy(tiles_hbm.at[part], tiles_ref.at[part], copied.at[offset])
        )
    for copy in copies:
        copy.start()
    return copies


def gather_kernel(
    place_ref,
    count_ref,
    dest_ref,
    source_ref,
    tiles_hbm,
    degree_ref,
    below_ref,
    level_ref,
    above_ref,
    out_ref,
    total_ref,
    band_ref,
    tiles_ref,
    copied,
):
    copies = tile_copies(tiles_hbm, tiles_ref, copied)
    blocks = total_ref.shape[0] - 1
    total_ref[...] = jnp.zeros_like(total_ref)
    for trio, ref in enumerate((below_ref, level_ref, above_ref)):
        band_ref[pl.ds(trio * TRIO, TRIO)] = ref[...]
    for offset in range(OFFS):
        slot = band_slot(place_ref, offset)

        def product(tile, slot=slot):
            picked = band_ref[slot, :, lanes(source_ref[tile] % blocks)]
            return lax.dot_general(
                picked, tiles_ref[tile], (((1,), (1,)), ((), ())), preferred_element_type=F32
            )

        copies[offset].wait()
        live_tiles(offset, count_ref, product, lambda tile: dest_ref[tile], total_ref)
    for block in range(blocks):
        part = pl.ds(block * BLOCK, BLOCK)
        value = (total_ref[block] / degree_ref[:, part].astype(F32)).astype(BF16)
        for copy in range(out_ref.shape[0]):
            out_ref[copy, :, part] = value


def middle_kernel(
    place_ref, core_ref, stack_ref, count_ref, dest_ref, source_ref, tiles_hbm, degree_ref, *refs
):
    packed, aggregates, refs = refs[:2], refs[2:4], refs[4:]
    bias_ref, cotangent_ref, refs = *refs[:2], refs[2:]
    act_ref, grad_ref, weight_ref, self_ref, neighbour_ref, refs = *refs[:5], refs[5:]
    level_ref, below_ref, above_ref, *refs = refs
    features_ref, scaled_ref, total_ref, tiles_ref, copied, *refs = refs
    turned_ref, to_below_ref, to_above_ref, stored = refs
    copies = tile_copies(tiles_hbm, tiles_ref, copied)
    stores = [
        pltpu.make_async_copy(source, target, stored.at[at])
        for at, (source, target) in enumerate(
            ((turned_ref, grad_ref), (to_below_ref, below_ref), (to_above_ref, above_ref))
        )
    ]
    blocks = scaled_ref.shape[0]
    stacks, width, _ = aggregates[0].shape
    half = stacks * width
    contract_first = (((0,), (0,)), ((), ()))
    for far, ref in enumerate(packed):
        for stack in range(stacks):
            rows = pl.ds(far * half + stack * width, width)
            features_ref[rows, :] = ref[stack, pl.ds(0, width), :]
            for kind, out in enumerate((self_ref, neighbour_ref)):
                out[rows, :] = ref[stack, pl.ds(width, width), lanes(core_ref[0] * 2 + kind)]
    pre = lax.dot_general(
        self_ref[...], features_ref[...], contract_first, preferred_element_type=F32
    )
    for far, ref in enumerate(aggregates):
        pre = pre + lax.dot_general(
            neighbour_ref[pl.ds(far * half, half), :],
            ref[...].reshape(half, -1),
            contract_first,
            preferred_element_type=F32,
        )
    preact = pre.T + bias_ref[...].astype(F32)
    gate_value = jax.nn.sigmoid(preact)
    act_ref[...] = (preact * gate_value).astype(BF16)
    grad = cotangent_ref[...].astype(F32) * gate_value * (1.0 + preact * (1.0 - gate_value))
    grad_pre = grad.astype(BF16)
    grad = grad_pre.astype(F32)
    planes, _, rows, lane = weight_ref.shape
    bias_rows = jnp.broadcast_to(jnp.sum(grad, axis=0, keepdims=True), (rows, lane)).astype(BF16)
    for plane in range(planes):
        weight_ref[plane, COLUMN] = bias_rows
    turned = grad.T
    turned_ref[...] = turned.astype(BF16)
    stores[0].start()
    scaled = (turned / degree_ref[...].astype(F32)).astype(BF16)
    for block in range(blocks):
        scaled_ref[block] = scaled[:, block * BLOCK : (block + 1) * BLOCK]
    for far in range(CORES):
        operands = (features_ref[pl.ds(far * half, half), :], aggregates[far][...].reshape(half, -1))
        for kind, operand in enumerate(operands):
            term = jnp.dot(operand, grad_pre, preferred_element_type=F32).astype(BF16)
            for stack in range(stacks):
                column = (stack ^ stack_ref[0]) * CORES + far
                for first in range(0, width, PIECE):
                    plane, row = divmod(kind * width + first, rows)
                    begin = stack * width + first
                    weight_ref[plane, column, pl.ds(row, PIECE), :] = term[begin : begin + PIECE]
    total_ref[...] = jnp.zeros_like(total_ref)
    for offset in range(OFFS):
        slot = band_slot(place_ref, offset)

        def product(tile):
            return jnp.dot(
                scaled_ref[dest_ref[tile]], tiles_ref[tile], preferred_element_type=F32
            )

        def place(tile, slot=slot):
            return slot * blocks + source_ref[tile] % blocks

        copies[offset].wait()
        live_tiles(offset, count_ref, product, place, total_ref)
    for trio, out, store in (
        (0, to_below_ref, stores[1]),
        (2, to_above_ref, stores[2]),
        (1, level_ref, None),
    ):
        for slot in range(TRIO):
            for block in range(blocks):
                out[slot, :, pl.ds(block * BLOCK, BLOCK)] = total_ref[
                    (trio * TRIO + slot) * blocks + block
                ].astype(out.dtype)
        if store is not None:
            store.start()
    for store in stores:
        store.wait()


def trio_kernel(level_ref, below_ref, above_ref, *outs):
    for slot, out in enumerate(outs):
        value = level_ref[slot] + below_ref[slot].astype(F32) + above_ref[slot].astype(F32)
        out[...] = value.astype(out.dtype)


def back_kernel(own_ref, first_ref, second_ref, grad_ref, self_ref, neighbour_ref, keep_ref, send_ref):
    spread = own_ref[...] + first_ref[...].astype(F32) + second_ref[...].astype(F32)
    spread = spread.astype(BF16)
    half = keep_ref.shape[0]
    for at, out in enumerate((keep_ref, send_ref)):
        rows = pl.ds(at * half, half)
        value = jnp.dot(self_ref[rows, :], grad_ref[...], preferred_element_type=F32)
        value = value + jnp.dot(neighbour_ref[rows, :], spread, preferred_element_type=F32)
        out[...] = value.astype(out.dtype)


def chip_kernel(stack_ref, keep_ref, got_ref, *outs):
    for at, out in enumerate(outs):
        piece = (stack_ref[0] + at) % len(outs)
        out[...] = (keep_ref[piece] + got_ref[piece].astype(F32)).astype(out.dtype)


def planes_kernel(got_ref, out_ref):
    for column in range(COLUMN + 1):
        value = got_ref[0, column].astype(F32)
        for plane in range(1, got_ref.shape[0]):
            value = value + got_ref[plane, column].astype(F32)
        value = value.astype(BF16)
        for copy in range(COLUMN):
            out_ref[copy, column] = value


def column_kernel(feat_ref, got_ref, pieces_ref, bias_ref):
    for at in range(COLUMN + 1):
        value = got_ref[0, at].astype(F32)
        for column in range(1, COLUMN):
            value = value + got_ref[column, at].astype(F32)
        if at < COLUMN:
            pieces_ref[at ^ feat_ref[0]] = value.astype(BF16)
        else:
            bias_ref[...] = value


def lay_kernel(pieces_ref, self_ref, neighbour_ref):
    planes, _, rows, _ = pieces_ref.shape
    for plane in range(planes):
        for first in range(0, rows, PIECE):
            kind, row = divmod(plane * rows + first, self_ref.shape[0])
            out = (self_ref, neighbour_ref)[kind]
            for column in range(COLUMN):
                out[pl.ds(row, PIECE), pl.ds(column * BLOCK, BLOCK)] = pieces_ref[
                    plane, column, pl.ds(first, PIECE), :
                ].astype(F32)


def call(kernel, in_specs, out_shape, scratch, flops, moved, out_specs=None, limit=VMEM_BYTES):
    return pl.pallas_call(
        kernel,
        in_specs=in_specs,
        out_shape=out_shape,
        out_specs=out_specs or jax.tree.map(lambda _: VMEM, out_shape),
        scratch_shapes=scratch,
        compiler_params=pltpu.CompilerParams(vmem_limit_bytes=limit),
        cost_estimate=pl.CostEstimate(flops=flops, bytes_accessed=moved, transcendentals=0),
    )


def shifted(value, steps):
    count = lax.axis_size("rows")
    pairs = [(source, (source + steps) % count) for source in range(count)]
    return lax.ppermute(value, "rows", pairs)


def turned_in_trio(value, steps):
    count = lax.axis_size("rows")
    pairs = [
        (source, source // TRIO * TRIO + (source + steps) % TRIO) for source in range(count)
    ]
    return lax.ppermute(value, "rows", pairs)


def on_device(
    features,
    tile_values,
    dest_block,
    source_block,
    tile_count,
    degree,
    self_weight,
    neighbour_weight,
    hidden_bias,
    cotangent,
):
    node_dev, width = features.shape
    blocks = node_dev // BLOCK
    groups = lax.axis_size("rows")
    feats = lax.axis_size("feat")
    stacks = feats // CORES
    half = stacks * width
    hidden_dev = hidden_bias.shape[0]
    core = (lax.axis_index("feat") % CORES).reshape(1)
    stack = (lax.axis_index("feat") // CORES).reshape(1)
    place = (lax.axis_index("rows") % TRIO).reshape(1)
    same_core = [[z * CORES + c for z in range(stacks)] for c in range(CORES)]
    other_core = [(f, f ^ 1) for f in range(feats)]
    same_plane = [
        [(p // TRIO * COLUMN + c) * TRIO + p % TRIO for c in range(COLUMN)]
        for p in range(groups // COLUMN)
    ]
    same_column = [list(members) for members in zip(*same_plane)]

    def over_stacks(value):
        return lax.all_to_all(value, "feat", 0, 0, axis_index_groups=same_core)

    def to_stack(value, steps):
        pairs = [(f, (f + steps * CORES) % feats) for f in range(feats)]
        return lax.ppermute(value, "feat", pairs)

    turned = features.T
    level, packed = call(
        pack_kernel,
        [WHOLE] * 5,
        [
            jax.ShapeDtypeStruct((TRIO, width, node_dev), BF16),
            jax.ShapeDtypeStruct((stacks, 2 * width, node_dev), BF16),
        ],
        [],
        0,
        6 * stacks * width * node_dev,
    )(
        turned,
        turned_in_trio(turned, -1),
        turned_in_trio(turned, -2),
        self_weight,
        neighbour_weight,
    )
    below = shifted(level, TRIO)
    above = shifted(level, -TRIO)
    packed_own = over_stacks(packed)
    packed_far = lax.ppermute(packed_own, "feat", other_core)

    degrees = degree.reshape(1, node_dev)
    scalars = (tile_count, dest_block, source_block)
    tile_flops = 2 * OFFS * SLOTS * BLOCK * BLOCK * BLOCK
    aggregate = call(
        gather_kernel,
        [SMEM] * 4 + [HBM] + [VMEM] * 4,
        jax.ShapeDtypeStruct((stacks, width, node_dev), BF16),
        [
            pltpu.VMEM((blocks + 1, width, BLOCK), F32),
            pltpu.VMEM((TRIO * TRIO, width, node_dev), BF16),
            pltpu.VMEM(tile_values.shape, BF16),
            pltpu.SemaphoreType.DMA((OFFS,)),
        ],
        tile_flops,
        tile_values.size * 2,
        limit=TILES_VMEM_BYTES,
    )(place, *scalars, tile_values, degrees, below, level, above)
    aggregate_own = over_stacks(aggregate)
    aggregate_far = lax.ppermute(aggregate_own, "feat", other_core)

    planes = groups // COLUMN
    rows_each = 4 * half // groups

    def trio(dtype):
        return jax.ShapeDtypeStruct((TRIO, hidden_dev, node_dev), dtype)

    middle = call(
        middle_kernel,
        [SMEM] * 6 + [HBM] + [VMEM] * 5 + [WHOLE] * 2,
        [
            jax.ShapeDtypeStruct((node_dev, hidden_dev), BF16),
            jax.ShapeDtypeStruct((hidden_dev, node_dev), BF16),
            jax.ShapeDtypeStruct((planes, COLUMN + 1, rows_each, hidden_dev), BF16),
            jax.ShapeDtypeStruct((2 * half, hidden_dev), BF16),
            jax.ShapeDtypeStruct((2 * half, hidden_dev), BF16),
            trio(F32),
            trio(BF16),
            trio(BF16),
        ],
        [
            pltpu.VMEM((2 * half, node_dev), BF16),
            pltpu.VMEM((blocks, hidden_dev, BLOCK), BF16),
            pltpu.VMEM((TRIO * TRIO * blocks + 1, hidden_dev, BLOCK), F32),
            pltpu.VMEM(tile_values.shape, BF16),
            pltpu.SemaphoreType.DMA((OFFS,)),
            pltpu.VMEM((hidden_dev, node_dev), BF16),
            pltpu.VMEM((TRIO, hidden_dev, node_dev), BF16),
            pltpu.VMEM((TRIO, hidden_dev, node_dev), BF16),
            pltpu.SemaphoreType.DMA((3,)),
        ],
        tile_flops * 2,
        tile_values.size * 2,
        [WHOLE, HBM, VMEM, VMEM, VMEM, VMEM, HBM, HBM],
        TILES_VMEM_BYTES,
    )(
        place,
        core,
        stack,
        *scalars,
        tile_values,
        degrees,
        packed_own,
        packed_far,
        aggregate_own,
        aggregate_far,
        hidden_bias.reshape(1, hidden_dev),
        cotangent,
    )
    activations, grad_turned, weight_part, weight_self, weight_neighbour = middle[:5]
    to_level, to_below, to_above = middle[5:]
    from_above = shifted(to_below, -TRIO)
    from_below = shifted(to_above, TRIO)

    got = jax.ShapeDtypeStruct((COLUMN, COLUMN + 1, rows_each, hidden_dev), BF16)
    got = call(planes_kernel, [VMEM], got, [], weight_part.size, weight_part.size * 2)(
        lax.all_to_all(weight_part, "rows", 0, 0, axis_index_groups=same_column)
    )
    pieces, bias_sum = call(
        column_kernel,
        [SMEM, VMEM],
        [
            jax.ShapeDtypeStruct((COLUMN, rows_each, hidden_dev), BF16),
            jax.ShapeDtypeStruct((rows_each, hidden_dev), F32),
        ],
        [],
        got.size,
        got.size * 2,
    )(
        lax.axis_index("feat").reshape(1),
        lax.all_to_all(got, "rows", 0, 0, axis_index_groups=same_plane),
    )
    pieces = lax.all_to_all(pieces, "feat", 0, 0)
    pieces = lax.all_to_all(
        jnp.broadcast_to(pieces[None], (planes,) + pieces.shape),
        "rows",
        0,
        0,
        axis_index_groups=same_column,
    )
    grad_weight = jax.ShapeDtypeStruct((width, feats * hidden_dev), F32)
    grad_self, grad_neighbour = call(
        lay_kernel, [VMEM], [grad_weight, grad_weight], [], 0, pieces.size * 6
    )(pieces)

    spread = jax.ShapeDtypeStruct((hidden_dev, node_dev), BF16)
    own, first, second = call(
        trio_kernel,
        [VMEM] * 3,
        [jax.ShapeDtypeStruct(spread.shape, F32), spread, spread],
        [],
        9 * spread.size,
        20 * spread.size,
    )(to_level, from_below, from_above)
    first = turned_in_trio(first, 1)
    second = turned_in_trio(second, 2)
    keep, send = call(
        back_kernel,
        [VMEM] * 6,
        [
            jax.ShapeDtypeStruct((half, node_dev), F32),
            jax.ShapeDtypeStruct((half, node_dev), BF16),
        ],
        [],
        8 * half * node_dev * hidden_dev,
        4 * half * node_dev,
    )(own, first, second, grad_turned, weight_self, weight_neighbour)
    got = lax.ppermute(send, "feat", other_core)
    part = jax.ShapeDtypeStruct((width, node_dev), BF16)
    parts = call(
        chip_kernel,
        [SMEM] + [VMEM] * 2,
        [jax.ShapeDtypeStruct(part.shape, F32)] + [part] * (stacks - 1),
        [],
        4 * half * node_dev,
        8 * half * node_dev,
    )(
        stack,
        keep.reshape(stacks, width, node_dev),
        got.reshape(stacks, width, node_dev),
    )
    grad_turned = parts[0]
    for steps in range(1, stacks):
        grad_turned = grad_turned + to_stack(parts[steps], steps).astype(F32)
    return (activations, grad_turned.astype(BF16).T, grad_self, grad_neighbour, bias_sum[0])


def solution(mesh):
    in_specs = (
        P("rows", "feat"),
        P("rows", None, None),
        P("rows"),
        P("rows"),
        P("rows"),
        P("rows"),
        P("feat", None),
        P("feat", None),
        P("feat"),
        P("rows", "feat"),
    )
    out_specs = (P("rows", "feat"), P("rows", "feat"), P("feat", None), P("feat", None), P("feat"))
    return jax.shard_map(
        on_device, mesh=mesh, in_specs=in_specs, out_specs=out_specs, check_vma=False
    )
```

```python
import functools

import jax
import jax.numpy as jnp
from jax import lax
from jax.experimental import pallas as pl
from jax.experimental.pallas import tpu as pltpu
from jax.sharding import PartitionSpec as P

REACH = 3
SLOTS = 16
OFFS = 2 * REACH + 1
BLOCK = 128
GROUP = 4
CORES = 2
TRIO = 3
COLUMN = 8
PIECE = 16
F32 = jnp.float32
BF16 = jnp.bfloat16
VMEM_BYTES = 16 * 1024 * 1024
TILES_VMEM_BYTES = 60_500_000
VMEM = pl.BlockSpec(memory_space=pltpu.VMEM)
SMEM = pl.BlockSpec(memory_space=pltpu.SMEM)
ANY = pl.BlockSpec(memory_space=pl.ANY)
HBM = pl.BlockSpec(memory_space=pltpu.HBM)
WHOLE = pl.BlockSpec()


def lanes(block):
    return pl.ds(pl.multiple_of(block * BLOCK, BLOCK), BLOCK)


def live_tiles(offset, count_ref, product, place_of, total_ref):
    count = count_ref[offset]
    spare = total_ref.shape[0] - 1

    def step(at, carry):
        products = []
        places = []
        for inner in range(GROUP):
            slot = at * GROUP + inner
            tile = offset * SLOTS + slot
            products.append(product(tile))
            places.append(jnp.where(slot < count, place_of(tile), spare))
        for place, value in zip(places, products):
            total_ref[place] += value
        return carry

    lax.fori_loop(0, (count + GROUP - 1) // GROUP, step, 0)


def band_slot(place_ref, offset):
    return (place_ref[0] + offset) // TRIO * TRIO + offset % TRIO


def pack_kernel(features_ref, first_ref, second_ref, self_ref, neighbour_ref, level_ref, out_ref):
    width = features_ref.shape[0]
    for slot, ref in enumerate((features_ref, first_ref, second_ref)):
        level_ref[slot] = ref[...]
    for stack in range(out_ref.shape[0]):
        out_ref[stack, pl.ds(0, width), :] = features_ref[...]
        for core in range(CORES):
            for kind, ref in enumerate((self_ref, neighbour_ref)):
                out_ref[stack, pl.ds(width, width), pl.ds((core * 2 + kind) * BLOCK, BLOCK)] = ref[
                    :, pl.ds((stack * CORES + core) * BLOCK, BLOCK)
                ]


def tile_copies(tiles_hbm, tiles_ref, copied):
    copies = []
    for offset in range(OFFS):
        part = pl.ds(offset * SLOTS, SLOTS)
        copies.append(
            pltpu.make_async_copy(tiles_hbm.at[part], tiles_ref.at[part], copied.at[offset])
        )
    for copy in copies:
        copy.start()
    return copies


def gather_kernel(
    place_ref,
    count_ref,
    dest_ref,
    source_ref,
    tiles_hbm,
    degree_ref,
    below_ref,
    level_ref,
    above_ref,
    out_ref,
    total_ref,
    band_ref,
    tiles_ref,
    copied,
):
    copies = tile_copies(tiles_hbm, tiles_ref, copied)
    blocks = total_ref.shape[0] - 1
    total_ref[...] = jnp.zeros_like(total_ref)
    for trio, ref in enumerate((below_ref, level_ref, above_ref)):
        band_ref[pl.ds(trio * TRIO, TRIO)] = ref[...]
    for offset in range(OFFS):
        slot = band_slot(place_ref, offset)

        def product(tile, slot=slot):
            picked = band_ref[slot, :, lanes(source_ref[tile] % blocks)]
            return lax.dot_general(
                picked, tiles_ref[tile], (((1,), (1,)), ((), ())), preferred_element_type=F32
            )

        copies[offset].wait()
        live_tiles(offset, count_ref, product, lambda tile: dest_ref[tile], total_ref)
    for block in range(blocks):
        part = pl.ds(block * BLOCK, BLOCK)
        value = (total_ref[block] / degree_ref[:, part].astype(F32)).astype(BF16)
        for copy in range(out_ref.shape[0]):
            out_ref[copy, :, part] = value


def middle_kernel(
    place_ref, core_ref, stack_ref, count_ref, dest_ref, source_ref, tiles_hbm, degree_ref, *refs
):
    packed, aggregates, refs = refs[:2], refs[2:4], refs[4:]
    bias_ref, cotangent_ref, refs = *refs[:2], refs[2:]
    act_ref, grad_ref, weight_ref, self_ref, neighbour_ref, refs = *refs[:5], refs[5:]
    level_ref, below_ref, above_ref, *refs = refs
    features_ref, scaled_ref, total_ref, tiles_ref, copied, *refs = refs
    turned_ref, to_below_ref, to_above_ref, stored = refs
    copies = tile_copies(tiles_hbm, tiles_ref, copied)
    stores = [
        pltpu.make_async_copy(source, target, stored.at[at])
        for at, (source, target) in enumerate(
            ((turned_ref, grad_ref), (to_below_ref, below_ref), (to_above_ref, above_ref))
        )
    ]
    blocks = scaled_ref.shape[0]
    stacks, width, _ = aggregates[0].shape
    half = stacks * width
    contract_first = (((0,), (0,)), ((), ()))
    for far, ref in enumerate(packed):
        for stack in range(stacks):
            rows = pl.ds(far * half + stack * width, width)
            features_ref[rows, :] = ref[stack, pl.ds(0, width), :]
            for kind, out in enumerate((self_ref, neighbour_ref)):
                out[rows, :] = ref[stack, pl.ds(width, width), lanes(core_ref[0] * 2 + kind)]
    pre = lax.dot_general(
        self_ref[...], features_ref[...], contract_first, preferred_element_type=F32
    )
    for far, ref in enumerate(aggregates):
        pre = pre + lax.dot_general(
            neighbour_ref[pl.ds(far * half, half), :],
            ref[...].reshape(half, -1),
            contract_first,
            preferred_element_type=F32,
        )
    preact = pre.T + bias_ref[...].astype(F32)
    gate_value = jax.nn.sigmoid(preact)
    act_ref[...] = (preact * gate_value).astype(BF16)
    grad = cotangent_ref[...].astype(F32) * gate_value * (1.0 + preact * (1.0 - gate_value))
    grad_pre = grad.astype(BF16)
    grad = grad_pre.astype(F32)
    planes, _, rows, lane = weight_ref.shape
    bias_rows = jnp.broadcast_to(jnp.sum(grad, axis=0, keepdims=True), (rows, lane)).astype(BF16)
    for plane in range(planes):
        weight_ref[plane, COLUMN] = bias_rows
    turned = grad.T
    turned_ref[...] = turned.astype(BF16)
    stores[0].start()
    scaled = (turned / degree_ref[...].astype(F32)).astype(BF16)
    for block in range(blocks):
        scaled_ref[block] = scaled[:, block * BLOCK : (block + 1) * BLOCK]
    for far in range(CORES):
        operands = (features_ref[pl.ds(far * half, half), :], aggregates[far][...].reshape(half, -1))
        for kind, operand in enumerate(operands):
            term = jnp.dot(operand, grad_pre, preferred_element_type=F32).astype(BF16)
            for stack in range(stacks):
                column = (stack ^ stack_ref[0]) * CORES + far
                for first in range(0, width, PIECE):
                    plane, row = divmod(kind * width + first, rows)
                    begin = stack * width + first
                    weight_ref[plane, column, pl.ds(row, PIECE), :] = term[begin : begin + PIECE]
    total_ref[...] = jnp.zeros_like(total_ref)
    for offset in range(OFFS):
        slot = band_slot(place_ref, offset)

        def product(tile):
            return jnp.dot(
                scaled_ref[dest_ref[tile]], tiles_ref[tile], preferred_element_type=F32
            )

        def place(tile, slot=slot):
            return slot * blocks + source_ref[tile] % blocks

        copies[offset].wait()
        live_tiles(offset, count_ref, product, place, total_ref)
    for trio, out, store in (
        (0, to_below_ref, stores[1]),
        (2, to_above_ref, stores[2]),
        (1, level_ref, None),
    ):
        for slot in range(TRIO):
            for block in range(blocks):
                out[slot, :, pl.ds(block * BLOCK, BLOCK)] = total_ref[
                    (trio * TRIO + slot) * blocks + block
                ].astype(out.dtype)
        if store is not None:
            store.start()
    for store in stores:
        store.wait()


def trio_kernel(level_ref, below_ref, above_ref, *outs):
    for slot, out in enumerate(outs):
        value = level_ref[slot] + below_ref[slot].astype(F32) + above_ref[slot].astype(F32)
        out[...] = value.astype(out.dtype)


def back_kernel(own_ref, first_ref, second_ref, grad_ref, self_ref, neighbour_ref, keep_ref, send_ref):
    spread = own_ref[...] + first_ref[...].astype(F32) + second_ref[...].astype(F32)
    spread = spread.astype(BF16)
    half = keep_ref.shape[0]
    for at, out in enumerate((keep_ref, send_ref)):
        rows = pl.ds(at * half, half)
        value = jnp.dot(self_ref[rows, :], grad_ref[...], preferred_element_type=F32)
        value = value + jnp.dot(neighbour_ref[rows, :], spread, preferred_element_type=F32)
        out[...] = value.astype(out.dtype)


def chip_kernel(stack_ref, keep_ref, got_ref, *outs):
    for at, out in enumerate(outs):
        piece = (stack_ref[0] + at) % len(outs)
        out[...] = (keep_ref[piece] + got_ref[piece].astype(F32)).astype(out.dtype)


def planes_kernel(got_ref, out_ref):
    for column in range(COLUMN + 1):
        value = got_ref[0, column].astype(F32)
        for plane in range(1, got_ref.shape[0]):
            value = value + got_ref[plane, column].astype(F32)
        value = value.astype(BF16)
        for copy in range(COLUMN):
            out_ref[copy, column] = value


def column_kernel(feat_ref, got_ref, pieces_ref, bias_ref):
    for at in range(COLUMN + 1):
        value = got_ref[0, at].astype(F32)
        for column in range(1, COLUMN):
            value = value + got_ref[column, at].astype(F32)
        if at < COLUMN:
            pieces_ref[at ^ feat_ref[0]] = value.astype(BF16)
        else:
            bias_ref[...] = value


def lay_kernel(pieces_ref, self_ref, neighbour_ref):
    planes, _, rows, _ = pieces_ref.shape
    for plane in range(planes):
        for first in range(0, rows, PIECE):
            kind, row = divmod(plane * rows + first, self_ref.shape[0])
            out = (self_ref, neighbour_ref)[kind]
            for column in range(COLUMN):
                out[pl.ds(row, PIECE), pl.ds(column * BLOCK, BLOCK)] = pieces_ref[
                    plane, column, pl.ds(first, PIECE), :
                ].astype(F32)


def call(kernel, in_specs, out_shape, scratch, flops, moved, out_specs=None, limit=VMEM_BYTES):
    return pl.pallas_call(
        kernel,
        in_specs=in_specs,
        out_shape=out_shape,
        out_specs=out_specs or jax.tree.map(lambda _: VMEM, out_shape),
        scratch_shapes=scratch,
        compiler_params=pltpu.CompilerParams(vmem_limit_bytes=limit),
        cost_estimate=pl.CostEstimate(flops=flops, bytes_accessed=moved, transcendentals=0),
    )


def shifted(value, steps):
    count = lax.axis_size("rows")
    pairs = [(source, (source + steps) % count) for source in range(count)]
    return lax.ppermute(value, "rows", pairs)


def turned_in_trio(value, steps):
    count = lax.axis_size("rows")
    pairs = [
        (source, source // TRIO * TRIO + (source + steps) % TRIO) for source in range(count)
    ]
    return lax.ppermute(value, "rows", pairs)


def on_device(
    features,
    tile_values,
    dest_block,
    source_block,
    tile_count,
    degree,
    self_weight,
    neighbour_weight,
    hidden_bias,
    cotangent,
):
    node_dev, width = features.shape
    blocks = node_dev // BLOCK
    groups = lax.axis_size("rows")
    feats = lax.axis_size("feat")
    stacks = feats // CORES
    half = stacks * width
    hidden_dev = hidden_bias.shape[0]
    core = (lax.axis_index("feat") % CORES).reshape(1)
    stack = (lax.axis_index("feat") // CORES).reshape(1)
    place = (lax.axis_index("rows") % TRIO).reshape(1)
    same_core = [[z * CORES + c for z in range(stacks)] for c in range(CORES)]
    other_core = [(f, f ^ 1) for f in range(feats)]
    same_plane = [
        [(p // TRIO * COLUMN + c) * TRIO + p % TRIO for c in range(COLUMN)]
        for p in range(groups // COLUMN)
    ]
    same_column = [list(members) for members in zip(*same_plane)]

    def over_stacks(value):
        return lax.all_to_all(value, "feat", 0, 0, axis_index_groups=same_core)

    def to_stack(value, steps):
        pairs = [(f, (f + steps * CORES) % feats) for f in range(feats)]
        return lax.ppermute(value, "feat", pairs)

    turned = features.T
    level, packed = call(
        pack_kernel,
        [WHOLE] * 5,
        [
            jax.ShapeDtypeStruct((TRIO, width, node_dev), BF16),
            jax.ShapeDtypeStruct((stacks, 2 * width, node_dev), BF16),
        ],
        [],
        0,
        6 * stacks * width * node_dev,
        limit=TILES_VMEM_BYTES,
    )(
        turned,
        turned_in_trio(turned, -1),
        turned_in_trio(turned, -2),
        self_weight,
        neighbour_weight,
    )
    below = shifted(level, TRIO)
    above = shifted(level, -TRIO)
    packed_own = over_stacks(packed)
    packed_far = lax.ppermute(packed_own, "feat", other_core)

    degrees = degree.reshape(1, node_dev)
    scalars = (tile_count, dest_block, source_block)
    tile_flops = 2 * OFFS * SLOTS * BLOCK * BLOCK * BLOCK
    aggregate = call(
        gather_kernel,
        [SMEM] * 4 + [HBM] + [VMEM] * 4,
        jax.ShapeDtypeStruct((stacks, width, node_dev), BF16),
        [
            pltpu.VMEM((blocks + 1, width, BLOCK), F32),
            pltpu.VMEM((TRIO * TRIO, width, node_dev), BF16),
            pltpu.VMEM(tile_values.shape, BF16),
            pltpu.SemaphoreType.DMA((OFFS,)),
        ],
        tile_flops,
        tile_values.size * 2,
        limit=TILES_VMEM_BYTES,
    )(place, *scalars, tile_values, degrees, below, level, above)
    aggregate_own = over_stacks(aggregate)
    aggregate_far = lax.ppermute(aggregate_own, "feat", other_core)

    planes = groups // COLUMN
    rows_each = 4 * half // groups

    def trio(dtype):
        return jax.ShapeDtypeStruct((TRIO, hidden_dev, node_dev), dtype)

    middle = call(
        middle_kernel,
        [SMEM] * 6 + [HBM] + [VMEM] * 5 + [WHOLE] * 2,
        [
            jax.ShapeDtypeStruct((node_dev, hidden_dev), BF16),
            jax.ShapeDtypeStruct((hidden_dev, node_dev), BF16),
            jax.ShapeDtypeStruct((planes, COLUMN + 1, rows_each, hidden_dev), BF16),
            jax.ShapeDtypeStruct((2 * half, hidden_dev), BF16),
            jax.ShapeDtypeStruct((2 * half, hidden_dev), BF16),
            trio(F32),
            trio(BF16),
            trio(BF16),
        ],
        [
            pltpu.VMEM((2 * half, node_dev), BF16),
            pltpu.VMEM((blocks, hidden_dev, BLOCK), BF16),
            pltpu.VMEM((TRIO * TRIO * blocks + 1, hidden_dev, BLOCK), F32),
            pltpu.VMEM(tile_values.shape, BF16),
            pltpu.SemaphoreType.DMA((OFFS,)),
            pltpu.VMEM((hidden_dev, node_dev), BF16),
            pltpu.VMEM((TRIO, hidden_dev, node_dev), BF16),
            pltpu.VMEM((TRIO, hidden_dev, node_dev), BF16),
            pltpu.SemaphoreType.DMA((3,)),
        ],
        tile_flops * 2,
        tile_values.size * 2,
        [WHOLE, HBM, VMEM, VMEM, VMEM, VMEM, HBM, HBM],
        TILES_VMEM_BYTES,
    )(
        place,
        core,
        stack,
        *scalars,
        tile_values,
        degrees,
        packed_own,
        packed_far,
        aggregate_own,
        aggregate_far,
        hidden_bias.reshape(1, hidden_dev),
        cotangent,
    )
    activations, grad_turned, weight_part, weight_self, weight_neighbour = middle[:5]
    to_level, to_below, to_above = middle[5:]
    from_above = shifted(to_below, -TRIO)
    from_below = shifted(to_above, TRIO)

    got = jax.ShapeDtypeStruct((COLUMN, COLUMN + 1, rows_each, hidden_dev), BF16)
    got = call(planes_kernel, [VMEM], got, [], weight_part.size, weight_part.size * 2)(
        lax.all_to_all(weight_part, "rows", 0, 0, axis_index_groups=same_column)
    )
    pieces, bias_sum = call(
        column_kernel,
        [SMEM, VMEM],
        [
            jax.ShapeDtypeStruct((COLUMN, rows_each, hidden_dev), BF16),
            jax.ShapeDtypeStruct((rows_each, hidden_dev), F32),
        ],
        [],
        got.size,
        got.size * 2,
    )(
        lax.axis_index("feat").reshape(1),
        lax.all_to_all(got, "rows", 0, 0, axis_index_groups=same_plane),
    )
    pieces = lax.all_to_all(pieces, "feat", 0, 0)
    pieces = lax.all_to_all(
        jnp.broadcast_to(pieces[None], (planes,) + pieces.shape),
        "rows",
        0,
        0,
        axis_index_groups=same_column,
    )
    grad_weight = jax.ShapeDtypeStruct((width, feats * hidden_dev), F32)
    grad_self, grad_neighbour = call(
        lay_kernel, [VMEM], [grad_weight, grad_weight], [], 0, pieces.size * 6
    )(pieces)

    spread = jax.ShapeDtypeStruct((hidden_dev, node_dev), BF16)
    own, first, second = call(
        trio_kernel,
        [VMEM] * 3,
        [jax.ShapeDtypeStruct(spread.shape, F32), spread, spread],
        [],
        9 * spread.size,
        20 * spread.size,
    )(to_level, from_below, from_above)
    first = turned_in_trio(first, 1)
    second = turned_in_trio(second, 2)
    keep, send = call(
        back_kernel,
        [VMEM] * 6,
        [
            jax.ShapeDtypeStruct((half, node_dev), F32),
            jax.ShapeDtypeStruct((half, node_dev), BF16),
        ],
        [],
        8 * half * node_dev * hidden_dev,
        4 * half * node_dev,
    )(own, first, second, grad_turned, weight_self, weight_neighbour)
    got = lax.ppermute(send, "feat", other_core)
    part = jax.ShapeDtypeStruct((width, node_dev), BF16)
    parts = call(
        chip_kernel,
        [SMEM] + [VMEM] * 2,
        [jax.ShapeDtypeStruct(part.shape, F32)] + [part] * (stacks - 1),
        [],
        4 * half * node_dev,
        8 * half * node_dev,
    )(
        stack,
        keep.reshape(stacks, width, node_dev),
        got.reshape(stacks, width, node_dev),
    )
    grad_turned = parts[0]
    for steps in range(1, stacks):
        grad_turned = grad_turned + to_stack(parts[steps], steps).astype(F32)
    return (activations, grad_turned.astype(BF16).T, grad_self, grad_neighbour, bias_sum[0])


def solution(mesh):
    in_specs = (
        P("rows", "feat"),
        P("rows", None, None),
        P("rows"),
        P("rows"),
        P("rows"),
        P("rows"),
        P("feat", None),
        P("feat", None),
        P("feat"),
        P("rows", "feat"),
    )
    out_specs = (P("rows", "feat"), P("rows", "feat"), P("feat", None), P("feat", None), P("feat"))
    return jax.shard_map(
        on_device, mesh=mesh, in_specs=in_specs, out_specs=out_specs, check_vma=False
    )
```
